32 devices in a mesh: prompt: 4 (over x, core), response: 4 (over z), tensor: 2 (over y).
Axes of the slice: x: 2, y: 2, z: 4, core: 2. Of those that a mesh axis runs over, the one named last changes fastest.
Arguments:
- queries: bfloat16 [4, 512, 8192], P('prompt', 'response', 'tensor'), may hold values from -30 to 30
- keys: bfloat16 [4, 512, 1024], P('prompt', 'response', 'tensor'), may hold values from -6 to 6
- values: bfloat16 [4, 512, 1024], P('prompt', 'response', 'tensor'), may hold values from -36 to 36
- prefix_keys: bfloat16 [4, 512, 1024], P('prompt', ('response', 'tensor')), may hold values from -6 to 6
- prefix_values: bfloat16 [4, 512, 1024], P('prompt', ('response', 'tensor')), may hold values from -36 to 36
- lengths: int32 [4, 4], P('prompt', 'response'), may hold values from 1 to 128, as said below
- out_grad: bfloat16 [4, 512, 8192], P('prompt', 'response', 'tensor'), may hold values from -36 to 36
Outputs:
- output: bfloat16 [4, 512, 8192], P('prompt', 'response', 'tensor')
- query_grad: bfloat16 [4, 512, 8192], P('prompt', 'response', 'tensor')
- key_grad: bfloat16 [4, 512, 1024], P('prompt', 'response', 'tensor')
- value_grad: bfloat16 [4, 512, 1024], P('prompt', 'response', 'tensor')
- prefix_key_grad: bfloat16 [4, 512, 1024], P('prompt', ('response', 'tensor'))
- prefix_value_grad: bfloat16 [4, 512, 1024], P('prompt', ('response', 'tensor'))
The draws below stay inside these ranges and needn't reach their ends.
Inputs may be any that keep to these rules, and one draw needn't show every extreme that they name: `lengths`: number of live tokens of response r of prompt p; they fill its first slots.
All inputs are finite; a program needn't handle non-finite values.
Results may differ from the reference program's by a relative error of at most 0.023.
Values may be sent and summed in bfloat16 or wider, within the bound.
No kernel may reach another device: no remote copies, remote signals or barrier semaphores. Data moves between devices by JAX's collectives and lax.ppermute only.
A program may use at most 192 MiB of HBM per device.

```python
import math
import jax
import jax.numpy as jnp
from jax import lax

KVH = 8
HD = 128
GROUP = 8
ROWS_DEV = 128
PROMPTS = 4
RESPONSES = 4
PREFIX = 512
RESP_ROWS = 512


def draw_queries(key, part):
    key = jax.random.fold_in(key, 11)
    drawn = jnp.clip(jax.random.normal(key, (PROMPTS, RESP_ROWS, GROUP * KVH * HD), jnp.float32), -6.0, 6.0)
    return drawn.astype(jnp.bfloat16)


def draw_prefix_keys(key, part):
    key = jax.random.fold_in(key, 13)
    drawn = jnp.clip(jax.random.normal(key, (PROMPTS, PREFIX, KVH * HD), jnp.float32), -6.0, 6.0)
    return drawn.astype(jnp.bfloat16)


def draw_lengths(key, part):
    key = jax.random.fold_in(key, 17)
    first_key, second_key, third_key = jax.random.split(key, 3)
    prompt_ids = jnp.arange(PROMPTS, dtype=jnp.int32)[:, None]
    response_ids = jnp.arange(RESPONSES, dtype=jnp.int32)[None, :]
    lower = jnp.maximum(1, ROWS_DEV * (prompt_ids + 1) // (2 * PROMPTS))
    upper = ROWS_DEV * (prompt_ids + 1) // PROMPTS + 1
    drawn = jax.random.randint(first_key, (PROMPTS, RESPONSES), lower, upper)
    shortest = jax.random.randint(third_key, (), 0, RESPONSES)
    shortrow = (prompt_ids == 0) & (response_ids == shortest)
    drawn = jnp.where(shortrow, 1, drawn)
    chosen = jax.random.randint(second_key, (), 0, RESPONSES)
    fullrow = (prompt_ids == PROMPTS - 1) & (response_ids == chosen)
    return jnp.where(fullrow, ROWS_DEV, drawn).astype(jnp.int32)


def steps_of(stream_key, dims, shards, smallest, top_value):
    def one(dim, parts):
        steps = jax.random.uniform(jax.random.fold_in(jax.random.fold_in(stream_key, 6), dim), (parts,), jnp.float32, smallest / len(shards), top_value / len(shards))
        return jnp.repeat(jnp.exp(steps), dims[dim] // parts).reshape((-1,) + (1,) * (len(dims) - dim - 1))

    loudness = one(*shards[0])
    for cut in shards[1:]:
        loudness = loudness * one(*cut)
    return loudness


def noise(key, dims, spread, bound, cuts=(), held_as=jnp.bfloat16):
    level = steps_of(key, dims, cuts, -0.22, 0.18) if cuts else 1.0
    values = jax.random.normal(key, dims, jnp.float32) * spread * level
    return jnp.minimum(jnp.maximum(values, -bound), bound).astype(held_as)


def setup_inputs(seed: int = 0) -> dict:
    key_of = jax.random.split(jax.random.key(seed), 8)
    queries = draw_queries(jax.random.fold_in(key_of[7], 71), 0)
    keys = noise(key_of[1], (PROMPTS, RESP_ROWS, KVH * HD), 1.0, 6.0, ((0, 4), (1, 4), (2, 2)))
    values = noise(key_of[2], (PROMPTS, RESP_ROWS, KVH * HD), 6.0, 36.0, ((0, 4), (1, 4), (2, 2)))
    prefix_keys = draw_prefix_keys(jax.random.fold_in(key_of[7], 71), 0)
    prefix_values = noise(key_of[4], (PROMPTS, PREFIX, KVH * HD), 6.0, 36.0, ((0, 4), (1, 8)))
    lengths = draw_lengths(jax.random.fold_in(key_of[7], 71), 0)
    out_grad = noise(key_of[6], (PROMPTS, RESP_ROWS, GROUP * KVH * HD), 6.0, 36.0, ((0, 4), (1, 4), (2, 2)))
    return {"queries": queries, "keys": keys, "values": values, "prefix_keys": prefix_keys, "prefix_values": prefix_values, "lengths": lengths, "out_grad": out_grad}


def attend_head(head_queries, own_keys, own_values, pre_keys, pre_values, live_rows, scaled_grad):
    row_count = head_queries.shape[0]
    prefix_len = pre_keys.shape[0]
    all_keys = jnp.concatenate([pre_keys, own_keys], axis=0).astype(jnp.float32)
    all_values = jnp.concatenate([pre_values, own_values], axis=0).astype(jnp.float32)
    query_rows = head_queries.astype(jnp.float32)
    grad_rows = scaled_grad.astype(jnp.float32)
    factor = 1.0 / math.sqrt(head_queries.shape[2])
    scores = jnp.einsum('rgd,kd->grk', query_rows, all_keys) * factor
    row_pos = jnp.arange(row_count, dtype=jnp.int32)[:, None]
    key_pos = jnp.arange(prefix_len + row_count, dtype=jnp.int32)[None, :] - prefix_len
    allowed = key_pos <= row_pos
    scores = jnp.where(allowed[None], scores, -1e+30)
    row_max = lax.optimization_barrier(jnp.max(scores, axis=2, keepdims=True))
    exponent = jnp.exp(scores - row_max)
    probs = exponent / lax.optimization_barrier(jnp.sum(exponent, axis=2, keepdims=True))
    rounded = probs.astype(jnp.bfloat16)
    rounded_wide = rounded.astype(jnp.float32)
    attended = jnp.einsum('grk,kd->rgd', rounded_wide, all_values)
    output = (attended * live_rows[:, None, None]).astype(jnp.bfloat16)
    grad_probs = jnp.einsum('rgd,kd->grk', grad_rows, all_values)
    centre = lax.optimization_barrier(jnp.sum(grad_rows * attended, axis=2))
    score_grad = (probs * (grad_probs - jnp.transpose(centre)[:, :, None]) * factor).astype(jnp.bfloat16)
    score_wide = score_grad.astype(jnp.float32)
    query_grad = jnp.einsum('grk,kd->rgd', score_wide, all_keys)
    key_grad = jnp.einsum('grk,rgd->kd', score_wide, query_rows)
    value_grad = jnp.einsum('grk,rgd->kd', rounded_wide, grad_rows)
    return (output, query_grad, key_grad[:prefix_len], key_grad[prefix_len:], value_grad[:prefix_len], value_grad[prefix_len:])

def response_rows(resp_queries, resp_keys, resp_values, pre_keys, pre_values, length, resp_grad, weight):
    row_count = resp_queries.shape[0]
    live_rows = (jnp.arange(row_count, dtype=jnp.int32) < length).astype(jnp.float32)
    scaled = (resp_grad.astype(jnp.float32) * live_rows[:, None] * weight).astype(jnp.bfloat16)
    head_count = resp_keys.shape[1] // HD
    outputs, query_grads, key_grads, value_grads, pre_kgs, pre_vgs = ([], [], [], [], [], [])
    for kv_head in range(head_count):
        qstart = kv_head * GROUP * HD
        kstart = kv_head * HD
        block_queries = resp_queries[:, qstart:qstart + GROUP * HD].reshape(row_count, GROUP, HD)
        block_grad = scaled[:, qstart:qstart + GROUP * HD].reshape(row_count, GROUP, HD)
        results = attend_head(block_queries, resp_keys[:, kstart:kstart + HD], resp_values[:, kstart:kstart + HD], pre_keys[:, kstart:kstart + HD], pre_values[:, kstart:kstart + HD], live_rows, block_grad)
        outputs.append(results[0].reshape(row_count, GROUP * HD))
        query_grads.append(results[1].reshape(row_count, GROUP * HD))
        pre_kgs.append(results[2])
        key_grads.append(results[3])
        pre_vgs.append(results[4])
        value_grads.append(results[5])
    return (jnp.concatenate(outputs, axis=1), jnp.concatenate(query_grads, axis=1).astype(jnp.bfloat16), jnp.concatenate(key_grads, axis=1).astype(jnp.bfloat16), jnp.concatenate(value_grads, axis=1).astype(jnp.bfloat16), jnp.concatenate(pre_kgs, axis=1), jnp.concatenate(pre_vgs, axis=1))

def by_response(array):
    return array.reshape(RESPONSES, ROWS_DEV, array.shape[1])

def reference(queries, keys, values, prefix_keys, prefix_values, lengths, out_grad):
    live_total = jnp.sum(lengths.astype(jnp.float32))
    weight = PROMPTS * RESPONSES * ROWS_DEV / live_total

    def per_prompt(prompt_items):
        p_queries, p_keys, p_values, p_pre_keys, p_pre_values, p_lengths, p_grad = prompt_items

        def per_response(running, response_items):
            r_queries, r_keys, r_values, r_length, r_grad = response_items
            results = response_rows(r_queries, r_keys, r_values, p_pre_keys, p_pre_values, r_length, r_grad, weight)
            return ((running[0] + results[4], running[1] + results[5]), (results[0], results[1], results[2], results[3]))
        zero_grads = jnp.zeros(p_pre_keys.shape, jnp.float32)
        prefix_sums, results = lax.scan(per_response, (zero_grads, zero_grads), (by_response(p_queries), by_response(p_keys), by_response(p_values), p_lengths, by_response(p_grad)))
        merged = [part_rows.reshape(RESPONSES * ROWS_DEV, part_rows.shape[2]) for part_rows in results]
        return (merged[0], merged[1], merged[2], merged[3], prefix_sums[0].astype(jnp.bfloat16), prefix_sums[1].astype(jnp.bfloat16))
    stacked = lax.map(per_prompt, (queries, keys, values, prefix_keys, prefix_values, lengths, out_grad))
    return (stacked[0], stacked[1], stacked[2], stacked[3], stacked[4], stacked[5])
```

```python
import functools
import math

import jax
import jax.numpy as jnp
from jax import lax
from jax.experimental import pallas as pl
from jax.experimental.pallas import tpu as pltpu
from jax.sharding import PartitionSpec as P

HD = 128
GROUP = 8
PAIR = 2
VMEM_LIMIT = 48 * 1024 * 1024
NT = (((1,), (1,)), ((), ()))


def heads_down(ref, first, count):
    return jnp.concatenate(
        [ref[:, (first + i) * HD : (first + i + 1) * HD] for i in range(count)], axis=0
    )


def probs_kernel(n_slots, scale, length_ref, q_ref, do_ref, kown_ref, *refs):
    slot_refs = refs[:n_slots]
    p_ref, dvown_ref = refs[n_slots : n_slots + 2]
    dv_refs = refs[n_slots + 2 : 2 * n_slots + 2]
    s_ref = refs[2 * n_slots + 2]
    rows = q_ref.shape[0]
    own = kown_ref.shape[0]
    keys = jnp.concatenate([kown_ref[...]] + [ref[...] for ref in slot_refs], axis=0)
    width = PAIR * rows
    key_pos = lax.broadcasted_iota(jnp.int32, (own, width), 0)
    row_pos = lax.broadcasted_iota(jnp.int32, (own, width), 1) % rows
    allowed = key_pos <= row_pos
    live = (lax.broadcasted_iota(jnp.int32, (1, width), 1) % rows) < length_ref[0]
    for pair in range(GROUP // PAIR):
        here = s_ref.at[pair % 2]
        cols = slice(pair * width, (pair + 1) * width)
        here[...] = lax.dot_general(
            keys, heads_down(q_ref, pair * PAIR, PAIR), NT, preferred_element_type=jnp.float32
        )
        here[:own] = jnp.where(allowed, here[:own], -1e30)
        top = jnp.max(here[...], axis=0, keepdims=True) * scale
        exponent = jnp.exp2(here[...] * scale - top)
        here[...] = exponent
        total = jnp.sum(exponent, axis=0, keepdims=True)
        inverse = jnp.where(live, 1.0 / total, 0.0)
        p_ref[0, :, cols] = (here[...] * inverse).astype(jnp.bfloat16)
    dv = jnp.dot(p_ref[0], heads_down(do_ref, 0, GROUP), preferred_element_type=jnp.float32)
    dvown_ref[...] = dv[:own]
    start = own
    for ref in dv_refs:
        ref[...] = dv[start : start + ref.shape[0]].astype(jnp.bfloat16)
        start += ref.shape[0]


def grads_kernel(n_slots, factor, weight_ref, q_ref, do_ref, p_ref, dv_ref, kown_ref, vown_ref, *refs):
    kslot_refs = refs[:n_slots]
    vslot_refs = refs[n_slots : 2 * n_slots]
    out_ref, dq_ref, dkown_ref, dvown_ref = refs[2 * n_slots : 2 * n_slots + 4]
    dk_refs = refs[2 * n_slots + 4 : 3 * n_slots + 4]
    dp_ref, ds_ref = refs[3 * n_slots + 4 :]
    rows = q_ref.shape[0]
    own = kown_ref.shape[0]
    weight = weight_ref[0]
    keys = jnp.concatenate([kown_ref[...]] + [ref[...] for ref in kslot_refs], axis=0)
    values = jnp.concatenate([vown_ref[...]] + [ref[...] for ref in vslot_refs], axis=0)
    keys_t = keys.T
    values_t = values.T
    width = PAIR * rows
    for pair in range(GROUP // PAIR):
        here = dp_ref.at[pair % 2]
        cols = slice(pair * width, (pair + 1) * width)
        do = heads_down(do_ref, pair * PAIR, PAIR)
        here[...] = lax.dot_general(values, do, NT, preferred_element_type=jnp.float32)
        attended = jnp.dot(values_t, p_ref[0, :, cols], preferred_element_type=jnp.float32)
        centre = jnp.sum(attended * do.astype(jnp.float32).T, axis=0, keepdims=True)
        ds_ref[:, cols] = (
            p_ref[0, :, cols].astype(jnp.float32) * (here[...] - centre)
        ).astype(jnp.bfloat16)
        dq = jnp.dot(keys_t, ds_ref[:, cols], preferred_element_type=jnp.float32) * (factor * weight)
        for i in range(PAIR):
            head = slice((pair * PAIR + i) * HD, (pair * PAIR + i + 1) * HD)
            lanes = slice(i * rows, (i + 1) * rows)
            out_ref[:, head] = attended[:, lanes].T.astype(jnp.bfloat16)
            dq_ref[:, head] = dq[:, lanes].T.astype(jnp.bfloat16)
    dk = jnp.dot(ds_ref[...], heads_down(q_ref, 0, GROUP), preferred_element_type=jnp.float32)
    dkown_ref[...] = (dk[:own] * (factor * weight)).astype(jnp.bfloat16)
    dvown_ref[...] = (dv_ref[...] * weight).astype(jnp.bfloat16)
    start = own
    for ref in dk_refs:
        ref[...] = dk[start : start + ref.shape[0]].astype(jnp.bfloat16)
        start += ref.shape[0]


def column_block(rows, cols):
    return pl.BlockSpec((rows, cols), lambda j: (0, j))


def shift(x, axis, by):
    size = lax.axis_size(axis)
    return lax.ppermute(x, axis, [(i, (i + by) % size) for i in range(size)])


def gather_slots(block):
    parts = lax.axis_size("tensor")
    rank = lax.axis_index("tensor")
    cols = block.shape[1] // parts
    pieces = []
    for s in range(parts):
        piece = lax.dynamic_slice_in_dim(block, ((rank + s) % parts) * cols, cols, 1)
        pieces.append(piece if s == 0 else shift(piece, "tensor", s))
    mine = jnp.concatenate(pieces, axis=0)
    return [mine] + [shift(mine, "response", s) for s in range(1, lax.axis_size("response"))]


def reduce_slots(slots, scale):
    parts = lax.axis_size("tensor")
    rank = lax.axis_index("tensor")
    total = slots[0].astype(jnp.float32)
    for s in range(1, len(slots)):
        total = total + shift(slots[s], "response", -s).astype(jnp.float32)
    total = (total * scale).astype(jnp.bfloat16)
    rows, cols = total.shape[0] // parts, total.shape[1]
    result = jnp.zeros((rows, cols * parts), jnp.bfloat16)
    for s in range(parts):
        piece = total[s * rows : (s + 1) * rows]
        piece = piece if s == 0 else shift(piece, "tensor", -s)
        result = lax.dynamic_update_slice_in_dim(result, piece, ((rank + s) % parts) * cols, 1)
    return result


def sum_over(x, axis):
    size = lax.axis_size(axis)
    if size & (size - 1):
        terms = [x] + [shift(x, axis, s) for s in range(1, size)]
        return functools.reduce(jnp.add, terms)
    step = 1
    while step < size:
        x = x + shift(x, axis, step)
        step *= 2
    return x


def body(queries, keys, values, prefix_keys, prefix_values, lengths, out_grad):
    q, k, v, do = queries[0], keys[0], values[0], out_grad[0]
    rows = q.shape[0]
    heads = k.shape[1] // HD
    bf16 = jnp.bfloat16
    kslots = gather_slots(prefix_keys[0])
    vslots = gather_slots(prefix_values[0])
    n_slots = len(kslots)
    slot_rows = kslots[0].shape[0]
    n_keys = rows + n_slots * slot_rows
    length = lengths[0]
    live_total = sum_over(sum_over(length.astype(jnp.float32), "prompt"), "response")
    slots = rows * lax.axis_size("prompt") * lax.axis_size("response")
    weight = slots / live_total
    factor = 1.0 / math.sqrt(HD)
    smem = pl.BlockSpec(memory_space=pltpu.SMEM)
    wide = column_block(rows, GROUP * HD)
    own = column_block(rows, HD)
    slot = column_block(slot_rows, HD)
    p_block = pl.BlockSpec((1, n_keys, GROUP * rows), lambda j: (j, 0, 0))
    slot_shape = jax.ShapeDtypeStruct((slot_rows, heads * HD), bf16)
    params = pltpu.CompilerParams(vmem_limit_bytes=VMEM_LIMIT)
    pairs_wide = PAIR * rows
    unit = 2 * n_keys * GROUP * rows * HD * heads
    probs, dv_own, *dv_slots = pl.pallas_call(
        functools.partial(probs_kernel, n_slots, factor * math.log2(math.e)),
        grid=(heads,),
        in_specs=[smem, wide, wide, own] + [slot] * n_slots,
        out_specs=[p_block, own] + [slot] * n_slots,
        out_shape=[
            jax.ShapeDtypeStruct((heads, n_keys, GROUP * rows), bf16),
            jax.ShapeDtypeStruct((rows, heads * HD), jnp.float32),
        ]
        + [slot_shape] * n_slots,
        scratch_shapes=[pltpu.VMEM((2, n_keys, pairs_wide), jnp.float32)],
        compiler_params=params,
        cost_estimate=pl.CostEstimate(
            flops=2 * unit, bytes_accessed=2 * heads * n_keys * GROUP * rows, transcendentals=heads * n_keys * GROUP * rows
        ),
        name="probs",
    )(length, q, do, k, *kslots)
    output, query_grad, key_grad, value_grad, *dk_slots = pl.pallas_call(
        functools.partial(grads_kernel, n_slots, factor),
        grid=(heads,),
        in_specs=[smem, wide, wide, p_block, own, own, own] + [slot] * (2 * n_slots),
        out_specs=[wide, wide, own, own] + [slot] * n_slots,
        out_shape=[
            jax.ShapeDtypeStruct(q.shape, bf16),
            jax.ShapeDtypeStruct(q.shape, bf16),
            jax.ShapeDtypeStruct(k.shape, bf16),
            jax.ShapeDtypeStruct(k.shape, bf16),
        ]
        + [slot_shape] * n_slots,
        scratch_shapes=[
            pltpu.VMEM((2, n_keys, pairs_wide), jnp.float32),
            pltpu.VMEM((n_keys, GROUP * rows), bf16),
        ],
        compiler_params=params,
        cost_estimate=pl.CostEstimate(
            flops=4 * unit, bytes_accessed=2 * heads * n_keys * GROUP * rows, transcendentals=0
        ),
        name="grads",
    )(weight, q, do, probs, dv_own, k, v, *kslots, *vslots)
    prefix_value_grad = reduce_slots(dv_slots, weight)
    prefix_key_grad = reduce_slots(dk_slots, weight * factor)
    return tuple(
        x[None]
        for x in (output, query_grad, key_grad, value_grad, prefix_key_grad, prefix_value_grad)
    )


def solution(mesh):
    in_specs = (
        P("prompt", "response", "tensor"),
        P("prompt", "response", "tensor"),
        P("prompt", "response", "tensor"),
        P("prompt", ("response", "tensor"), None),
        P("prompt", ("response", "tensor"), None),
        P("prompt", "response"),
        P("prompt", "response", "tensor"),
    )
    out_specs = (
        P("prompt", "response", "tensor"),
        P("prompt", "response", "tensor"),
        P("prompt", "response", "tensor"),
        P("prompt", "response", "tensor"),
        P("prompt", ("response", "tensor"), None),
        P("prompt", ("response", "tensor"), None),
    )
    return jax.shard_map(body, mesh=mesh, in_specs=in_specs, out_specs=out_specs, check_vma=False)
```

```python
import functools
import math

import jax
import jax.numpy as jnp
from jax import lax
from jax.experimental import pallas as pl
from jax.experimental.pallas import tpu as pltpu
from jax.sharding import PartitionSpec as P

HD = 128
GROUP = 8
PAIR = 2
VMEM_LIMIT = 60 * 1024 * 1024
NT = (((1,), (1,)), ((), ()))


def heads_down(ref, first, count):
    return jnp.concatenate(
        [ref[:, (first + i) * HD : (first + i + 1) * HD] for i in range(count)], axis=0
    )


def probs_kernel(n_slots, scale, length_ref, q_ref, do_ref, kown_ref, *refs):
    slot_refs = refs[:n_slots]
    p_ref, dvown_ref = refs[n_slots : n_slots + 2]
    dv_refs = refs[n_slots + 2 : 2 * n_slots + 2]
    s_ref = refs[2 * n_slots + 2]
    rows = q_ref.shape[0]
    own = kown_ref.shape[0]
    keys = jnp.concatenate([kown_ref[...]] + [ref[...] for ref in slot_refs], axis=0)
    width = PAIR * rows
    key_pos = lax.broadcasted_iota(jnp.int32, (own, width), 0)
    row_pos = lax.broadcasted_iota(jnp.int32, (own, width), 1) % rows
    allowed = key_pos <= row_pos
    live = (lax.broadcasted_iota(jnp.int32, (1, width), 1) % rows) < length_ref[0]
    for pair in range(GROUP // PAIR):
        here = s_ref.at[pair % 2]
        cols = slice(pair * width, (pair + 1) * width)
        here[...] = lax.dot_general(
            keys, heads_down(q_ref, pair * PAIR, PAIR), NT, preferred_element_type=jnp.float32
        )
        here[:own] = jnp.where(allowed, here[:own], -1e30)
        top = jnp.max(here[...], axis=0, keepdims=True) * scale
        exponent = jnp.exp2(here[...] * scale - top)
        here[...] = exponent
        total = jnp.sum(exponent, axis=0, keepdims=True)
        inverse = jnp.where(live, 1.0 / total, 0.0)
        p_ref[0, :, cols] = (here[...] * inverse).astype(jnp.bfloat16)
    dv = jnp.dot(p_ref[0], heads_down(do_ref, 0, GROUP), preferred_element_type=jnp.float32)
    dvown_ref[...] = dv[:own]
    start = own
    for ref in dv_refs:
        ref[...] = dv[start : start + ref.shape[0]].astype(jnp.bfloat16)
        start += ref.shape[0]


def grads_kernel(n_slots, factor, weight_ref, q_ref, do_ref, p_ref, dv_ref, kown_ref, vown_ref, *refs):
    kslot_refs = refs[:n_slots]
    vslot_refs = refs[n_slots : 2 * n_slots]
    out_ref, dq_ref, dkown_ref, dvown_ref = refs[2 * n_slots : 2 * n_slots + 4]
    dk_refs = refs[2 * n_slots + 4 : 3 * n_slots + 4]
    dp_ref, ds_ref = refs[3 * n_slots + 4 :]
    rows = q_ref.shape[0]
    own = kown_ref.shape[0]
    weight = weight_ref[0]
    keys = jnp.concatenate([kown_ref[...]] + [ref[...] for ref in kslot_refs], axis=0)
    values = jnp.concatenate([vown_ref[...]] + [ref[...] for ref in vslot_refs], axis=0)
    keys_t = keys.T
    values_t = values.T
    width = PAIR * rows
    for pair in range(GROUP // PAIR):
        here = dp_ref.at[pair % 2]
        cols = slice(pair * width, (pair + 1) * width)
        do = heads_down(do_ref, pair * PAIR, PAIR)
        here[...] = lax.dot_general(values, do, NT, preferred_element_type=jnp.float32)
        attended = jnp.dot(values_t, p_ref[0, :, cols], preferred_element_type=jnp.float32)
        centre = jnp.sum(attended * do.astype(jnp.float32).T, axis=0, keepdims=True)
        ds_ref[:, cols] = (
            p_ref[0, :, cols].astype(jnp.float32) * (here[...] - centre)
        ).astype(jnp.bfloat16)
        dq = jnp.dot(keys_t, ds_ref[:, cols], preferred_element_type=jnp.float32) * (factor * weight)
        for i in range(PAIR):
            head = slice((pair * PAIR + i) * HD, (pair * PAIR + i + 1) * HD)
            lanes = slice(i * rows, (i + 1) * rows)
            out_ref[:, head] = attended[:, lanes].T.astype(jnp.bfloat16)
            dq_ref[:, head] = dq[:, lanes].T.astype(jnp.bfloat16)
    dk = jnp.dot(ds_ref[...], heads_down(q_ref, 0, GROUP), preferred_element_type=jnp.float32)
    dkown_ref[...] = (dk[:own] * (factor * weight)).astype(jnp.bfloat16)
    dvown_ref[...] = (dv_ref[...] * weight).astype(jnp.bfloat16)
    start = own
    for ref in dk_refs:
        ref[...] = dk[start : start + ref.shape[0]].astype(jnp.bfloat16)
        start += ref.shape[0]


def column_block(rows, cols):
    return pl.BlockSpec((rows, cols), lambda j: (0, j))


def shift(x, axis, by):
    size = lax.axis_size(axis)
    return lax.ppermute(x, axis, [(i, (i + by) % size) for i in range(size)])


def exchange(x):
    return lax.all_to_all(x, ("response", "tensor"), split_axis=0, concat_axis=0, tiled=True)


def gather_prefix(block):
    parts = lax.axis_size("tensor")
    cut = jnp.split(block, parts, axis=1)
    return exchange(jnp.concatenate(cut * lax.axis_size("response"), axis=0))


def reduce_prefix(terms, scale):
    parts = lax.axis_size("tensor")
    cols = terms.shape[1]
    pieces = exchange(terms).reshape(lax.axis_size("response"), parts, -1, cols)
    total = jnp.sum(pieces.astype(jnp.float32), axis=0) * scale
    total = total.astype(jnp.bfloat16)
    return jnp.concatenate([total[i] for i in range(parts)], axis=1)


def sum_over(x, axis):
    terms = [x] + [shift(x, axis, s) for s in range(1, lax.axis_size(axis))]
    return functools.reduce(jnp.add, terms)


def body(queries, keys, values, prefix_keys, prefix_values, lengths, out_grad):
    q, k, v, do = queries[0], keys[0], values[0], out_grad[0]
    rows = q.shape[0]
    heads = k.shape[1] // HD
    bf16 = jnp.bfloat16
    kslots = [gather_prefix(prefix_keys[0])]
    vslots = [gather_prefix(prefix_values[0])]
    n_slots = len(kslots)
    slot_rows = kslots[0].shape[0]
    n_keys = rows + n_slots * slot_rows
    length = lengths[0]
    live_total = sum_over(sum_over(length.astype(jnp.float32), "prompt"), "response")
    slots = rows * lax.axis_size("prompt") * lax.axis_size("response")
    weight = slots / live_total
    factor = 1.0 / math.sqrt(HD)
    smem = pl.BlockSpec(memory_space=pltpu.SMEM)
    wide = column_block(rows, GROUP * HD)
    own = column_block(rows, HD)
    slot = column_block(slot_rows, HD)
    p_block = pl.BlockSpec((1, n_keys, GROUP * rows), lambda j: (j, 0, 0))
    slot_shape = jax.ShapeDtypeStruct((slot_rows, heads * HD), bf16)
    params = pltpu.CompilerParams(vmem_limit_bytes=VMEM_LIMIT)
    pairs_wide = PAIR * rows
    unit = 2 * n_keys * GROUP * rows * HD * heads
    probs, dv_own, *dv_slots = pl.pallas_call(
        functools.partial(probs_kernel, n_slots, factor * math.log2(math.e)),
        grid=(heads,),
        in_specs=[smem, wide, wide, own] + [slot] * n_slots,
        out_specs=[p_block, own] + [slot] * n_slots,
        out_shape=[
            jax.ShapeDtypeStruct((heads, n_keys, GROUP * rows), bf16),
            jax.ShapeDtypeStruct((rows, heads * HD), jnp.float32),
        ]
        + [slot_shape] * n_slots,
        scratch_shapes=[pltpu.VMEM((2, n_keys, pairs_wide), jnp.float32)],
        compiler_params=params,
        cost_estimate=pl.CostEstimate(
            flops=2 * unit, bytes_accessed=2 * heads * n_keys * GROUP * rows, transcendentals=heads * n_keys * GROUP * rows
        ),
        name="probs",
    )(length, q, do, k, *kslots)
    output, query_grad, key_grad, value_grad, *dk_slots = pl.pallas_call(
        functools.partial(grads_kernel, n_slots, factor),
        grid=(heads,),
        in_specs=[smem, wide, wide, p_block, own, own, own] + [slot] * (2 * n_slots),
        out_specs=[wide, wide, own, own] + [slot] * n_slots,
        out_shape=[
            jax.ShapeDtypeStruct(q.shape, bf16),
            jax.ShapeDtypeStruct(q.shape, bf16),
            jax.ShapeDtypeStruct(k.shape, bf16),
            jax.ShapeDtypeStruct(k.shape, bf16),
        ]
        + [slot_shape] * n_slots,
        scratch_shapes=[
            pltpu.VMEM((2, n_keys, pairs_wide), jnp.float32),
            pltpu.VMEM((n_keys, GROUP * rows), bf16),
        ],
        compiler_params=params,
        cost_estimate=pl.CostEstimate(
            flops=4 * unit, bytes_accessed=2 * heads * n_keys * GROUP * rows, transcendentals=0
        ),
        name="grads",
    )(weight, q, do, probs, dv_own, k, v, *kslots, *vslots)
    prefix_value_grad = reduce_prefix(dv_slots[0], weight)
    prefix_key_grad = reduce_prefix(dk_slots[0], weight * factor)
    return tuple(
        x[None]
        for x in (output, query_grad, key_grad, value_grad, prefix_key_grad, prefix_value_grad)
    )


def solution(mesh):
    in_specs = (
        P("prompt", "response", "tensor"),
        P("prompt", "response", "tensor"),
        P("prompt", "response", "tensor"),
        P("prompt", ("response", "tensor"), None),
        P("prompt", ("response", "tensor"), None),
        P("prompt", "response"),
        P("prompt", "response", "tensor"),
    )
    out_specs = (
        P("prompt", "response", "tensor"),
        P("prompt", "response", "tensor"),
        P("prompt", "response", "tensor"),
        P("prompt", "response", "tensor"),
        P("prompt", ("response", "tensor"), None),
        P("prompt", ("response", "tensor"), None),
    )
    return jax.shard_map(body, mesh=mesh, in_specs=in_specs, out_specs=out_specs, check_vma=False)
```

```python
import functools
import math

import jax
import jax.numpy as jnp
from jax import lax
from jax.experimental import pallas as pl
from jax.experimental.pallas import tpu as pltpu
from jax.sharding import PartitionSpec as P

HD = 128
GROUP = 8
PAIR = 2
CHUNKS = 2
VMEM_LIMIT = 48 * 1024 * 1024
NT = (((1,), (1,)), ((), ()))


def heads_down(ref, first, count):
    return jnp.concatenate(
        [ref[:, (first + i) * HD : (first + i + 1) * HD] for i in range(count)], axis=0
    )


def attend_kernel(n_slots, count, first, factor, carried, *refs):
    length_ref, total_ref, q_hbm, do_hbm, kown_hbm, vown_hbm = refs[:6]
    slot_refs = refs[6 : 6 + n_slots]
    refs = refs[6 + n_slots + carried :]
    out_hbm, dq_hbm, dkown_hbm, dvown_hbm = refs[:4]
    dslot_refs = refs[4 : 4 + n_slots]
    refs = refs[4 + n_slots :]
    q_ref, do_ref, kown_ref, vown_ref, out_ref, dq_ref, dkown_ref, dvown_ref = refs[:8]
    s_ref, dp_ref, p_ref, ds_ref, in_sem, out_sem = refs[8:]

    def columns(head, cols):
        return pl.ds((first + head) * cols, cols)

    loads = []
    for head in range(count):
        loads.append(
            [
                pltpu.make_async_copy(
                    hbm.at[:, columns(head, size)], ref.at[head], in_sem.at[head, i]
                )
                for i, (hbm, ref, size) in enumerate(
                    [
                        (kown_hbm, kown_ref, HD),
                        (q_hbm, q_ref, GROUP * HD),
                        (vown_hbm, vown_ref, HD),
                        (do_hbm, do_ref, GROUP * HD),
                    ]
                )
            ]
        )
        for copy in loads[-1]:
            copy.start()
    stores = []

    def store(ref, hbm, head, size, i):
        copy = pltpu.make_async_copy(ref.at[head], hbm.at[:, columns(head, size)], out_sem.at[head, i])
        copy.start()
        stores.append(copy)

    rows = q_ref.shape[1]
    own = kown_ref.shape[1]
    half = slot_refs[0].shape[0] // 2
    weight = total_ref[0]
    scale = factor * math.log2(math.e)
    width = PAIR * rows
    key_pos = lax.broadcasted_iota(jnp.int32, (own, width), 0)
    row_pos = lax.broadcasted_iota(jnp.int32, (own, width), 1) % rows
    allowed = key_pos <= row_pos
    live = (lax.broadcasted_iota(jnp.int32, (1, width), 1) % rows) < length_ref[0]
    for head in range(count):
        for copy in loads[head]:
            copy.wait()
        here = slice(head * HD, (head + 1) * HD)
        keys = jnp.concatenate([kown_ref[head]] + [ref[:half, here] for ref in slot_refs], axis=0)
        values = jnp.concatenate([vown_ref[head]] + [ref[half:, here] for ref in slot_refs], axis=0)
        keys_t = keys.T
        values_t = values.T
        for pair in range(GROUP // PAIR):
            s_now, dp_now = s_ref.at[pair % 2], dp_ref.at[pair % 2]
            cols = slice(pair * width, (pair + 1) * width)
            do = heads_down(do_ref.at[head], pair * PAIR, PAIR)
            s_now[...] = lax.dot_general(
                keys,
                heads_down(q_ref.at[head], pair * PAIR, PAIR),
                NT,
                preferred_element_type=jnp.float32,
            )
            dp_now[...] = lax.dot_general(values, do, NT, preferred_element_type=jnp.float32)
            s_now[:own] = jnp.where(allowed, s_now[:own], -1e30)
            top = jnp.max(s_now[...], axis=0, keepdims=True) * scale
            exponent = jnp.exp2(s_now[...] * scale - top)
            s_now[...] = exponent
            total = jnp.sum(exponent, axis=0, keepdims=True)
            inverse = jnp.where(live, 1.0 / total, 0.0)
            p_ref[:, cols] = (s_now[...] * inverse).astype(jnp.bfloat16)
            attended = jnp.dot(values_t, p_ref[:, cols], preferred_element_type=jnp.float32)
            centre = jnp.sum(attended * do.astype(jnp.float32).T, axis=0, keepdims=True)
            ds_ref[:, cols] = (
                p_ref[:, cols].astype(jnp.float32) * (dp_now[...] - centre)
            ).astype(jnp.bfloat16)
            dq = jnp.dot(keys_t, ds_ref[:, cols], preferred_element_type=jnp.float32)
            dq = dq * (factor * weight)
            for i in range(PAIR):
                lanes = slice(i * rows, (i + 1) * rows)
                place = slice((pair * PAIR + i) * HD, (pair * PAIR + i + 1) * HD)
                out_ref[head, :, place] = attended[:, lanes].T.astype(jnp.bfloat16)
                dq_ref[head, :, place] = dq[:, lanes].T.astype(jnp.bfloat16)
        store(out_ref, out_hbm, head, GROUP * HD, 0)
        store(dq_ref, dq_hbm, head, GROUP * HD, 1)
        dv = jnp.dot(
            p_ref[...], heads_down(do_ref.at[head], 0, GROUP), preferred_element_type=jnp.float32
        )
        dv = (dv * weight).astype(jnp.bfloat16)
        dk = jnp.dot(
            ds_ref[...], heads_down(q_ref.at[head], 0, GROUP), preferred_element_type=jnp.float32
        )
        dk = (dk * (factor * weight)).astype(jnp.bfloat16)
        dkown_ref[head] = dk[:own]
        dvown_ref[head] = dv[:own]
        store(dkown_ref, dkown_hbm, head, HD, 2)
        store(dvown_ref, dvown_hbm, head, HD, 3)
        for slot, ref in enumerate(dslot_refs):
            part = slice(own + slot * half, own + (slot + 1) * half)
            ref[:half, here] = dk[part]
            ref[half:, here] = dv[part]
    for copy in stores:
        copy.wait()


def swap(x, axis, by):
    return lax.ppermute(x, axis, [(i, i ^ by) for i in range(lax.axis_size(axis))])


def inner(axis):
    rank = lax.axis_index(axis)
    return (rank == 1) | (rank == 2)


def line_gather(block, relay, after=None):
    size = lax.axis_size("response")
    if size != 4 or not relay:
        if after is not None:
            block, after = lax.optimization_barrier((block, after))
        return [block] + [swap(block, "response", m) for m in range(1, size)], after
    far = swap(block, "response", 3)
    near = swap(block, "response", 1)
    onward = jnp.where(inner("response"), far, block)
    onward, after = lax.optimization_barrier((onward, after))
    cycle = [(1, 0), (3, 1), (2, 3), (0, 2)]
    return [block, near, lax.ppermute(onward, "response", cycle), far], after


def line_reduce(slots, relay, after):
    size = lax.axis_size("response")
    wide = jnp.float32
    if size != 4 or not relay:
        terms = [slots[0]] + [swap(slots[m], "response", m) for m in range(1, size)]
        return functools.reduce(jnp.add, [term.astype(wide) for term in terms]), after
    across = lax.ppermute(slots[2], "response", [(0, 1), (1, 3), (3, 2), (2, 0)]).astype(wide)
    near = swap(slots[1], "response", 1)
    mid = inner("response")
    onward = (slots[3].astype(wide) + jnp.where(mid, across, 0.0)).astype(slots[3].dtype)
    onward, after = lax.optimization_barrier((onward, after))
    far = swap(onward, "response", 3)
    total = slots[0].astype(wide) + near.astype(wide) + far.astype(wide)
    return total + jnp.where(mid, 0.0, across), after


def own_columns(block, chunk, by):
    cols = block.shape[1] // (lax.axis_size("tensor") * CHUNKS)
    rank = lax.axis_index("tensor") ^ by
    return lax.dynamic_slice_in_dim(block, (rank * CHUNKS + chunk) * cols, cols, 1)


def tensor_gather(blocks, chunk):
    parts = lax.axis_size("tensor")
    pieces = []
    for m in range(parts):
        piece = jnp.concatenate([own_columns(block, chunk, m) for block in blocks], axis=0)
        pieces.append(piece if m == 0 else swap(piece, "tensor", m))
    rows = blocks[0].shape[0]
    return jnp.concatenate(
        [piece[i * rows : (i + 1) * rows] for i in range(len(blocks)) for piece in pieces], axis=0
    )


def tensor_spread(total, n_arrays):
    parts = lax.axis_size("tensor")
    rows = total.shape[0] // (n_arrays * parts)
    pieces = []
    for m in range(parts):
        piece = jnp.concatenate(
            [total[(i * parts + m) * rows : (i * parts + m + 1) * rows] for i in range(n_arrays)],
            axis=0,
        )
        pieces.append(piece if m == 0 else swap(piece, "tensor", m))
    return pieces


def whole_columns(chunk_pieces, array):
    parts = lax.axis_size("tensor")
    rank = lax.axis_index("tensor")
    rows = chunk_pieces[0][0].shape[0] // 2
    by_rank = [
        jnp.concatenate([pieces[m][array * rows : (array + 1) * rows] for pieces in chunk_pieces], axis=1)
        for m in range(parts)
    ]
    ordered = []
    for t in range(parts):
        column = by_rank[0]
        for m in range(1, parts):
            column = jnp.where(rank ^ m == t, by_rank[m], column)
        ordered.append(column)
    return jnp.concatenate(ordered, axis=1)


def sum_over(x, axis):
    return functools.reduce(jnp.add, [x] + [swap(x, axis, m) for m in range(1, lax.axis_size(axis))])


def attend(chunk, heads, slots, length, weight, q, do, k, v, carried):
    rows = q.shape[0]
    n_slots = len(slots)
    slot_rows = slots[0].shape[0] // 2
    n_keys = rows + n_slots * slot_rows
    count = heads // CHUNKS
    first = chunk * count
    bf16 = jnp.bfloat16
    smem = pl.BlockSpec(memory_space=pltpu.SMEM)
    hbm = pl.BlockSpec(memory_space=pltpu.HBM)
    vmem = pl.BlockSpec(memory_space=pltpu.VMEM)
    like = lambda x: jax.ShapeDtypeStruct(x.shape, bf16)
    unit = 2 * n_keys * GROUP * rows * HD * count
    pair_buffer = pltpu.VMEM((2, n_keys, PAIR * rows), jnp.float32)
    group_buffer = pltpu.VMEM((n_keys, GROUP * rows), bf16)
    wide = pltpu.VMEM((count, rows, GROUP * HD), bf16)
    own = pltpu.VMEM((count, rows, HD), bf16)
    return pl.pallas_call(
        functools.partial(
            attend_kernel, n_slots, count, first, 1.0 / math.sqrt(HD), len(carried)
        ),
        in_specs=[smem, smem] + [hbm] * 4 + [vmem] * n_slots + [hbm] * len(carried),
        out_specs=[hbm] * 4 + [vmem] * n_slots,
        out_shape=[like(q), like(q), like(k), like(v)] + [like(x) for x in slots],
        input_output_aliases={6 + n_slots + i: i for i in range(len(carried))},
        scratch_shapes=[wide, wide, own, own, wide, wide, own, own]
        + [pair_buffer, pair_buffer, group_buffer, group_buffer]
        + [pltpu.SemaphoreType.DMA((count, 4))] * 2,
        compiler_params=pltpu.CompilerParams(vmem_limit_bytes=VMEM_LIMIT),
        cost_estimate=pl.CostEstimate(
            flops=24 * unit,
            bytes_accessed=8 * rows * GROUP * HD * count,
            transcendentals=count * n_keys * GROUP * rows,
        ),
        name=f"attend_{chunk}",
    )(length, weight, q, do, k, v, *slots, *carried)


def body(queries, keys, values, prefix_keys, prefix_values, lengths, out_grad):
    q, k, v, do = queries[0], keys[0], values[0], out_grad[0]
    heads = k.shape[1] // HD
    length = lengths[0]
    prefix = (prefix_keys[0], prefix_values[0])
    prompt_total = sum_over(length.astype(jnp.float32), "prompt")
    blocks = [tensor_gather(prefix, chunk) for chunk in range(CHUNKS)]
    slots, (prompt_total, *blocks[1:]) = line_gather(blocks[0], True, (prompt_total, *blocks[1:]))
    live_total = sum_over(prompt_total, "response")
    weight = q.shape[0] * lax.axis_size("prompt") * lax.axis_size("response") / live_total
    chunk_pieces, carried, total = [], [], ()
    for chunk in range(CHUNKS):
        if chunk + 1 < CHUNKS:
            next_slots, _ = line_gather(blocks[chunk + 1], False)
        results = attend(chunk, heads, slots, length, weight, q, do, k, v, carried)
        carried = list(results[:4])
        terms, total = lax.optimization_barrier((results[4:], total))
        last = chunk + 1 == CHUNKS
        new_total, total = line_reduce(terms, last, total)
        if chunk:
            chunk_pieces.append(tensor_spread(total, len(prefix)))
        total = new_total.astype(jnp.bfloat16)
        slots = next_slots
    chunk_pieces.append(tensor_spread(total, len(prefix)))
    grads = [whole_columns(chunk_pieces, array) for array in range(len(prefix))]
    return tuple(x[None] for x in (*carried, *grads))


def solution(mesh):
    in_specs = (
        P("prompt", "response", "tensor"),
        P("prompt", "response", "tensor"),
        P("prompt", "response", "tensor"),
        P("prompt", ("response", "tensor"), None),
        P("prompt", ("response", "tensor"), None),
        P("prompt", "response"),
        P("prompt", "response", "tensor"),
    )
    out_specs = (
        P("prompt", "response", "tensor"),
        P("prompt", "response", "tensor"),
        P("prompt", "response", "tensor"),
        P("prompt", "response", "tensor"),
        P("prompt", ("response", "tensor"), None),
        P("prompt", ("response", "tensor"), None),
    )
    return jax.shard_map(body, mesh=mesh, in_specs=in_specs, out_specs=out_specs, check_vma=False)
```

```python
import functools
import math

import jax
import jax.numpy as jnp
from jax import lax
from jax.experimental import pallas as pl
from jax.experimental.pallas import tpu as pltpu
from jax.sharding import PartitionSpec as P

HD = 128
GROUP = 8
PAIR = 2
CHUNKS = 2
EXTRA = 16
VMEM_LIMIT = 52 * 1024 * 1024
NT = (((1,), (1,)), ((), ()))


def heads_down(ref, first, count):
    return jnp.concatenate(
        [ref[:, (first + i) * HD : (first + i + 1) * HD] for i in range(count)], axis=0
    )


def attend_kernel(n_slots, count, chunk, factor, *refs):
    last = chunk + 1 == CHUNKS
    length_ref, q_hbm, do_hbm, kown_hbm, vown_hbm = refs[:5]
    slot_refs, refs = refs[5 : 5 + n_slots], refs[5 + n_slots :]
    if last:
        slots_all, refs = refs[0], refs[1:]
        carried, refs = refs[1:4], refs[4:]
        out_hbm, dq_hbm, dkown_hbm, dvown_hbm, weight_ref = refs[:5]
        refs = refs[5:]
    else:
        out_hbm, dq_ref, dkown_ref, dvown_ref = refs[:4]
        refs = refs[4:]
    term_refs, refs = refs[:n_slots], refs[n_slots:]
    q_ref, do_ref, kown_ref, vown_ref, out_ref, s_ref, dp_ref, p_ref, ds_ref = refs[:9]
    in_sem, out_sem = refs[9:11]
    if last:
        dq_ref, dkown_ref, dvown_ref = refs[11:]
    first = chunk * count

    def columns(head, size):
        return pl.ds(head * size, size)

    loads = []
    for head in range(count):
        loads.append(
            [
                pltpu.make_async_copy(
                    hbm.at[:, columns(first + head, size)],
                    ref.at[:, columns(head, size)],
                    in_sem.at[head, i],
                )
                for i, (hbm, ref, size) in enumerate(
                    [
                        (kown_hbm, kown_ref, HD),
                        (q_hbm, q_ref, GROUP * HD),
                        (vown_hbm, vown_ref, HD),
                        (do_hbm, do_ref, GROUP * HD),
                    ]
                )
            ]
        )
        for copy in loads[-1]:
            copy.start()
    stores = []

    def store(ref, head, hbm, to, size, i):
        copy = pltpu.make_async_copy(
            ref.at[:, columns(head, size)], hbm.at[:, columns(to, size)], out_sem.at[to, i]
        )
        copy.start()
        stores.append(copy)

    rows = q_ref.shape[0]
    own = kown_ref.shape[0]
    held = term_refs[0].shape[0] // 2
    scale = factor * math.log2(math.e)
    weight = jnp.ones((1, 1), jnp.float32)
    if last:
        totals = [ref[2 * held :, :HD].astype(jnp.float32) for ref in slot_refs]
        totals = functools.reduce(jnp.add, totals)
        live_total = totals[:1] * 256 + totals[EXTRA // 2 : EXTRA // 2 + 1]
        weight_row = slots_all[0] / live_total
        weight_ref[...] = jnp.broadcast_to(weight_row, weight_ref.shape)
        weight = weight_row[:, :1]
        for source, ref, hbm, size, i in (
            (carried[0], dq_ref, dq_hbm, GROUP * HD, 1),
            (carried[1], dkown_ref, dkown_hbm, HD, 2),
            (carried[2], dvown_ref, dvown_hbm, HD, 3),
        ):
            for head in range(first):
                cols = slice(head * size, (head + 1) * size)
                ref[:, cols] = (source[:, cols].astype(jnp.float32) * weight).astype(jnp.bfloat16)
                store(ref, head, hbm, head, size, i)
    grad_scale = weight * factor
    base = first if last else 0
    width = PAIR * rows
    key_pos = lax.broadcasted_iota(jnp.int32, (own, width), 0)
    row_pos = lax.broadcasted_iota(jnp.int32, (own, width), 1) % rows
    allowed = key_pos <= row_pos
    live = (lax.broadcasted_iota(jnp.int32, (1, width), 1) % rows) < length_ref[0]
    for head in range(count):
        for copy in loads[head]:
            copy.wait()
        here = slice(head * HD, (head + 1) * HD)
        q_at = head * GROUP
        keys = jnp.concatenate(
            [kown_ref[:, here]] + [ref[:held, here] for ref in slot_refs], axis=0
        )
        values = jnp.concatenate(
            [vown_ref[:, here]] + [ref[held : 2 * held, here] for ref in slot_refs], axis=0
        )
        keys_t = keys.T
        values_t = values.T
        for pair in range(GROUP // PAIR):
            s_now, dp_now = s_ref.at[pair % 2], dp_ref.at[pair % 2]
            cols = slice(pair * width, (pair + 1) * width)
            do = heads_down(do_ref, q_at + pair * PAIR, PAIR)
            s_now[...] = lax.dot_general(
                keys,
                heads_down(q_ref, q_at + pair * PAIR, PAIR),
                NT,
                preferred_element_type=jnp.float32,
            )
            dp_now[...] = lax.dot_general(values, do, NT, preferred_element_type=jnp.float32)
            s_now[:own] = jnp.where(allowed, s_now[:own], -1e30)
            top = jnp.max(s_now[...], axis=0, keepdims=True) * scale
            exponent = jnp.exp2(s_now[...] * scale - top)
            s_now[...] = exponent
            total = jnp.sum(exponent, axis=0, keepdims=True)
            inverse = jnp.where(live, 1.0 / total, 0.0)
            p_ref[:, cols] = (s_now[...] * inverse).astype(jnp.bfloat16)
            attended = jnp.dot(values_t, p_ref[:, cols], preferred_element_type=jnp.float32)
            centre = jnp.sum(attended * do.astype(jnp.float32).T, axis=0, keepdims=True)
            ds_ref[:, cols] = (
                p_ref[:, cols].astype(jnp.float32) * (dp_now[...] - centre)
            ).astype(jnp.bfloat16)
            dq = jnp.dot(keys_t, ds_ref[:, cols], preferred_element_type=jnp.float32) * grad_scale
            for i in range(PAIR):
                lanes = slice(i * rows, (i + 1) * rows)
                at = pair * PAIR + i
                place = slice((q_at + at) * HD, (q_at + at + 1) * HD)
                out_ref[:, place] = attended[:, lanes].T.astype(jnp.bfloat16)
                place = slice((base * GROUP + q_at + at) * HD, (base * GROUP + q_at + at + 1) * HD)
                dq_ref[:, place] = dq[:, lanes].T.astype(jnp.bfloat16)
        store(out_ref, head, out_hbm, first + head, GROUP * HD, 0)
        dv = jnp.dot(
            p_ref[...], heads_down(do_ref, q_at, GROUP), preferred_element_type=jnp.float32
        )
        dk = jnp.dot(
            ds_ref[...], heads_down(q_ref, q_at, GROUP), preferred_element_type=jnp.float32
        )
        place = slice((base + head) * HD, (base + head + 1) * HD)
        dk = (dk * grad_scale).astype(jnp.bfloat16)
        dv = (dv * weight).astype(jnp.bfloat16)
        dkown_ref[:, place] = dk[:own]
        dvown_ref[:, place] = dv[:own]
        if last:
            store(dq_ref, first + head, dq_hbm, first + head, GROUP * HD, 1)
            store(dkown_ref, first + head, dkown_hbm, first + head, HD, 2)
            store(dvown_ref, first + head, dvown_hbm, first + head, HD, 3)
        for i, ref in enumerate(term_refs):
            part = slice(own + i * held, own + (i + 1) * held)
            ref[:held, here] = dk[part]
            ref[held:, here] = dv[part]
    for copy in stores:
        copy.wait()


def swap(x, axis, by):
    return lax.ppermute(x, axis, [(i, i ^ by) for i in range(lax.axis_size(axis))])


def sum_over(x, axis):
    by = 1
    while by < lax.axis_size(axis):
        x = x + swap(x, axis, by)
        by *= 2
    return x


def line_gather(block):
    return [block] + [swap(block, "response", m) for m in range(1, lax.axis_size("response"))]


def line_reduce(slots, scale):
    terms = [slots[0]] + [swap(slots[m], "response", m) for m in range(1, len(slots))]
    total = functools.reduce(jnp.add, [term.astype(jnp.float32) for term in terms])
    return (total * scale).astype(slots[0].dtype)


def own_columns(block, chunk, by):
    cols = block.shape[1] // (lax.axis_size("tensor") * CHUNKS)
    rank = lax.axis_index("tensor") ^ by
    return lax.dynamic_slice_in_dim(block, (rank * CHUNKS + chunk) * cols, cols, 1)


def tensor_gather(blocks, chunk):
    parts = lax.axis_size("tensor")
    pieces = []
    for m in range(parts):
        piece = jnp.concatenate([own_columns(block, chunk, m) for block in blocks], axis=0)
        pieces.append(piece if m == 0 else swap(piece, "tensor", m))
    rows = blocks[0].shape[0]
    return jnp.concatenate(
        [piece[i * rows : (i + 1) * rows] for i in range(len(blocks)) for piece in pieces], axis=0
    )


def tensor_spread(total, n_arrays):
    parts = lax.axis_size("tensor")
    rows = total.shape[0] // (n_arrays * parts)
    pieces = []
    for m in range(parts):
        piece = jnp.concatenate(
            [total[(i * parts + m) * rows : (i * parts + m + 1) * rows] for i in range(n_arrays)],
            axis=0,
        )
        pieces.append(piece if m == 0 else swap(piece, "tensor", m))
    return pieces


def whole_columns(chunk_pieces, array):
    parts = lax.axis_size("tensor")
    rank = lax.axis_index("tensor")
    rows = chunk_pieces[0][0].shape[0] // 2
    by_rank = [
        jnp.concatenate([pieces[m][array * rows : (array + 1) * rows] for pieces in chunk_pieces], axis=1)
        for m in range(parts)
    ]
    ordered = []
    for t in range(parts):
        column = by_rank[0]
        for m in range(1, parts):
            column = jnp.where(rank ^ m == t, by_rank[m], column)
        ordered.append(column)
    return jnp.concatenate(ordered, axis=1)


SMEM = pl.BlockSpec(memory_space=pltpu.SMEM)
HBM = pl.BlockSpec(memory_space=pltpu.HBM)
VMEM = pl.BlockSpec(memory_space=pltpu.VMEM)


def like(x):
    return jax.ShapeDtypeStruct(x.shape, x.dtype)


def attend(chunk, slots, length, q, do, k, v, slots_all, carried):
    rows = q.shape[0]
    heads = k.shape[1] // HD
    count = heads // CHUNKS
    n_slots = len(slots)
    last = chunk + 1 == CHUNKS
    held = (slots[0].shape[0] - EXTRA * last) // 2
    n_keys = rows + n_slots * held
    bf16 = jnp.bfloat16
    unit = 2 * n_keys * GROUP * rows * HD * count
    pair_buffer = pltpu.VMEM((2, n_keys, PAIR * rows), jnp.float32)
    group_buffer = pltpu.VMEM((n_keys, GROUP * rows), bf16)
    wide = pltpu.VMEM((rows, count * GROUP * HD), bf16)
    own = pltpu.VMEM((rows, count * HD), bf16)
    scratch = [wide, wide, own, own, wide, pair_buffer, pair_buffer, group_buffer, group_buffer]
    scratch += [pltpu.SemaphoreType.DMA((count, 4)), pltpu.SemaphoreType.DMA((heads, 4))]
    terms = [jax.ShapeDtypeStruct((2 * held, count * HD), bf16)] * n_slots
    in_specs = [SMEM] + [HBM] * 4 + [VMEM] * n_slots
    if last:
        in_specs += [SMEM, HBM] + [VMEM] * 3
        out_specs = [HBM] * 4 + [VMEM] * (1 + n_slots)
        out_shape = [like(q), like(q), like(k), like(v)]
        out_shape += [jax.ShapeDtypeStruct((8, HD), jnp.float32)] + terms
        scratch += [pltpu.VMEM(x.shape, bf16) for x in (q, k, v)]
        operands = [slots_all, *carried]
    else:
        out_specs = [HBM] + [VMEM] * (3 + n_slots)
        part = lambda x: jax.ShapeDtypeStruct((x.shape[0], x.shape[1] // CHUNKS), bf16)
        out_shape = [like(q), part(q), part(k), part(v)] + terms
        operands = []
    return pl.pallas_call(
        functools.partial(attend_kernel, n_slots, count, chunk, 1.0 / math.sqrt(HD)),
        in_specs=in_specs,
        out_specs=out_specs,
        out_shape=out_shape,
        input_output_aliases={6 + n_slots: 0} if last else {},
        scratch_shapes=scratch,
        compiler_params=pltpu.CompilerParams(vmem_limit_bytes=VMEM_LIMIT),
        cost_estimate=pl.CostEstimate(
            flops=24 * unit,
            bytes_accessed=8 * rows * GROUP * HD * count,
            transcendentals=count * n_keys * GROUP * rows,
        ),
        name=f"attend_{chunk}",
    )(length, q, do, k, v, *slots, *operands)


def total_rows(total, cols):
    high = jnp.floor(total / 256)
    rows = jnp.repeat(jnp.stack([high, total - 256 * high]), EXTRA // 2, axis=0)
    return jnp.broadcast_to(rows, (EXTRA, cols)).astype(jnp.bfloat16)


def body(queries, keys, values, prefix_keys, prefix_values, lengths, out_grad):
    q, k, v, do = queries[0], keys[0], values[0], out_grad[0]
    length = lengths[0]
    prefix = (prefix_keys[0], prefix_values[0])
    slots_all = q.shape[0] * lax.axis_size("prompt") * lax.axis_size("response")
    slots_all = jnp.full((1,), slots_all, jnp.float32)
    first, second = [tensor_gather(prefix, chunk) for chunk in range(CHUNKS)]
    behind = 0 * second[-1, :1].astype(jnp.float32)
    prompt_total = sum_over(length.astype(jnp.float32) + behind, "prompt")
    second = jnp.concatenate([second, total_rows(prompt_total, second.shape[1])], axis=0)
    slots = line_gather(first)
    next_slots = line_gather(second)
    results = attend(0, slots, length, q, do, k, v, slots_all, [])
    carried, terms = results[:4], results[4:]
    results = attend(1, next_slots, length, q, do, k, v, slots_all, carried)
    outs, weight, next_terms = results[:4], results[4][0, 0], results[5:]
    first_sum = line_reduce(terms, weight)
    second_sum = line_reduce(next_terms, 1.0)
    pieces = [tensor_spread(total, len(prefix)) for total in (first_sum, second_sum)]
    grads = [whole_columns(pieces, array) for array in range(len(prefix))]
    return tuple(x[None] for x in (*outs, *grads))


def solution(mesh):
    in_specs = (
        P("prompt", "response", "tensor"),
        P("prompt", "response", "tensor"),
        P("prompt", "response", "tensor"),
        P("prompt", ("response", "tensor"), None),
        P("prompt", ("response", "tensor"), None),
        P("prompt", "response"),
        P("prompt", "response", "tensor"),
    )
    out_specs = (
        P("prompt", "response", "tensor"),
        P("prompt", "response", "tensor"),
        P("prompt", "response", "tensor"),
        P("prompt", "response", "tensor"),
        P("prompt", ("response", "tensor"), None),
        P("prompt", ("response", "tensor"), None),
    )
    return jax.shard_map(body, mesh=mesh, in_specs=in_specs, out_specs=out_specs, check_vma=False)
```

```python
import functools
import math

import jax
import jax.numpy as jnp
from jax import lax
from jax.experimental import pallas as pl
from jax.experimental.pallas import tpu as pltpu
from jax.sharding import PartitionSpec as P

HD = 128
GROUP = 8
PAIR = 2
CHUNKS = 2
EXTRA = 16
STEP = 64
VMEM_LIMIT = 52 * 1024 * 1024
NT = (((1,), (1,)), ((), ()))


def heads_down(ref, first, count):
    return jnp.concatenate(
        [ref[:, (first + i) * HD : (first + i + 1) * HD] for i in range(count)], axis=0
    )


def attend_kernel(n_slots, count, chunk, held, factor, *refs):
    last = chunk + 1 == CHUNKS
    length_ref, q_hbm, do_hbm, kown_hbm, vown_hbm = refs[:5]
    slot_refs, refs = refs[5 : 5 + n_slots], refs[5 + n_slots + last :]
    out_hbm, dq_ref, dkown_ref, dvown_ref = refs[:4]
    term_refs, refs = refs[4 : 4 + n_slots], refs[4 + n_slots :]
    if last:
        total_ref, refs = refs[0], refs[1:]
        totals = [ref[2 * held : 2 * held + 8, :HD].astype(jnp.float32) for ref in slot_refs]
        total_ref[...] = functools.reduce(jnp.add, totals)
    q_ref, do_ref, kown_ref, vown_ref, out_ref = refs[:5]
    s_ref, dp_ref, e_ref, ds_ref, dot_ref = refs[5:10]
    keys_ref, keys_t_ref, values_ref, values_t_ref, in_sem, out_sem = refs[10:]
    first = chunk * count
    rows = q_ref.shape[0]
    own = kown_ref.shape[0]
    n_keys = s_ref.shape[1]
    width = PAIR * rows
    pairs = GROUP // PAIR
    scale = factor * math.log2(math.e)

    def columns(head, size):
        return pl.ds(head * size, size)

    loads = []
    for head in range(count):
        loads.append(
            [
                pltpu.make_async_copy(
                    hbm.at[:, columns(first + head, size)],
                    ref.at[:, columns(head, size)],
                    in_sem.at[head, i],
                )
                for i, (hbm, ref, size) in enumerate(
                    [
                        (kown_hbm, kown_ref, HD),
                        (q_hbm, q_ref, GROUP * HD),
                        (do_hbm, do_ref, GROUP * HD),
                        (vown_hbm, vown_ref, HD),
                    ]
                )
            ]
        )
        for copy in loads[-1]:
            copy.start()
    stores = []

    live = (lax.broadcasted_iota(jnp.int32, (1, width), 1) % rows) < length_ref[0]

    def assemble(head, own_ref, slot_start, wide_ref, tall_ref):
        here = slice(head * HD, (head + 1) * HD)
        wide_ref[head, :own] = own_ref[:, here]
        for i, ref in enumerate(slot_refs):
            part = slice(own + i * held, own + (i + 1) * held)
            wide_ref[head, part] = ref[slot_start : slot_start + held, here]
        tall_ref[head] = wide_ref[head].T

    def place(head, pair):
        return slice(pair * width, (pair + 1) * width)

    def scores(head, pair):
        if pair == 0:
            loads[head][0].wait()
            loads[head][1].wait()
            assemble(head, kown_ref, 0, keys_ref, keys_t_ref)
        s_ref[pair % 2] = lax.dot_general(
            keys_ref[head],
            heads_down(q_ref, head * GROUP + pair * PAIR, PAIR),
            NT,
            preferred_element_type=jnp.float32,
        )

    def softmax(head, pair):
        here = s_ref.at[pair % 2]
        cols = place(head, pair)
        fold = lambda x: x.reshape(x.shape[0] // 8, 8, width)
        top = jnp.full((8, width), -1e30, jnp.float32)
        for at in range(0, n_keys, STEP):
            x = here[at : at + STEP]
            if at < own:
                key_pos = lax.broadcasted_iota(jnp.int32, x.shape, 0) + at
                row_pos = lax.broadcasted_iota(jnp.int32, x.shape, 1) % rows
                x = jnp.where(key_pos <= row_pos, x, -1e30)
                here[at : at + STEP] = x
            top = jnp.maximum(top, jnp.max(fold(x), axis=0))
        top = jnp.max(top, axis=0, keepdims=True) * scale
        top = jnp.broadcast_to(top, (8, width))
        total = jnp.zeros((8, width), jnp.float32)
        for at in range(0, n_keys, STEP):
            e = jnp.exp2(fold(here[at : at + STEP]) * scale - top)
            total = total + jnp.sum(e, axis=0)
            e_ref[head % 2, at : at + STEP, cols] = e.reshape(-1, width).astype(jnp.bfloat16)
        total = jnp.sum(total, axis=0, keepdims=True)
        inverse = jnp.where(live, 1.0 / total, 0.0)
        if pair == 0:
            loads[head][2].wait()
        do = heads_down(do_ref, head * GROUP + pair * PAIR, PAIR)
        dot_ref[head % 2, :, cols] = (do.T.astype(jnp.float32) * inverse).astype(jnp.bfloat16)
        return inverse

    def attended(head, pair, inverse):
        cols = place(head, pair)
        if pair == 0:
            loads[head][3].wait()
            assemble(head, vown_ref, held, values_ref, values_t_ref)
        grad = dot_ref[head % 2, :, cols]
        dp_ref[pair % 2] = jnp.dot(values_ref[head], grad, preferred_element_type=jnp.float32)
        out = jnp.dot(
            values_t_ref[head], e_ref[head % 2, :, cols], preferred_element_type=jnp.float32
        )
        out = out * inverse
        turned = out.astype(jnp.bfloat16).T
        for i in range(PAIR):
            at = head * GROUP + pair * PAIR + i
            out_ref[:, at * HD : (at + 1) * HD] = turned[i * rows : (i + 1) * rows]
        return jnp.sum(out * grad.astype(jnp.float32), axis=0, keepdims=True)

    def score_grads(head, pair, centre):
        cols = place(head, pair)
        here = dp_ref.at[pair % 2]
        centre = jnp.broadcast_to(centre, (STEP, width))
        for at in range(0, n_keys, STEP):
            e = e_ref[head % 2, at : at + STEP, cols].astype(jnp.float32)
            grad = e * (here[at : at + STEP] - centre)
            ds_ref[head % 2, at : at + STEP, cols] = grad.astype(jnp.bfloat16)

    def query_grads(head, pair):
        cols = place(head, pair)
        dq = jnp.dot(
            keys_t_ref[head], ds_ref[head % 2, :, cols], preferred_element_type=jnp.float32
        )
        turned = (dq * factor).astype(jnp.bfloat16).T
        for i in range(PAIR):
            at = head * GROUP + pair * PAIR + i
            dq_ref[:, at * HD : (at + 1) * HD] = turned[i * rows : (i + 1) * rows]

    def key_grads(head):
        copy = pltpu.make_async_copy(
            out_ref.at[:, columns(head, GROUP * HD)],
            out_hbm.at[:, columns(first + head, GROUP * HD)],
            out_sem.at[head],
        )
        copy.start()
        stores.append(copy)
        here = slice(head * HD, (head + 1) * HD)
        dv = lax.dot_general(
            e_ref[head % 2], dot_ref[head % 2], NT, preferred_element_type=jnp.float32
        ).astype(jnp.bfloat16)
        dvown_ref[:, here] = dv[:own]
        for i, ref in enumerate(term_refs):
            ref[held:, here] = dv[own + i * held : own + (i + 1) * held]
        dk = jnp.dot(
            ds_ref[head % 2],
            heads_down(q_ref, head * GROUP, GROUP),
            preferred_element_type=jnp.float32,
        )
        dk = (dk * factor).astype(jnp.bfloat16)
        dkown_ref[:, here] = dk[:own]
        for i, ref in enumerate(term_refs):
            ref[:held, here] = dk[own + i * held : own + (i + 1) * held]

    steps = [(head, pair) for head in range(count) for pair in range(pairs)]
    scores(*steps[0])
    inverse = softmax(*steps[0])
    for now, then in zip(steps, steps[1:] + [None]):
        if then:
            scores(*then)
        centre = attended(*now, inverse)
        if then:
            inverse = softmax(*then)
        score_grads(*now, centre)
        query_grads(*now)
        if now[1] + 1 == pairs:
            key_grads(now[0])
    for copy in stores:
        copy.wait()


def scale_kernel(slots_all, total_ref, *refs):
    sources, refs = refs[: 3 * CHUNKS], refs[3 * CHUNKS :]
    outs, held, sem = refs[:3], refs[3:6], refs[6]
    weight = slots_all / total_ref[:1, :1]
    copies = []
    for chunk in range(CHUNKS):
        for i in range(3):
            source = sources[chunk * 3 + i]
            cols = pl.ds(chunk * source.shape[1], source.shape[1])
            scaled = source[...].astype(jnp.float32) * weight
            held[i][:, cols] = scaled.astype(jnp.bfloat16)
            copy = pltpu.make_async_copy(held[i].at[:, cols], outs[i].at[:, cols], sem.at[chunk, i])
            copy.start()
            copies.append(copy)
    for copy in copies:
        copy.wait()


def swap(x, axis, by):
    return lax.ppermute(x, axis, [(i, i ^ by) for i in range(lax.axis_size(axis))])


def sum_over(x, axis):
    by = 1
    while by < lax.axis_size(axis):
        x = x + swap(x, axis, by)
        by *= 2
    return x


def line_gather(block):
    return [block] + [swap(block, "response", m) for m in range(1, lax.axis_size("response"))]


def line_reduce(slots):
    terms = [slots[0]] + [swap(slots[m], "response", m) for m in range(1, len(slots))]
    total = functools.reduce(jnp.add, [term.astype(jnp.float32) for term in terms])
    return total


def own_columns(block, chunk, by):
    cols = block.shape[1] // (lax.axis_size("tensor") * CHUNKS)
    rank = lax.axis_index("tensor") ^ by
    return lax.dynamic_slice_in_dim(block, (rank * CHUNKS + chunk) * cols, cols, 1)


def tensor_gather(blocks, chunk):
    parts = lax.axis_size("tensor")
    pieces = []
    for m in range(parts):
        piece = jnp.concatenate([own_columns(block, chunk, m) for block in blocks], axis=0)
        pieces.append(piece if m == 0 else swap(piece, "tensor", m))
    rows = blocks[0].shape[0]
    return jnp.concatenate(
        [piece[i * rows : (i + 1) * rows] for i in range(len(blocks)) for piece in pieces], axis=0
    )


def tensor_spread(total, n_arrays):
    parts = lax.axis_size("tensor")
    rows = total.shape[0] // (n_arrays * parts)
    pieces = []
    for m in range(parts):
        piece = jnp.concatenate(
            [total[(i * parts + m) * rows : (i * parts + m + 1) * rows] for i in range(n_arrays)],
            axis=0,
        )
        pieces.append(piece if m == 0 else swap(piece, "tensor", m))
    return pieces


def whole_columns(chunk_pieces, array):
    parts = lax.axis_size("tensor")
    rank = lax.axis_index("tensor")
    rows = chunk_pieces[0][0].shape[0] // 2
    by_rank = [
        jnp.concatenate([pieces[m][array * rows : (array + 1) * rows] for pieces in chunk_pieces], axis=1)
        for m in range(parts)
    ]
    ordered = []
    for t in range(parts):
        column = by_rank[0]
        for m in range(1, parts):
            column = jnp.where(rank ^ m == t, by_rank[m], column)
        ordered.append(column)
    return jnp.concatenate(ordered, axis=1)


SMEM = pl.BlockSpec(memory_space=pltpu.SMEM)
HBM = pl.BlockSpec(memory_space=pltpu.HBM)
VMEM = pl.BlockSpec(memory_space=pltpu.VMEM)


def like(x):
    return jax.ShapeDtypeStruct(x.shape, x.dtype)


def attend(chunk, held, slots, length, q, do, k, v, carried):
    rows = q.shape[0]
    count = k.shape[1] // (HD * CHUNKS)
    n_slots = len(slots)
    last = chunk + 1 == CHUNKS
    n_keys = rows + n_slots * held
    bf16 = jnp.bfloat16
    unit = 2 * n_keys * GROUP * rows * HD * count
    step_buffer = pltpu.VMEM((2, n_keys, PAIR * rows), jnp.float32)
    head_buffer = pltpu.VMEM((2, n_keys, GROUP * rows), bf16)
    wide = pltpu.VMEM((rows, count * GROUP * HD), bf16)
    own = pltpu.VMEM((rows, count * HD), bf16)
    down = pltpu.VMEM((count, n_keys, HD), bf16)
    across = pltpu.VMEM((count, HD, n_keys), bf16)
    scratch = [wide, wide, own, own, wide, step_buffer, step_buffer, head_buffer, head_buffer]
    scratch += [pltpu.VMEM((2, HD, GROUP * rows), bf16), down, across, down, across]
    scratch += [pltpu.SemaphoreType.DMA((count, 4)), pltpu.SemaphoreType.DMA((count,))]
    part = lambda x: jax.ShapeDtypeStruct((x.shape[0], x.shape[1] // CHUNKS), bf16)
    terms = [jax.ShapeDtypeStruct((2 * held, count * HD), bf16)] * n_slots
    total = [jax.ShapeDtypeStruct((8, HD), jnp.float32)] * last
    return pl.pallas_call(
        functools.partial(attend_kernel, n_slots, count, chunk, held, 1.0 / math.sqrt(HD)),
        in_specs=[SMEM] + [HBM] * 4 + [VMEM] * n_slots + [HBM] * last,
        out_specs=[HBM] + [VMEM] * (3 + n_slots + last),
        out_shape=[like(q), part(q), part(k), part(v)] + terms + total,
        input_output_aliases={5 + n_slots: 0} if last else {},
        scratch_shapes=scratch,
        compiler_params=pltpu.CompilerParams(vmem_limit_bytes=VMEM_LIMIT),
        cost_estimate=pl.CostEstimate(
            flops=24 * unit,
            bytes_accessed=8 * rows * GROUP * HD * count,
            transcendentals=count * n_keys * GROUP * rows,
        ),
        name=f"attend_{chunk}",
    )(length, q, do, k, v, *slots, *carried)


def scale_all(slots_all, total, chunk_grads, shapes):
    flat = [grad for grads in chunk_grads for grad in grads]
    return pl.pallas_call(
        functools.partial(scale_kernel, slots_all),
        in_specs=[VMEM] * (1 + len(flat)),
        out_specs=[HBM] * len(shapes),
        out_shape=shapes,
        scratch_shapes=[pltpu.VMEM(x.shape, x.dtype) for x in shapes]
        + [pltpu.SemaphoreType.DMA((CHUNKS, len(shapes)))],
        cost_estimate=pl.CostEstimate(
            flops=sum(x.size for x in shapes),
            bytes_accessed=sum(4 * x.size for x in shapes),
            transcendentals=0,
        ),
        name="scale",
    )(total, *flat)


def body(queries, keys, values, prefix_keys, prefix_values, lengths, out_grad):
    q, k, v, do = queries[0], keys[0], values[0], out_grad[0]
    length = lengths[0]
    prefix = (prefix_keys[0], prefix_values[0])
    slots_all = q.shape[0] * lax.axis_size("prompt") * lax.axis_size("response")
    first, second = [tensor_gather(prefix, chunk) for chunk in range(CHUNKS)]
    held = first.shape[0] // 2
    length_rows = jnp.full((EXTRA, second.shape[1]), length[0].astype(second.dtype))
    slots = line_gather(first)
    next_slots = line_gather(jnp.concatenate([second, length_rows], axis=0))
    results = attend(0, held, slots, length, q, do, k, v, [])
    next_results = attend(1, held, next_slots, length, q, do, k, v, results[:1])
    sums = [line_reduce(results[4:]), line_reduce(next_results[4:-1])]
    total = sum_over(next_results[-1] + 0 * sums[0][:8, :HD], "prompt")
    weight = slots_all / total[0, 0]
    scaled = scale_all(
        slots_all, total, [results[1:4], next_results[1:4]], [like(q), like(k), like(v)]
    )
    pieces = [tensor_spread(terms.astype(jnp.bfloat16), len(prefix)) for terms in sums]
    grads = [whole_columns(pieces, array) for array in range(len(prefix))]
    grads = [(grad.astype(jnp.float32) * weight).astype(jnp.bfloat16) for grad in grads]
    return tuple(x[None] for x in (next_results[0], *scaled, *grads))


def solution(mesh):
    in_specs = (
        P("prompt", "response", "tensor"),
        P("prompt", "response", "tensor"),
        P("prompt", "response", "tensor"),
        P("prompt", ("response", "tensor"), None),
        P("prompt", ("response", "tensor"), None),
        P("prompt", "response"),
        P("prompt", "response", "tensor"),
    )
    out_specs = (
        P("prompt", "response", "tensor"),
        P("prompt", "response", "tensor"),
        P("prompt", "response", "tensor"),
        P("prompt", "response", "tensor"),
        P("prompt", ("response", "tensor"), None),
        P("prompt", ("response", "tensor"), None),
    )
    return jax.shard_map(body, mesh=mesh, in_specs=in_specs, out_specs=out_specs, check_vma=False)
```

```python
import functools
import math

import jax
import jax.numpy as jnp
from jax import lax
from jax.experimental import pallas as pl
from jax.experimental.pallas import tpu as pltpu
from jax.sharding import PartitionSpec as P

HD = 128
GROUP = 8
PAIR = 2
CHUNKS = 2
EXTRA = 16
STEP = 64
VMEM_LIMIT = 52 * 1024 * 1024
NT = (((1,), (1,)), ((), ()))


def heads_down(ref, first, count):
    return jnp.concatenate(
        [ref[:, (first + i) * HD : (first + i + 1) * HD] for i in range(count)], axis=0
    )


def attend_kernel(n_slots, count, chunk, held, factor, *refs):
    last = chunk + 1 == CHUNKS
    length_ref, q_hbm, do_hbm, kown_hbm, vown_hbm = refs[:5]
    slot_refs, refs = refs[5 : 5 + n_slots], refs[5 + n_slots + last :]
    out_hbm, dq_ref, dkown_ref, dvown_ref = refs[:4]
    term_refs, refs = refs[4 : 4 + n_slots], refs[4 + n_slots :]
    if last:
        total_ref, refs = refs[0], refs[1:]
        totals = [ref[2 * held : 2 * held + 8, :HD].astype(jnp.float32) for ref in slot_refs]
        total_ref[...] = functools.reduce(jnp.add, totals)
    q_ref, do_ref, kown_ref, vown_ref, out_ref = refs[:5]
    s_ref, dp_ref, e_ref, ds_ref, dot_ref = refs[5:10]
    keys_ref, keys_t_ref, values_ref, values_t_ref, in_sem, out_sem = refs[10:]
    first = chunk * count
    rows = q_ref.shape[0]
    own = kown_ref.shape[0]
    n_keys = s_ref.shape[1]
    width = PAIR * rows
    pairs = GROUP // PAIR
    scale = factor * math.log2(math.e)

    def columns(head, size):
        return pl.ds(head * size, size)

    loads = []
    for head in range(count):
        loads.append(
            [
                pltpu.make_async_copy(
                    hbm.at[:, columns(first + head, size)],
                    ref.at[:, columns(head, size)],
                    in_sem.at[head, i],
                )
                for i, (hbm, ref, size) in enumerate(
                    [
                        (kown_hbm, kown_ref, HD),
                        (q_hbm, q_ref, GROUP * HD),
                        (do_hbm, do_ref, GROUP * HD),
                        (vown_hbm, vown_ref, HD),
                    ]
                )
            ]
        )
        for copy in loads[-1]:
            copy.start()
    stores = []

    live = (lax.broadcasted_iota(jnp.int32, (1, width), 1) % rows) < length_ref[0]

    def assemble(head, own_ref, slot_start, wide_ref, tall_ref):
        here = slice(head * HD, (head + 1) * HD)
        wide_ref[head, :own] = own_ref[:, here]
        for i, ref in enumerate(slot_refs):
            part = slice(own + i * held, own + (i + 1) * held)
            wide_ref[head, part] = ref[slot_start : slot_start + held, here]
        tall_ref[head] = wide_ref[head].T

    def place(head, pair):
        return slice(pair * width, (pair + 1) * width)

    def scores(head, pair):
        if pair == 0:
            loads[head][0].wait()
            loads[head][1].wait()
            assemble(head, kown_ref, 0, keys_ref, keys_t_ref)
        s_ref[pair % 2] = lax.dot_general(
            keys_ref[head],
            heads_down(q_ref, head * GROUP + pair * PAIR, PAIR),
            NT,
            preferred_element_type=jnp.float32,
        )

    def softmax(head, pair):
        here = s_ref.at[pair % 2]
        cols = place(head, pair)
        fold = lambda x: x.reshape(x.shape[0] // 8, 8, width)
        top = jnp.full((8, width), -1e30, jnp.float32)
        for at in range(0, n_keys, STEP):
            x = here[at : at + STEP]
            if at < own:
                key_pos = lax.broadcasted_iota(jnp.int32, x.shape, 0) + at
                row_pos = lax.broadcasted_iota(jnp.int32, x.shape, 1) % rows
                x = jnp.where(key_pos <= row_pos, x, -1e30)
                here[at : at + STEP] = x
            top = jnp.maximum(top, jnp.max(fold(x), axis=0))
        top = jnp.max(top, axis=0, keepdims=True) * scale
        top = jnp.broadcast_to(top, (8, width))
        total = jnp.zeros((8, width), jnp.float32)
        for at in range(0, n_keys, STEP):
            e = jnp.exp2(fold(here[at : at + STEP]) * scale - top)
            total = total + jnp.sum(e, axis=0)
            e_ref[head % 2, at : at + STEP, cols] = e.reshape(-1, width).astype(jnp.bfloat16)
        total = jnp.sum(total, axis=0, keepdims=True)
        inverse = jnp.where(live, 1.0 / total, 0.0)
        if pair == 0:
            loads[head][2].wait()
        do = heads_down(do_ref, head * GROUP + pair * PAIR, PAIR)
        dot_ref[head % 2, :, cols] = (do.T.astype(jnp.float32) * inverse).astype(jnp.bfloat16)
        return inverse

    def attended(head, pair, inverse):
        cols = place(head, pair)
        if pair == 0:
            loads[head][3].wait()
            assemble(head, vown_ref, held, values_ref, values_t_ref)
        grad = dot_ref[head % 2, :, cols]
        dp_ref[pair % 2] = jnp.dot(values_ref[head], grad, preferred_element_type=jnp.float32)
        out = jnp.dot(
            values_t_ref[head], e_ref[head % 2, :, cols], preferred_element_type=jnp.float32
        )
        out = out * inverse
        turned = out.astype(jnp.bfloat16).T
        for i in range(PAIR):
            at = head * GROUP + pair * PAIR + i
            out_ref[:, at * HD : (at + 1) * HD] = turned[i * rows : (i + 1) * rows]
        return jnp.sum(out * grad.astype(jnp.float32), axis=0, keepdims=True)

    def score_grads(head, pair, centre):
        cols = place(head, pair)
        here = dp_ref.at[pair % 2]
        centre = jnp.broadcast_to(centre, (STEP, width))
        for at in range(0, n_keys, STEP):
            e = e_ref[head % 2, at : at + STEP, cols].astype(jnp.float32)
            grad = e * (here[at : at + STEP] - centre)
            ds_ref[head % 2, at : at + STEP, cols] = grad.astype(jnp.bfloat16)

    def query_grads(head, pair):
        cols = place(head, pair)
        dq = jnp.dot(
            keys_t_ref[head], ds_ref[head % 2, :, cols], preferred_element_type=jnp.float32
        )
        turned = (dq * factor).astype(jnp.bfloat16).T
        for i in range(PAIR):
            at = head * GROUP + pair * PAIR + i
            dq_ref[:, at * HD : (at + 1) * HD] = turned[i * rows : (i + 1) * rows]

    def key_grads(head):
        copy = pltpu.make_async_copy(
            out_ref.at[:, columns(head, GROUP * HD)],
            out_hbm.at[:, columns(first + head, GROUP * HD)],
            out_sem.at[head],
        )
        copy.start()
        stores.append(copy)
        here = slice(head * HD, (head + 1) * HD)
        dv = lax.dot_general(
            e_ref[head % 2], dot_ref[head % 2], NT, preferred_element_type=jnp.float32
        ).astype(jnp.bfloat16)
        dvown_ref[:, here] = dv[:own]
        for i, ref in enumerate(term_refs):
            ref[held:, here] = dv[own + i * held : own + (i + 1) * held]
        dk = jnp.dot(
            ds_ref[head % 2],
            heads_down(q_ref, head * GROUP, GROUP),
            preferred_element_type=jnp.float32,
        )
        dk = (dk * factor).astype(jnp.bfloat16)
        dkown_ref[:, here] = dk[:own]
        for i, ref in enumerate(term_refs):
            ref[:held, here] = dk[own + i * held : own + (i + 1) * held]

    steps = [(head, pair) for head in range(count) for pair in range(pairs)]
    scores(*steps[0])
    inverse = softmax(*steps[0])
    for now, then in zip(steps, steps[1:] + [None]):
        if then:
            scores(*then)
        centre = attended(*now, inverse)
        if then:
            inverse = softmax(*then)
        score_grads(*now, centre)
        query_grads(*now)
        if now[1] + 1 == pairs:
            key_grads(now[0])
    for copy in stores:
        copy.wait()


def scale_kernel(slots_all, total_ref, *refs):
    sources, refs = refs[: 3 * CHUNKS], refs[3 * CHUNKS :]
    outs, held, sem = refs[:3], refs[3:6], refs[6]
    weight = slots_all / total_ref[:1, :1]
    copies = []
    for chunk in range(CHUNKS):
        for i in range(3):
            source = sources[chunk * 3 + i]
            cols = pl.ds(chunk * source.shape[1], source.shape[1])
            scaled = source[...].astype(jnp.float32) * weight
            held[i][:, cols] = scaled.astype(jnp.bfloat16)
            copy = pltpu.make_async_copy(held[i].at[:, cols], outs[i].at[:, cols], sem.at[chunk, i])
            copy.start()
            copies.append(copy)
    for copy in copies:
        copy.wait()


def swap(x, axis, by):
    return lax.ppermute(x, axis, [(i, i ^ by) for i in range(lax.axis_size(axis))])


def sum_over(x, axis):
    by = 1
    while by < lax.axis_size(axis):
        x = x + swap(x, axis, by)
        by *= 2
    return x


def line_gather(block, butterfly):
    size = lax.axis_size("response")
    if size != 4 or not butterfly:
        return [block] + [swap(block, "response", m) for m in range(1, size)]
    far = swap(block, "response", 3)
    near = swap(block, "response", 1)
    return [block, near, swap(far, "response", 1), far]


def line_reduce(slots):
    terms = [slots[0]] + [swap(slots[m], "response", m) for m in range(1, len(slots))]
    total = functools.reduce(jnp.add, [term.astype(jnp.float32) for term in terms])
    return total


def own_columns(block, chunk, by):
    cols = block.shape[1] // (lax.axis_size("tensor") * CHUNKS)
    rank = lax.axis_index("tensor") ^ by
    return lax.dynamic_slice_in_dim(block, (rank * CHUNKS + chunk) * cols, cols, 1)


def tensor_gather(blocks, chunk):
    parts = lax.axis_size("tensor")
    pieces = []
    for m in range(parts):
        piece = jnp.concatenate([own_columns(block, chunk, m) for block in blocks], axis=0)
        pieces.append(piece if m == 0 else swap(piece, "tensor", m))
    rows = blocks[0].shape[0]
    return jnp.concatenate(
        [piece[i * rows : (i + 1) * rows] for i in range(len(blocks)) for piece in pieces], axis=0
    )


def tensor_spread(total, n_arrays):
    parts = lax.axis_size("tensor")
    rows = total.shape[0] // (n_arrays * parts)
    pieces = []
    for m in range(parts):
        piece = jnp.concatenate(
            [total[(i * parts + m) * rows : (i * parts + m + 1) * rows] for i in range(n_arrays)],
            axis=0,
        )
        pieces.append(piece if m == 0 else swap(piece, "tensor", m))
    return pieces


def whole_columns(chunk_pieces, array):
    parts = lax.axis_size("tensor")
    rank = lax.axis_index("tensor")
    rows = chunk_pieces[0][0].shape[0] // 2
    by_rank = [
        jnp.concatenate([pieces[m][array * rows : (array + 1) * rows] for pieces in chunk_pieces], axis=1)
        for m in range(parts)
    ]
    ordered = []
    for t in range(parts):
        column = by_rank[0]
        for m in range(1, parts):
            column = jnp.where(rank ^ m == t, by_rank[m], column)
        ordered.append(column)
    return jnp.concatenate(ordered, axis=1)


SMEM = pl.BlockSpec(memory_space=pltpu.SMEM)
HBM = pl.BlockSpec(memory_space=pltpu.HBM)
VMEM = pl.BlockSpec(memory_space=pltpu.VMEM)


def like(x):
    return jax.ShapeDtypeStruct(x.shape, x.dtype)


def attend(chunk, held, slots, length, q, do, k, v, carried):
    rows = q.shape[0]
    count = k.shape[1] // (HD * CHUNKS)
    n_slots = len(slots)
    last = chunk + 1 == CHUNKS
    n_keys = rows + n_slots * held
    bf16 = jnp.bfloat16
    unit = 2 * n_keys * GROUP * rows * HD * count
    step_buffer = pltpu.VMEM((2, n_keys, PAIR * rows), jnp.float32)
    head_buffer = pltpu.VMEM((2, n_keys, GROUP * rows), bf16)
    wide = pltpu.VMEM((rows, count * GROUP * HD), bf16)
    own = pltpu.VMEM((rows, count * HD), bf16)
    down = pltpu.VMEM((count, n_keys, HD), bf16)
    across = pltpu.VMEM((count, HD, n_keys), bf16)
    scratch = [wide, wide, own, own, wide, step_buffer, step_buffer, head_buffer, head_buffer]
    scratch += [pltpu.VMEM((2, HD, GROUP * rows), bf16), down, across, down, across]
    scratch += [pltpu.SemaphoreType.DMA((count, 4)), pltpu.SemaphoreType.DMA((count,))]
    part = lambda x: jax.ShapeDtypeStruct((x.shape[0], x.shape[1] // CHUNKS), bf16)
    terms = [jax.ShapeDtypeStruct((2 * held, count * HD), bf16)] * n_slots
    total = [jax.ShapeDtypeStruct((8, HD), jnp.float32)] * last
    return pl.pallas_call(
        functools.partial(attend_kernel, n_slots, count, chunk, held, 1.0 / math.sqrt(HD)),
        in_specs=[SMEM] + [HBM] * 4 + [VMEM] * n_slots + [HBM] * last,
        out_specs=[HBM] + [VMEM] * (3 + n_slots + last),
        out_shape=[like(q), part(q), part(k), part(v)] + terms + total,
        input_output_aliases={5 + n_slots: 0} if last else {},
        scratch_shapes=scratch,
        compiler_params=pltpu.CompilerParams(vmem_limit_bytes=VMEM_LIMIT),
        cost_estimate=pl.CostEstimate(
            flops=24 * unit,
            bytes_accessed=8 * rows * GROUP * HD * count,
            transcendentals=count * n_keys * GROUP * rows,
        ),
        name=f"attend_{chunk}",
    )(length, q, do, k, v, *slots, *carried)


def scale_all(slots_all, total, chunk_grads, shapes):
    flat = [grad for grads in chunk_grads for grad in grads]
    return pl.pallas_call(
        functools.partial(scale_kernel, slots_all),
        in_specs=[VMEM] * (1 + len(flat)),
        out_specs=[HBM] * len(shapes),
        out_shape=shapes,
        scratch_shapes=[pltpu.VMEM(x.shape, x.dtype) for x in shapes]
        + [pltpu.SemaphoreType.DMA((CHUNKS, len(shapes)))],
        cost_estimate=pl.CostEstimate(
            flops=sum(x.size for x in shapes),
            bytes_accessed=sum(4 * x.size for x in shapes),
            transcendentals=0,
        ),
        name="scale",
    )(total, *flat)


def body(queries, keys, values, prefix_keys, prefix_values, lengths, out_grad):
    q, k, v, do = queries[0], keys[0], values[0], out_grad[0]
    length = lengths[0]
    prefix = (prefix_keys[0], prefix_values[0])
    slots_all = q.shape[0] * lax.axis_size("prompt") * lax.axis_size("response")
    first, second = [tensor_gather(prefix, chunk) for chunk in range(CHUNKS)]
    held = first.shape[0] // 2
    slots = line_gather(first, True)
    length_rows = length[0].astype(second.dtype) + 0 * slots[-1][-EXTRA:]
    next_slots = line_gather(jnp.concatenate([second, length_rows], axis=0), False)
    results = attend(0, held, slots, length, q, do, k, v, [])
    next_results = attend(1, held, next_slots, length, q, do, k, v, results[:1])
    sums = [line_reduce(results[4:]), line_reduce(next_results[4:-1])]
    total = sum_over(next_results[-1] + 0 * sums[0][:8, :HD], "prompt")
    weight = slots_all / total[0, 0]
    scaled = scale_all(
        slots_all, total, [results[1:4], next_results[1:4]], [like(q), like(k), like(v)]
    )
    pieces = [tensor_spread(terms.astype(jnp.bfloat16), len(prefix)) for terms in sums]
    grads = [whole_columns(pieces, array) for array in range(len(prefix))]
    grads = [(grad.astype(jnp.float32) * weight).astype(jnp.bfloat16) for grad in grads]
    return tuple(x[None] for x in (next_results[0], *scaled, *grads))


def solution(mesh):
    in_specs = (
        P("prompt", "response", "tensor"),
        P("prompt", "response", "tensor"),
        P("prompt", "response", "tensor"),
        P("prompt", ("response", "tensor"), None),
        P("prompt", ("response", "tensor"), None),
        P("prompt", "response"),
        P("prompt", "response", "tensor"),
    )
    out_specs = (
        P("prompt", "response", "tensor"),
        P("prompt", "response", "tensor"),
        P("prompt", "response", "tensor"),
        P("prompt", "response", "tensor"),
        P("prompt", ("response", "tensor"), None),
        P("prompt", ("response", "tensor"), None),
    )
    return jax.shard_map(body, mesh=mesh, in_specs=in_specs, out_specs=out_specs, check_vma=False)
```

```python
import functools
import math

import jax
import jax.numpy as jnp
from jax import lax
from jax.experimental import pallas as pl
from jax.experimental.pallas import tpu as pltpu
from jax.sharding import PartitionSpec as P

HD = 128
GROUP = 8
PAIR = 2
CHUNKS = 2
EXTRA = 16
STEP = 64
VMEM_LIMIT = 40 * 1024 * 1024
NT = (((1,), (1,)), ((), ()))


def heads_down(ref, first, count):
    return jnp.concatenate(
        [ref[:, (first + i) * HD : (first + i + 1) * HD] for i in range(count)], axis=0
    )


def attend_kernel(n_slots, count, chunk, held, factor, *refs):
    last = chunk + 1 == CHUNKS
    length_ref, q_ref, turned_ref, kown_ref, vown_ref = refs[:5]
    slot_refs, refs = refs[5 : 5 + n_slots], refs[5 + n_slots + last :]
    out_hbm, dq_ref, dkown_ref, dvown_ref = refs[:4]
    term_refs, refs = refs[4 : 4 + n_slots], refs[4 + n_slots :]
    if last:
        total_ref, refs = refs[0], refs[1:]
        totals = [ref[2 * held : 2 * held + 8, :HD].astype(jnp.float32) for ref in slot_refs]
        total_ref[...] = functools.reduce(jnp.add, totals)
    out_ref, s_ref, dp_ref, e_ref, ds_ref, dot_ref = refs[:6]
    keys_ref, keys_t_ref, values_ref, values_t_ref, out_sem = refs[6:]
    first = chunk * count
    rows = q_ref.shape[0]
    own = kown_ref.shape[0]
    n_keys = s_ref.shape[1]
    width = PAIR * rows
    pairs = GROUP // PAIR
    scale = factor * math.log2(math.e)

    def columns(head, size):
        return pl.ds(head * size, size)

    stores = []

    live = (lax.broadcasted_iota(jnp.int32, (1, width), 1) % rows) < length_ref[0]

    def assemble(head, own_ref, slot_start, wide_ref, tall_ref):
        here = slice(head * HD, (head + 1) * HD)
        wide_ref[head, :own] = own_ref[:, (first + head) * HD : (first + head + 1) * HD]
        for i, ref in enumerate(slot_refs):
            part = slice(own + i * held, own + (i + 1) * held)
            wide_ref[head, part] = ref[slot_start : slot_start + held, here]
        tall_ref[head] = wide_ref[head].T

    def place(head, pair):
        return slice(pair * width, (pair + 1) * width)

    def scores(head, pair):
        if pair == 0:
            assemble(head, kown_ref, 0, keys_ref, keys_t_ref)
        s_ref[pair % 2] = lax.dot_general(
            keys_ref[head],
            heads_down(q_ref, (first + head) * GROUP + pair * PAIR, PAIR),
            NT,
            preferred_element_type=jnp.float32,
        )

    def softmax(head, pair):
        here = s_ref.at[pair % 2]
        cols = place(head, pair)
        fold = lambda x: x.reshape(x.shape[0] // 8, 8, width)
        top = jnp.full((8, width), -1e30, jnp.float32)
        for at in range(0, n_keys, STEP):
            x = here[at : at + STEP]
            if at < own:
                key_pos = lax.broadcasted_iota(jnp.int32, x.shape, 0) + at
                row_pos = lax.broadcasted_iota(jnp.int32, x.shape, 1) % rows
                x = jnp.where(key_pos <= row_pos, x, -1e30)
                here[at : at + STEP] = x
            top = jnp.maximum(top, jnp.max(fold(x), axis=0))
        top = jnp.max(top, axis=0, keepdims=True) * scale
        top = jnp.broadcast_to(top, (8, width))
        total = jnp.zeros((8, width), jnp.float32)
        for at in range(0, n_keys, STEP):
            e = jnp.exp2(fold(here[at : at + STEP]) * scale - top)
            total = total + jnp.sum(e, axis=0)
            e_ref[head % 2, at : at + STEP, cols] = e.reshape(-1, width).astype(jnp.bfloat16)
        total = jnp.sum(total, axis=0, keepdims=True)
        inverse = jnp.where(live, 1.0 / total, 0.0)
        grad = turned_ref[first + head, :, cols].astype(jnp.float32) * inverse
        dot_ref[head % 2, :, cols] = grad.astype(jnp.bfloat16)
        return inverse

    def attended(head, pair, inverse):
        cols = place(head, pair)
        if pair == 0:
            assemble(head, vown_ref, held, values_ref, values_t_ref)
        grad = dot_ref[head % 2, :, cols]
        dp_ref[pair % 2] = jnp.dot(values_ref[head], grad, preferred_element_type=jnp.float32)
        out = jnp.dot(
            values_t_ref[head], e_ref[head % 2, :, cols], preferred_element_type=jnp.float32
        )
        out = out * inverse
        turned = out.astype(jnp.bfloat16).T
        for i in range(PAIR):
            at = head * GROUP + pair * PAIR + i
            out_ref[:, at * HD : (at + 1) * HD] = turned[i * rows : (i + 1) * rows]
        return jnp.sum(out * grad.astype(jnp.float32), axis=0, keepdims=True)

    def score_grads(head, pair, centre):
        cols = place(head, pair)
        here = dp_ref.at[pair % 2]
        centre = jnp.broadcast_to(centre, (STEP, width))
        for at in range(0, n_keys, STEP):
            e = e_ref[head % 2, at : at + STEP, cols].astype(jnp.float32)
            grad = e * (here[at : at + STEP] - centre)
            ds_ref[head % 2, at : at + STEP, cols] = grad.astype(jnp.bfloat16)

    def query_grads(head, pair):
        cols = place(head, pair)
        dq = jnp.dot(
            keys_t_ref[head], ds_ref[head % 2, :, cols], preferred_element_type=jnp.float32
        )
        turned = (dq * factor).astype(jnp.bfloat16).T
        for i in range(PAIR):
            at = head * GROUP + pair * PAIR + i
            dq_ref[:, at * HD : (at + 1) * HD] = turned[i * rows : (i + 1) * rows]

    def key_grads(head):
        copy = pltpu.make_async_copy(
            out_ref.at[:, columns(head, GROUP * HD)],
            out_hbm.at[:, columns(first + head, GROUP * HD)],
            out_sem.at[head],
        )
        copy.start()
        stores.append(copy)
        here = slice(head * HD, (head + 1) * HD)
        dv = lax.dot_general(
            e_ref[head % 2], dot_ref[head % 2], NT, preferred_element_type=jnp.float32
        ).astype(jnp.bfloat16)
        dvown_ref[:, here] = dv[:own]
        for i, ref in enumerate(term_refs):
            ref[held:, here] = dv[own + i * held : own + (i + 1) * held]
        dk = jnp.dot(
            ds_ref[head % 2],
            heads_down(q_ref, (first + head) * GROUP, GROUP),
            preferred_element_type=jnp.float32,
        )
        dk = (dk * factor).astype(jnp.bfloat16)
        dkown_ref[:, here] = dk[:own]
        for i, ref in enumerate(term_refs):
            ref[:held, here] = dk[own + i * held : own + (i + 1) * held]

    steps = [(head, pair) for head in range(count) for pair in range(pairs)]
    scores(*steps[0])
    inverse = softmax(*steps[0])
    for now, then in zip(steps, steps[1:] + [None]):
        if then:
            scores(*then)
        centre = attended(*now, inverse)
        if then:
            inverse = softmax(*then)
        score_grads(*now, centre)
        query_grads(*now)
        if now[1] + 1 == pairs:
            key_grads(now[0])
    for copy in stores:
        copy.wait()


def turn_kernel(do_ref, after_ref, out_ref):
    out_ref[0] = heads_down(do_ref, 0, GROUP).T


def scale_kernel(slots_all, total_ref, *refs):
    sources, refs = refs[: 3 * CHUNKS], refs[3 * CHUNKS :]
    outs, held, sem = refs[:3], refs[3:6], refs[6]
    weight = slots_all / total_ref[:1, :1]
    copies = []
    for chunk in range(CHUNKS):
        for i in range(3):
            source = sources[chunk * 3 + i]
            cols = pl.ds(chunk * source.shape[1], source.shape[1])
            scaled = source[...].astype(jnp.float32) * weight
            held[i][:, cols] = scaled.astype(jnp.bfloat16)
            copy = pltpu.make_async_copy(held[i].at[:, cols], outs[i].at[:, cols], sem.at[chunk, i])
            copy.start()
            copies.append(copy)
    for copy in copies:
        copy.wait()


def swap(x, axis, by):
    return lax.ppermute(x, axis, [(i, i ^ by) for i in range(lax.axis_size(axis))])


def sum_over(x, axis):
    by = 1
    while by < lax.axis_size(axis):
        x = x + swap(x, axis, by)
        by *= 2
    return x


def line_gather(block, butterfly):
    size = lax.axis_size("response")
    if size != 4 or not butterfly:
        return [block] + [swap(block, "response", m) for m in range(1, size)]
    far = swap(block, "response", 3)
    near = swap(block, "response", 1)
    return [block, near, swap(far, "response", 1), far]


def line_reduce(slots):
    terms = [slots[0]] + [swap(slots[m], "response", m) for m in range(1, len(slots))]
    total = functools.reduce(jnp.add, [term.astype(jnp.float32) for term in terms])
    return total


def own_columns(block, chunk, by):
    cols = block.shape[1] // (lax.axis_size("tensor") * CHUNKS)
    rank = lax.axis_index("tensor") ^ by
    return lax.dynamic_slice_in_dim(block, (rank * CHUNKS + chunk) * cols, cols, 1)


def tensor_gather(blocks, chunk):
    parts = lax.axis_size("tensor")
    pieces = []
    for m in range(parts):
        piece = jnp.concatenate([own_columns(block, chunk, m) for block in blocks], axis=0)
        pieces.append(piece if m == 0 else swap(piece, "tensor", m))
    rows = blocks[0].shape[0]
    return jnp.concatenate(
        [piece[i * rows : (i + 1) * rows] for i in range(len(blocks)) for piece in pieces], axis=0
    )


def tensor_spread(total, n_arrays):
    parts = lax.axis_size("tensor")
    rows = total.shape[0] // (n_arrays * parts)
    pieces = []
    for m in range(parts):
        piece = jnp.concatenate(
            [total[(i * parts + m) * rows : (i * parts + m + 1) * rows] for i in range(n_arrays)],
            axis=0,
        )
        pieces.append(piece if m == 0 else swap(piece, "tensor", m))
    return pieces


def whole_columns(chunk_pieces, array):
    parts = lax.axis_size("tensor")
    rank = lax.axis_index("tensor")
    rows = chunk_pieces[0][0].shape[0] // 2
    by_rank = [
        jnp.concatenate([pieces[m][array * rows : (array + 1) * rows] for pieces in chunk_pieces], axis=1)
        for m in range(parts)
    ]
    ordered = []
    for t in range(parts):
        column = by_rank[0]
        for m in range(1, parts):
            column = jnp.where(rank ^ m == t, by_rank[m], column)
        ordered.append(column)
    return jnp.concatenate(ordered, axis=1)


SMEM = pl.BlockSpec(memory_space=pltpu.SMEM)
HBM = pl.BlockSpec(memory_space=pltpu.HBM)
VMEM = pl.BlockSpec(memory_space=pltpu.VMEM)


def like(x):
    return jax.ShapeDtypeStruct(x.shape, x.dtype)


def turn(do, after):
    rows, heads = do.shape[0], do.shape[1] // (GROUP * HD)
    return pl.pallas_call(
        turn_kernel,
        grid=(heads,),
        in_specs=[pl.BlockSpec((rows, GROUP * HD), lambda j: (0, j)), HBM],
        out_specs=pl.BlockSpec((1, HD, GROUP * rows), lambda j: (j, 0, 0)),
        out_shape=jax.ShapeDtypeStruct((heads, HD, GROUP * rows), do.dtype),
        name="turn",
    )(do, after)


def attend(chunk, held, slots, length, q, turned, k, v, carried):
    rows = q.shape[0]
    count = k.shape[1] // (HD * CHUNKS)
    n_slots = len(slots)
    last = chunk + 1 == CHUNKS
    n_keys = rows + n_slots * held
    bf16 = jnp.bfloat16
    unit = 2 * n_keys * GROUP * rows * HD * count
    step_buffer = pltpu.VMEM((2, n_keys, PAIR * rows), jnp.float32)
    head_buffer = pltpu.VMEM((2, n_keys, GROUP * rows), bf16)
    wide = pltpu.VMEM((rows, count * GROUP * HD), bf16)
    down = pltpu.VMEM((count, n_keys, HD), bf16)
    across = pltpu.VMEM((count, HD, n_keys), bf16)
    scratch = [wide, step_buffer, step_buffer, head_buffer, head_buffer]
    scratch += [pltpu.VMEM((2, HD, GROUP * rows), bf16), down, across, down, across]
    scratch += [pltpu.SemaphoreType.DMA((count,))]
    part = lambda x: jax.ShapeDtypeStruct((x.shape[0], x.shape[1] // CHUNKS), bf16)
    terms = [jax.ShapeDtypeStruct((2 * held, count * HD), bf16)] * n_slots
    total = [jax.ShapeDtypeStruct((8, HD), jnp.float32)] * last
    return pl.pallas_call(
        functools.partial(attend_kernel, n_slots, count, chunk, held, 1.0 / math.sqrt(HD)),
        in_specs=[SMEM] + [VMEM] * (4 + n_slots) + [HBM] * last,
        out_specs=[HBM] + [VMEM] * (3 + n_slots + last),
        out_shape=[like(q), part(q), part(k), part(v)] + terms + total,
        input_output_aliases={5 + n_slots: 0} if last else {},
        scratch_shapes=scratch,
        compiler_params=pltpu.CompilerParams(vmem_limit_bytes=VMEM_LIMIT),
        cost_estimate=pl.CostEstimate(
            flops=24 * unit,
            bytes_accessed=8 * rows * GROUP * HD * count,
            transcendentals=count * n_keys * GROUP * rows,
        ),
        name=f"attend_{chunk}",
    )(length, q, turned, k, v, *slots, *carried)


def scale_all(slots_all, total, chunk_grads, shapes):
    flat = [grad for grads in chunk_grads for grad in grads]
    return pl.pallas_call(
        functools.partial(scale_kernel, slots_all),
        in_specs=[VMEM] * (1 + len(flat)),
        out_specs=[HBM] * len(shapes),
        out_shape=shapes,
        scratch_shapes=[pltpu.VMEM(x.shape, x.dtype) for x in shapes]
        + [pltpu.SemaphoreType.DMA((CHUNKS, len(shapes)))],
        cost_estimate=pl.CostEstimate(
            flops=sum(x.size for x in shapes),
            bytes_accessed=sum(4 * x.size for x in shapes),
            transcendentals=0,
        ),
        name="scale",
    )(total, *flat)


def body(queries, keys, values, prefix_keys, prefix_values, lengths, out_grad):
    q, k, v, do = queries[0], keys[0], values[0], out_grad[0]
    length = lengths[0]
    prefix = (prefix_keys[0], prefix_values[0])
    slots_all = q.shape[0] * lax.axis_size("prompt") * lax.axis_size("response")
    first, second = [tensor_gather(prefix, chunk) for chunk in range(CHUNKS)]
    held = first.shape[0] // 2
    slots = line_gather(first, True)
    length_rows = length[0].astype(second.dtype) + 0 * slots[-1][-EXTRA:]
    next_slots = line_gather(jnp.concatenate([second, length_rows], axis=0), False)
    turned = turn(do, first)
    results = attend(0, held, slots, length, q, turned, k, v, [])
    next_results = attend(1, held, next_slots, length, q, turned, k, v, results[:1])
    sums = [line_reduce(results[4:]), line_reduce(next_results[4:-1])]
    total = sum_over(next_results[-1] + 0 * sums[0][:8, :HD], "prompt")
    weight = slots_all / total[0, 0]
    scaled = scale_all(
        slots_all, total, [results[1:4], next_results[1:4]], [like(q), like(k), like(v)]
    )
    pieces = [tensor_spread(terms.astype(jnp.bfloat16), len(prefix)) for terms in sums]
    grads = [whole_columns(pieces, array) for array in range(len(prefix))]
    grads = [(grad.astype(jnp.float32) * weight).astype(jnp.bfloat16) for grad in grads]
    return tuple(x[None] for x in (next_results[0], *scaled, *grads))


def solution(mesh):
    in_specs = (
        P("prompt", "response", "tensor"),
        P("prompt", "response", "tensor"),
        P("prompt", "response", "tensor"),
        P("prompt", ("response", "tensor"), None),
        P("prompt", ("response", "tensor"), None),
        P("prompt", "response"),
        P("prompt", "response", "tensor"),
    )
    out_specs = (
        P("prompt", "response", "tensor"),
        P("prompt", "response", "tensor"),
        P("prompt", "response", "tensor"),
        P("prompt", "response", "tensor"),
        P("prompt", ("response", "tensor"), None),
        P("prompt", ("response", "tensor"), None),
    )
    return jax.shard_map(body, mesh=mesh, in_specs=in_specs, out_specs=out_specs, check_vma=False)
```

```python
import functools
import math

import jax
import jax.numpy as jnp
from jax import lax
from jax.experimental import pallas as pl
from jax.experimental.pallas import tpu as pltpu
from jax.sharding import PartitionSpec as P

HD = 128
GROUP = 8
PAIR = 2
CHUNKS = 2
EXTRA = 16
STEP = 64
VMEM_LIMIT = 40 * 1024 * 1024
SMALL_LIMIT = 8 * 1024 * 1024
NT = (((1,), (1,)), ((), ()))


def heads_down(ref, first, count):
    return jnp.concatenate(
        [ref[:, (first + i) * HD : (first + i + 1) * HD] for i in range(count)], axis=0
    )


def attend_kernel(n_slots, count, chunk, held, factor, *refs):
    last = chunk + 1 == CHUNKS
    length_ref, q_ref, turned_ref, kown_ref, vown_ref = refs[:5]
    slot_refs, refs = refs[5 : 5 + n_slots], refs[5 + n_slots + last :]
    out_hbm, dq_ref, dkown_ref, dvown_ref = refs[:4]
    term_refs, refs = refs[4 : 4 + n_slots], refs[4 + n_slots :]
    if last:
        total_ref, refs = refs[0], refs[1:]
        totals = [ref[2 * held : 2 * held + 8, :HD].astype(jnp.float32) for ref in slot_refs]
        total_ref[...] = functools.reduce(jnp.add, totals)
    out_ref, s_ref, dp_ref, e_ref, ds_ref, dot_ref = refs[:6]
    keys_ref, keys_t_ref, values_ref, values_t_ref, out_sem = refs[6:]
    first = chunk * count
    rows = q_ref.shape[0]
    own = kown_ref.shape[0]
    n_keys = s_ref.shape[1]
    width = PAIR * rows
    pairs = GROUP // PAIR
    scale = factor * math.log2(math.e)

    def columns(head, size):
        return pl.ds(head * size, size)

    stores = []

    live = (lax.broadcasted_iota(jnp.int32, (1, width), 1) % rows) < length_ref[0]

    def assemble(head, own_ref, slot_start, wide_ref, tall_ref):
        here = slice(head * HD, (head + 1) * HD)
        wide_ref[head, :own] = own_ref[:, (first + head) * HD : (first + head + 1) * HD]
        for i, ref in enumerate(slot_refs):
            part = slice(own + i * held, own + (i + 1) * held)
            wide_ref[head, part] = ref[slot_start : slot_start + held, here]
        tall_ref[head] = wide_ref[head].T

    def place(head, pair):
        return slice(pair * width, (pair + 1) * width)

    def scores(head, pair):
        if pair == 0:
            assemble(head, kown_ref, 0, keys_ref, keys_t_ref)
        s_ref[pair % 2] = lax.dot_general(
            keys_ref[head],
            heads_down(q_ref, (first + head) * GROUP + pair * PAIR, PAIR),
            NT,
            preferred_element_type=jnp.float32,
        )

    def softmax(head, pair):
        here = s_ref.at[pair % 2]
        cols = place(head, pair)
        fold = lambda x: x.reshape(x.shape[0] // 8, 8, width)
        top = jnp.full((8, width), -1e30, jnp.float32)
        for at in range(0, n_keys, STEP):
            x = here[at : at + STEP]
            if at < own:
                key_pos = lax.broadcasted_iota(jnp.int32, x.shape, 0) + at
                row_pos = lax.broadcasted_iota(jnp.int32, x.shape, 1) % rows
                x = jnp.where(key_pos <= row_pos, x, -1e30)
                here[at : at + STEP] = x
            top = jnp.maximum(top, jnp.max(fold(x), axis=0))
        top = jnp.max(top, axis=0, keepdims=True) * scale
        top = jnp.broadcast_to(top, (8, width))
        total = jnp.zeros((8, width), jnp.float32)
        for at in range(0, n_keys, STEP):
            e = jnp.exp2(fold(here[at : at + STEP]) * scale - top)
            total = total + jnp.sum(e, axis=0)
            e_ref[head % 2, at : at + STEP, cols] = e.reshape(-1, width).astype(jnp.bfloat16)
        total = jnp.sum(total, axis=0, keepdims=True)
        inverse = jnp.where(live, 1.0 / total, 0.0)
        grad = turned_ref[first + head, :, cols].astype(jnp.float32) * inverse
        dot_ref[head % 2, :, cols] = grad.astype(jnp.bfloat16)
        return inverse

    def attended(head, pair, inverse):
        cols = place(head, pair)
        if pair == 0:
            assemble(head, vown_ref, held, values_ref, values_t_ref)
        grad = dot_ref[head % 2, :, cols]
        dp_ref[pair % 2] = jnp.dot(values_ref[head], grad, preferred_element_type=jnp.float32)
        out = jnp.dot(
            values_t_ref[head], e_ref[head % 2, :, cols], preferred_element_type=jnp.float32
        )
        out = out * inverse
        turned = out.astype(jnp.bfloat16).T
        for i in range(PAIR):
            at = head * GROUP + pair * PAIR + i
            out_ref[:, at * HD : (at + 1) * HD] = turned[i * rows : (i + 1) * rows]
        return jnp.sum(out * grad.astype(jnp.float32), axis=0, keepdims=True)

    def score_grads(head, pair, centre):
        cols = place(head, pair)
        here = dp_ref.at[pair % 2]
        centre = jnp.broadcast_to(centre, (STEP, width))
        for at in range(0, n_keys, STEP):
            e = e_ref[head % 2, at : at + STEP, cols].astype(jnp.float32)
            grad = e * (here[at : at + STEP] - centre)
            ds_ref[head % 2, at : at + STEP, cols] = grad.astype(jnp.bfloat16)

    def query_grads(head, pair):
        cols = place(head, pair)
        dq = jnp.dot(
            keys_t_ref[head], ds_ref[head % 2, :, cols], preferred_element_type=jnp.float32
        )
        turned = (dq * factor).astype(jnp.bfloat16).T
        for i in range(PAIR):
            at = head * GROUP + pair * PAIR + i
            dq_ref[:, at * HD : (at + 1) * HD] = turned[i * rows : (i + 1) * rows]

    def key_grads(head):
        copy = pltpu.make_async_copy(
            out_ref.at[:, columns(head, GROUP * HD)],
            out_hbm.at[:, columns(first + head, GROUP * HD)],
            out_sem.at[head],
        )
        copy.start()
        stores.append(copy)
        here = slice(head * HD, (head + 1) * HD)
        dv = lax.dot_general(
            e_ref[head % 2], dot_ref[head % 2], NT, preferred_element_type=jnp.float32
        ).astype(jnp.bfloat16)
        dvown_ref[:, here] = dv[:own]
        for i, ref in enumerate(term_refs):
            ref[held:, here] = dv[own + i * held : own + (i + 1) * held]
        dk = jnp.dot(
            ds_ref[head % 2],
            heads_down(q_ref, (first + head) * GROUP, GROUP),
            preferred_element_type=jnp.float32,
        )
        dk = (dk * factor).astype(jnp.bfloat16)
        dkown_ref[:, here] = dk[:own]
        for i, ref in enumerate(term_refs):
            ref[:held, here] = dk[own + i * held : own + (i + 1) * held]

    steps = [(head, pair) for head in range(count) for pair in range(pairs)]
    scores(*steps[0])
    inverse = softmax(*steps[0])
    for now, then in zip(steps, steps[1:] + [None]):
        if then:
            scores(*then)
        centre = attended(*now, inverse)
        if then:
            inverse = softmax(*then)
        score_grads(*now, centre)
        query_grads(*now)
        if now[1] + 1 == pairs:
            key_grads(now[0])
    for copy in stores:
        copy.wait()


def turn_kernel(do_ref, after_ref, out_ref):
    out_ref[0] = heads_down(do_ref, 0, GROUP).T


def scale_kernel(slots_all, total_ref, *refs):
    sources, refs = refs[: 3 * CHUNKS], refs[3 * CHUNKS :]
    outs, held, sem = refs[:3], refs[3:6], refs[6]
    weight = slots_all / total_ref[:1, :1]
    copies = []
    for chunk in range(CHUNKS):
        for i in range(3):
            source = sources[chunk * 3 + i]
            cols = pl.ds(chunk * source.shape[1], source.shape[1])
            scaled = source[...].astype(jnp.float32) * weight
            held[i][:, cols] = scaled.astype(jnp.bfloat16)
            copy = pltpu.make_async_copy(held[i].at[:, cols], outs[i].at[:, cols], sem.at[chunk, i])
            copy.start()
            copies.append(copy)
    for copy in copies:
        copy.wait()


def swap(x, axis, by):
    return lax.ppermute(x, axis, [(i, i ^ by) for i in range(lax.axis_size(axis))])


def sum_over(x, axis):
    by = 1
    while by < lax.axis_size(axis):
        x = x + swap(x, axis, by)
        by *= 2
    return x


def line_gather(block, butterfly):
    size = lax.axis_size("response")
    if size != 4 or not butterfly:
        return [block] + [swap(block, "response", m) for m in range(1, size)]
    far = swap(block, "response", 3)
    near = swap(block, "response", 1)
    return [block, near, swap(far, "response", 1), far]


def line_reduce(slots):
    terms = [slots[0]] + [swap(slots[m], "response", m) for m in range(1, len(slots))]
    total = functools.reduce(jnp.add, [term.astype(jnp.float32) for term in terms])
    return total


def own_columns(block, chunk, by):
    cols = block.shape[1] // (lax.axis_size("tensor") * CHUNKS)
    rank = lax.axis_index("tensor") ^ by
    return lax.dynamic_slice_in_dim(block, (rank * CHUNKS + chunk) * cols, cols, 1)


def tensor_gather(blocks, chunk):
    parts = lax.axis_size("tensor")
    pieces = []
    for m in range(parts):
        piece = jnp.concatenate([own_columns(block, chunk, m) for block in blocks], axis=0)
        pieces.append(piece if m == 0 else swap(piece, "tensor", m))
    rows = blocks[0].shape[0]
    return jnp.concatenate(
        [piece[i * rows : (i + 1) * rows] for i in range(len(blocks)) for piece in pieces], axis=0
    )


def tensor_spread(total, n_arrays):
    parts = lax.axis_size("tensor")
    rows = total.shape[0] // (n_arrays * parts)
    pieces = []
    for m in range(parts):
        piece = jnp.concatenate(
            [total[(i * parts + m) * rows : (i * parts + m + 1) * rows] for i in range(n_arrays)],
            axis=0,
        )
        pieces.append(piece if m == 0 else swap(piece, "tensor", m))
    return pieces


def whole_columns(chunk_pieces, array):
    parts = lax.axis_size("tensor")
    rank = lax.axis_index("tensor")
    rows = chunk_pieces[0][0].shape[0] // 2
    by_rank = [
        jnp.concatenate([pieces[m][array * rows : (array + 1) * rows] for pieces in chunk_pieces], axis=1)
        for m in range(parts)
    ]
    ordered = []
    for t in range(parts):
        column = by_rank[0]
        for m in range(1, parts):
            column = jnp.where(rank ^ m == t, by_rank[m], column)
        ordered.append(column)
    return jnp.concatenate(ordered, axis=1)


SMEM = pl.BlockSpec(memory_space=pltpu.SMEM)
HBM = pl.BlockSpec(memory_space=pltpu.HBM)
VMEM = pl.BlockSpec(memory_space=pltpu.VMEM)


def like(x):
    return jax.ShapeDtypeStruct(x.shape, x.dtype)


def turn(do, after):
    rows, heads = do.shape[0], do.shape[1] // (GROUP * HD)
    return pl.pallas_call(
        turn_kernel,
        grid=(heads,),
        in_specs=[pl.BlockSpec((rows, GROUP * HD), lambda j: (0, j)), HBM],
        out_specs=pl.BlockSpec((1, HD, GROUP * rows), lambda j: (j, 0, 0)),
        out_shape=jax.ShapeDtypeStruct((heads, HD, GROUP * rows), do.dtype),
        compiler_params=pltpu.CompilerParams(vmem_limit_bytes=SMALL_LIMIT),
        name="turn",
    )(do, after)


def attend(chunk, held, slots, length, q, turned, k, v, carried):
    rows = q.shape[0]
    count = k.shape[1] // (HD * CHUNKS)
    n_slots = len(slots)
    last = chunk + 1 == CHUNKS
    n_keys = rows + n_slots * held
    bf16 = jnp.bfloat16
    unit = 2 * n_keys * GROUP * rows * HD * count
    step_buffer = pltpu.VMEM((2, n_keys, PAIR * rows), jnp.float32)
    head_buffer = pltpu.VMEM((2, n_keys, GROUP * rows), bf16)
    wide = pltpu.VMEM((rows, count * GROUP * HD), bf16)
    down = pltpu.VMEM((count, n_keys, HD), bf16)
    across = pltpu.VMEM((count, HD, n_keys), bf16)
    scratch = [wide, step_buffer, step_buffer, head_buffer, head_buffer]
    scratch += [pltpu.VMEM((2, HD, GROUP * rows), bf16), down, across, down, across]
    scratch += [pltpu.SemaphoreType.DMA((count,))]
    part = lambda x: jax.ShapeDtypeStruct((x.shape[0], x.shape[1] // CHUNKS), bf16)
    terms = [jax.ShapeDtypeStruct((2 * held, count * HD), bf16)] * n_slots
    total = [jax.ShapeDtypeStruct((8, HD), jnp.float32)] * last
    return pl.pallas_call(
        functools.partial(attend_kernel, n_slots, count, chunk, held, 1.0 / math.sqrt(HD)),
        in_specs=[SMEM] + [VMEM] * (4 + n_slots) + [HBM] * last,
        out_specs=[HBM] + [VMEM] * (3 + n_slots + last),
        out_shape=[like(q), part(q), part(k), part(v)] + terms + total,
        input_output_aliases={5 + n_slots: 0} if last else {},
        scratch_shapes=scratch,
        compiler_params=pltpu.CompilerParams(vmem_limit_bytes=VMEM_LIMIT),
        cost_estimate=pl.CostEstimate(
            flops=24 * unit,
            bytes_accessed=8 * rows * GROUP * HD * count,
            transcendentals=count * n_keys * GROUP * rows,
        ),
        name=f"attend_{chunk}",
    )(length, q, turned, k, v, *slots, *carried)


def scale_all(slots_all, total, chunk_grads, shapes):
    flat = [grad for grads in chunk_grads for grad in grads]
    return pl.pallas_call(
        functools.partial(scale_kernel, slots_all),
        in_specs=[VMEM] * (1 + len(flat)),
        out_specs=[HBM] * len(shapes),
        out_shape=shapes,
        scratch_shapes=[pltpu.VMEM(x.shape, x.dtype) for x in shapes]
        + [pltpu.SemaphoreType.DMA((CHUNKS, len(shapes)))],
        compiler_params=pltpu.CompilerParams(vmem_limit_bytes=SMALL_LIMIT),
        cost_estimate=pl.CostEstimate(
            flops=sum(x.size for x in shapes),
            bytes_accessed=sum(4 * x.size for x in shapes),
            transcendentals=0,
        ),
        name="scale",
    )(total, *flat)


def body(queries, keys, values, prefix_keys, prefix_values, lengths, out_grad):
    q, k, v, do = queries[0], keys[0], values[0], out_grad[0]
    length = lengths[0]
    prefix = (prefix_keys[0], prefix_values[0])
    slots_all = q.shape[0] * lax.axis_size("prompt") * lax.axis_size("response")
    first, second = [tensor_gather(prefix, chunk) for chunk in range(CHUNKS)]
    held = first.shape[0] // 2
    slots = line_gather(first, True)
    length_rows = length[0].astype(second.dtype) + 0 * slots[-1][-EXTRA:]
    next_slots = line_gather(jnp.concatenate([second, length_rows], axis=0), False)
    turned = turn(do, first)
    results = attend(0, held, slots, length, q, turned, k, v, [])
    next_results = attend(1, held, next_slots, length, q, turned, k, v, results[:1])
    sums = [line_reduce(results[4:]), line_reduce(next_results[4:-1])]
    total = sum_over(next_results[-1] + 0 * sums[0][:8, :HD], "prompt")
    weight = jnp.tile(slots_all / total[:1], (1, prefix[0].shape[1] // HD))
    scaled = scale_all(
        slots_all, total, [results[1:4], next_results[1:4]], [like(q), like(k), like(v)]
    )
    pieces = [tensor_spread(terms.astype(jnp.bfloat16), len(prefix)) for terms in sums]
    grads = [whole_columns(pieces, array) for array in range(len(prefix))]
    grads = [(grad.astype(jnp.float32) * weight).astype(jnp.bfloat16) for grad in grads]
    return tuple(x[None] for x in (next_results[0], *scaled, *grads))


def solution(mesh):
    in_specs = (
        P("prompt", "response", "tensor"),
        P("prompt", "response", "tensor"),
        P("prompt", "response", "tensor"),
        P("prompt", ("response", "tensor"), None),
        P("prompt", ("response", "tensor"), None),
        P("prompt", "response"),
        P("prompt", "response", "tensor"),
    )
    out_specs = (
        P("prompt", "response", "tensor"),
        P("prompt", "response", "tensor"),
        P("prompt", "response", "tensor"),
        P("prompt", "response", "tensor"),
        P("prompt", ("response", "tensor"), None),
        P("prompt", ("response", "tensor"), None),
    )
    return jax.shard_map(body, mesh=mesh, in_specs=in_specs, out_specs=out_specs, check_vma=False)
```

```python
import functools
import math

import jax
import jax.numpy as jnp
from jax import lax
from jax.experimental import pallas as pl
from jax.experimental.pallas import tpu as pltpu
from jax.sharding import PartitionSpec as P

HD = 128
GROUP = 8
PAIR = 2
CHUNKS = 2
EXTRA = 16
STEP = 64
VMEM_LIMIT = 40 * 1024 * 1024
SMALL_LIMIT = 8 * 1024 * 1024
NT = (((1,), (1,)), ((), ()))


def heads_down(ref, first, count):
    return jnp.concatenate(
        [ref[:, (first + i) * HD : (first + i + 1) * HD] for i in range(count)], axis=0
    )


def attend_kernel(n_slots, count, chunk, held, factor, *refs):
    last = chunk + 1 == CHUNKS
    length_ref, q_ref, turned_ref, kown_ref, vown_ref = refs[:5]
    slot_refs, refs = refs[5 : 5 + n_slots], refs[5 + n_slots + last :]
    out_hbm, dq_ref, dkown_ref, dvown_ref = refs[:4]
    term_refs, refs = refs[4 : 4 + n_slots], refs[4 + n_slots :]
    if last:
        total_ref, refs = refs[0], refs[1:]
        totals = [ref[2 * held : 2 * held + 8, :HD].astype(jnp.float32) for ref in slot_refs]
        total_ref[...] = functools.reduce(jnp.add, totals)
    out_ref, s_ref, dp_ref, e_ref, ds_ref, dot_ref = refs[:6]
    keys_ref, keys_t_ref, values_ref, values_t_ref, out_sem = refs[6:]
    first = chunk * count
    rows = q_ref.shape[0]
    own = kown_ref.shape[0]
    n_keys = s_ref.shape[1]
    width = PAIR * rows
    pairs = GROUP // PAIR
    scale = factor * math.log2(math.e)

    def columns(head, size):
        return pl.ds(head * size, size)

    stores = []

    live = (lax.broadcasted_iota(jnp.int32, (1, width), 1) % rows) < length_ref[0]

    def assemble(head, own_ref, slot_start, wide_ref, tall_ref):
        here = slice(head * HD, (head + 1) * HD)
        wide_ref[head, :own] = own_ref[:, (first + head) * HD : (first + head + 1) * HD]
        for i, ref in enumerate(slot_refs):
            part = slice(own + i * held, own + (i + 1) * held)
            wide_ref[head, part] = ref[slot_start : slot_start + held, here]
        tall_ref[head] = wide_ref[head].T

    def place(head, pair):
        return slice(pair * width, (pair + 1) * width)

    def scores(head, pair):
        if pair == 0:
            assemble(head, kown_ref, 0, keys_ref, keys_t_ref)
        s_ref[pair % 2] = lax.dot_general(
            keys_ref[head],
            heads_down(q_ref, (first + head) * GROUP + pair * PAIR, PAIR),
            NT,
            preferred_element_type=jnp.float32,
        )

    def softmax(head, pair):
        here = s_ref.at[pair % 2]
        cols = place(head, pair)
        fold = lambda x: x.reshape(x.shape[0] // 8, 8, width)
        top = jnp.full((8, width), -1e30, jnp.float32)
        for at in range(0, n_keys, STEP):
            x = here[at : at + STEP]
            if at < own:
                key_pos = lax.broadcasted_iota(jnp.int32, x.shape, 0) + at
                row_pos = lax.broadcasted_iota(jnp.int32, x.shape, 1) % rows
                x = jnp.where(key_pos <= row_pos, x, -1e30)
                here[at : at + STEP] = x
            top = jnp.maximum(top, jnp.max(fold(x), axis=0))
        top = jnp.max(top, axis=0, keepdims=True) * scale
        top = jnp.broadcast_to(top, (8, width))
        total = jnp.zeros((8, width), jnp.float32)
        for at in range(0, n_keys, STEP):
            e = jnp.exp2(fold(here[at : at + STEP]) * scale - top)
            total = total + jnp.sum(e, axis=0)
            e_ref[head % 2, at : at + STEP, cols] = e.reshape(-1, width).astype(jnp.bfloat16)
        total = jnp.sum(total, axis=0, keepdims=True)
        inverse = jnp.where(live, 1.0 / total, 0.0)
        grad = turned_ref[first + head, :, cols].astype(jnp.float32) * inverse
        dot_ref[head % 2, :, cols] = grad.astype(jnp.bfloat16)
        return inverse

    def attended(head, pair, inverse):
        cols = place(head, pair)
        if pair == 0:
            assemble(head, vown_ref, held, values_ref, values_t_ref)
        grad = dot_ref[head % 2, :, cols]
        dp_ref[pair % 2] = jnp.dot(values_ref[head], grad, preferred_element_type=jnp.float32)
        out = jnp.dot(
            values_t_ref[head], e_ref[head % 2, :, cols], preferred_element_type=jnp.float32
        )
        out = out * inverse
        turned = out.astype(jnp.bfloat16).T
        for i in range(PAIR):
            at = head * GROUP + pair * PAIR + i
            out_ref[:, at * HD : (at + 1) * HD] = turned[i * rows : (i + 1) * rows]
        return jnp.sum(out * grad.astype(jnp.float32), axis=0, keepdims=True)

    def score_grads(head, pair, centre):
        cols = place(head, pair)
        here = dp_ref.at[pair % 2]
        centre = jnp.broadcast_to(centre, (STEP, width))
        for at in range(0, n_keys, STEP):
            e = e_ref[head % 2, at : at + STEP, cols].astype(jnp.float32)
            grad = e * (here[at : at + STEP] - centre)
            ds_ref[head % 2, at : at + STEP, cols] = grad.astype(jnp.bfloat16)

    def query_grads(head, pair):
        cols = place(head, pair)
        dq = jnp.dot(
            keys_t_ref[head], ds_ref[head % 2, :, cols], preferred_element_type=jnp.float32
        )
        turned = (dq * factor).astype(jnp.bfloat16).T
        for i in range(PAIR):
            at = head * GROUP + pair * PAIR + i
            dq_ref[:, at * HD : (at + 1) * HD] = turned[i * rows : (i + 1) * rows]

    def key_grads(head):
        copy = pltpu.make_async_copy(
            out_ref.at[:, columns(head, GROUP * HD)],
            out_hbm.at[:, columns(first + head, GROUP * HD)],
            out_sem.at[head],
        )
        copy.start()
        stores.append(copy)
        here = slice(head * HD, (head + 1) * HD)
        dv = lax.dot_general(
            e_ref[head % 2], dot_ref[head % 2], NT, preferred_element_type=jnp.float32
        ).astype(jnp.bfloat16)
        dvown_ref[:, here] = dv[:own]
        for i, ref in enumerate(term_refs):
            ref[held:, here] = dv[own + i * held : own + (i + 1) * held]
        dk = jnp.dot(
            ds_ref[head % 2],
            heads_down(q_ref, (first + head) * GROUP, GROUP),
            preferred_element_type=jnp.float32,
        )
        dk = (dk * factor).astype(jnp.bfloat16)
        dkown_ref[:, here] = dk[:own]
        for i, ref in enumerate(term_refs):
            ref[:held, here] = dk[own + i * held : own + (i + 1) * held]

    steps = [(head, pair) for head in range(count) for pair in range(pairs)]
    scores(*steps[0])
    inverse = softmax(*steps[0])
    for now, then in zip(steps, steps[1:] + [None]):
        if then:
            scores(*then)
        centre = attended(*now, inverse)
        if then:
            inverse = softmax(*then)
        score_grads(*now, centre)
        query_grads(*now)
        if now[1] + 1 == pairs:
            key_grads(now[0])
    for copy in stores:
        copy.wait()


def turn_kernel(do_ref, after_ref, out_ref):
    out_ref[0] = heads_down(do_ref, 0, GROUP).T


def scale_kernel(slots_all, total_ref, *refs):
    sources, refs = refs[: 3 * CHUNKS], refs[3 * CHUNKS :]
    outs, held, sem = refs[:3], refs[3:6], refs[6]
    weight = slots_all / total_ref[:1, :1]
    copies = []
    for chunk in range(CHUNKS):
        for i in range(3):
            source = sources[chunk * 3 + i]
            cols = pl.ds(chunk * source.shape[1], source.shape[1])
            scaled = source[...].astype(jnp.float32) * weight
            held[i][:, cols] = scaled.astype(jnp.bfloat16)
            copy = pltpu.make_async_copy(held[i].at[:, cols], outs[i].at[:, cols], sem.at[chunk, i])
            copy.start()
            copies.append(copy)
    for copy in copies:
        copy.wait()


def swap(x, axis, by):
    return lax.ppermute(x, axis, [(i, i ^ by) for i in range(lax.axis_size(axis))])


def sum_over(x, axis):
    by = 1
    while by < lax.axis_size(axis):
        x = x + swap(x, axis, by)
        by *= 2
    return x


def line_gather(block, butterfly):
    size = lax.axis_size("response")
    if size != 4 or not butterfly:
        return [block] + [swap(block, "response", m) for m in range(1, size)]
    far = swap(block, "response", 3)
    near = swap(block, "response", 1)
    return [block, near, swap(far, "response", 1), far]


def line_reduce(slots):
    terms = [swap(slots[m], "response", m) for m in range(len(slots) - 1, 0, -1)]
    return functools.reduce(jnp.add, [term.astype(jnp.float32) for term in [slots[0]] + terms])


def own_columns(block, chunk, by):
    cols = block.shape[1] // (lax.axis_size("tensor") * CHUNKS)
    rank = lax.axis_index("tensor") ^ by
    return lax.dynamic_slice_in_dim(block, (rank * CHUNKS + chunk) * cols, cols, 1)


def tensor_gather(blocks, chunk):
    parts = lax.axis_size("tensor")
    pieces = []
    for m in range(parts):
        piece = jnp.concatenate([own_columns(block, chunk, m) for block in blocks], axis=0)
        pieces.append(piece if m == 0 else swap(piece, "tensor", m))
    rows = blocks[0].shape[0]
    return jnp.concatenate(
        [piece[i * rows : (i + 1) * rows] for i in range(len(blocks)) for piece in pieces], axis=0
    )


def tensor_spread(total, n_arrays):
    parts = lax.axis_size("tensor")
    rows = total.shape[0] // (n_arrays * parts)
    pieces = []
    for m in range(parts):
        piece = jnp.concatenate(
            [total[(i * parts + m) * rows : (i * parts + m + 1) * rows] for i in range(n_arrays)],
            axis=0,
        )
        pieces.append(piece if m == 0 else swap(piece, "tensor", m))
    return pieces


def whole_columns(chunk_pieces, array):
    parts = lax.axis_size("tensor")
    rank = lax.axis_index("tensor")
    rows = chunk_pieces[0][0].shape[0] // 2
    by_rank = [
        jnp.concatenate([pieces[m][array * rows : (array + 1) * rows] for pieces in chunk_pieces], axis=1)
        for m in range(parts)
    ]
    ordered = []
    for t in range(parts):
        column = by_rank[0]
        for m in range(1, parts):
            column = jnp.where(rank ^ m == t, by_rank[m], column)
        ordered.append(column)
    return jnp.concatenate(ordered, axis=1)


SMEM = pl.BlockSpec(memory_space=pltpu.SMEM)
HBM = pl.BlockSpec(memory_space=pltpu.HBM)
VMEM = pl.BlockSpec(memory_space=pltpu.VMEM)


def like(x):
    return jax.ShapeDtypeStruct(x.shape, x.dtype)


def turn(do, after):
    rows, heads = do.shape[0], do.shape[1] // (GROUP * HD)
    return pl.pallas_call(
        turn_kernel,
        grid=(heads,),
        in_specs=[pl.BlockSpec((rows, GROUP * HD), lambda j: (0, j)), HBM],
        out_specs=pl.BlockSpec((1, HD, GROUP * rows), lambda j: (j, 0, 0)),
        out_shape=jax.ShapeDtypeStruct((heads, HD, GROUP * rows), do.dtype),
        compiler_params=pltpu.CompilerParams(vmem_limit_bytes=SMALL_LIMIT),
        name="turn",
    )(do, after)


def attend(chunk, held, slots, length, q, turned, k, v, carried):
    rows = q.shape[0]
    count = k.shape[1] // (HD * CHUNKS)
    n_slots = len(slots)
    last = chunk + 1 == CHUNKS
    n_keys = rows + n_slots * held
    bf16 = jnp.bfloat16
    unit = 2 * n_keys * GROUP * rows * HD * count
    step_buffer = pltpu.VMEM((2, n_keys, PAIR * rows), jnp.float32)
    head_buffer = pltpu.VMEM((2, n_keys, GROUP * rows), bf16)
    wide = pltpu.VMEM((rows, count * GROUP * HD), bf16)
    down = pltpu.VMEM((count, n_keys, HD), bf16)
    across = pltpu.VMEM((count, HD, n_keys), bf16)
    scratch = [wide, step_buffer, step_buffer, head_buffer, head_buffer]
    scratch += [pltpu.VMEM((2, HD, GROUP * rows), bf16), down, across, down, across]
    scratch += [pltpu.SemaphoreType.DMA((count,))]
    part = lambda x: jax.ShapeDtypeStruct((x.shape[0], x.shape[1] // CHUNKS), bf16)
    terms = [jax.ShapeDtypeStruct((2 * held, count * HD), bf16)] * n_slots
    total = [jax.ShapeDtypeStruct((8, HD), jnp.float32)] * last
    return pl.pallas_call(
        functools.partial(attend_kernel, n_slots, count, chunk, held, 1.0 / math.sqrt(HD)),
        in_specs=[SMEM] + [VMEM] * (4 + n_slots) + [HBM] * last,
        out_specs=[HBM] + [VMEM] * (3 + n_slots + last),
        out_shape=[like(q), part(q), part(k), part(v)] + terms + total,
        input_output_aliases={5 + n_slots: 0} if last else {},
        scratch_shapes=scratch,
        compiler_params=pltpu.CompilerParams(vmem_limit_bytes=VMEM_LIMIT),
        cost_estimate=pl.CostEstimate(
            flops=24 * unit,
            bytes_accessed=8 * rows * GROUP * HD * count,
            transcendentals=count * n_keys * GROUP * rows,
        ),
        name=f"attend_{chunk}",
    )(length, q, turned, k, v, *slots, *carried)


def scale_all(slots_all, total, chunk_grads, shapes):
    flat = [grad for grads in chunk_grads for grad in grads]
    return pl.pallas_call(
        functools.partial(scale_kernel, slots_all),
        in_specs=[VMEM] * (1 + len(flat)),
        out_specs=[HBM] * len(shapes),
        out_shape=shapes,
        scratch_shapes=[pltpu.VMEM(x.shape, x.dtype) for x in shapes]
        + [pltpu.SemaphoreType.DMA((CHUNKS, len(shapes)))],
        compiler_params=pltpu.CompilerParams(vmem_limit_bytes=SMALL_LIMIT),
        cost_estimate=pl.CostEstimate(
            flops=sum(x.size for x in shapes),
            bytes_accessed=sum(4 * x.size for x in shapes),
            transcendentals=0,
        ),
        name="scale",
    )(total, *flat)


def body(queries, keys, values, prefix_keys, prefix_values, lengths, out_grad):
    q, k, v, do = queries[0], keys[0], values[0], out_grad[0]
    length = lengths[0]
    prefix = (prefix_keys[0], prefix_values[0])
    slots_all = q.shape[0] * lax.axis_size("prompt") * lax.axis_size("response")
    first, second = [tensor_gather(prefix, chunk) for chunk in range(CHUNKS)]
    held = first.shape[0] // 2
    slots = line_gather(first, True)
    turned = turn(do, slots[-1])
    length_rows = length[0].astype(second.dtype) + 0 * turned[0, :EXTRA, : second.shape[1]]
    next_slots = line_gather(jnp.concatenate([second, length_rows], axis=0), False)
    results = attend(0, held, slots, length, q, turned, k, v, [])
    next_results = attend(1, held, next_slots, length, q, turned, k, v, results[:1])
    sums = [line_reduce(results[4:]), line_reduce(next_results[4:-1])]
    total = sum_over(next_results[-1] + 0 * sums[0][:8, :HD], "prompt")
    weight = jnp.tile(slots_all / total[:1], (1, prefix[0].shape[1] // HD))
    scaled = scale_all(
        slots_all, total, [results[1:4], next_results[1:4]], [like(q), like(k), like(v)]
    )
    pieces = [tensor_spread(terms.astype(jnp.bfloat16), len(prefix)) for terms in sums]
    grads = [whole_columns(pieces, array) for array in range(len(prefix))]
    grads = [(grad.astype(jnp.float32) * weight).astype(jnp.bfloat16) for grad in grads]
    return tuple(x[None] for x in (next_results[0], *scaled, *grads))


def solution(mesh):
    in_specs = (
        P("prompt", "response", "tensor"),
        P("prompt", "response", "tensor"),
        P("prompt", "response", "tensor"),
        P("prompt", ("response", "tensor"), None),
        P("prompt", ("response", "tensor"), None),
        P("prompt", "response"),
        P("prompt", "response", "tensor"),
    )
    out_specs = (
        P("prompt", "response", "tensor"),
        P("prompt", "response", "tensor"),
        P("prompt", "response", "tensor"),
        P("prompt", "response", "tensor"),
        P("prompt", ("response", "tensor"), None),
        P("prompt", ("response", "tensor"), None),
    )
    return jax.shard_map(body, mesh=mesh, in_specs=in_specs, out_specs=out_specs, check_vma=False)
```

```python
import functools
import math

import jax
import jax.numpy as jnp
from jax import lax
from jax.experimental import pallas as pl
from jax.experimental.pallas import tpu as pltpu
from jax.sharding import PartitionSpec as P

HD = 128
GROUP = 8
PAIR = 2
CHUNKS = 2
EXTRA = 16
STEP = 64
VMEM_LIMIT = 40 * 1024 * 1024
SMALL_LIMIT = 8 * 1024 * 1024
NT = (((1,), (1,)), ((), ()))


def heads_down(ref, first, count):
    return jnp.concatenate(
        [ref[:, (first + i) * HD : (first + i + 1) * HD] for i in range(count)], axis=0
    )


def attend_kernel(n_slots, count, chunk, held, factor, *refs):
    last = chunk + 1 == CHUNKS
    length_ref, q_ref, turned_ref, kown_ref, vown_ref = refs[:5]
    slot_refs, refs = refs[5 : 5 + n_slots], refs[5 + n_slots + last :]
    out_hbm, dq_ref, dkown_ref, dvown_ref = refs[:4]
    term_refs, refs = refs[4 : 4 + n_slots], refs[4 + n_slots :]
    if last:
        total_ref, refs = refs[0], refs[1:]
        totals = [ref[2 * held : 2 * held + 8, :HD].astype(jnp.float32) for ref in slot_refs]
        total_ref[...] = functools.reduce(jnp.add, totals)
    out_ref, s_ref, dp_ref, e_ref, ds_ref, dot_ref = refs[:6]
    keys_ref, keys_t_ref, values_ref, values_t_ref, out_sem = refs[6:]
    first = chunk * count
    rows = q_ref.shape[0]
    own = kown_ref.shape[0]
    n_keys = s_ref.shape[1]
    width = PAIR * rows
    pairs = GROUP // PAIR
    scale = factor * math.log2(math.e)

    def columns(head, size):
        return pl.ds(head * size, size)

    stores = []

    live = (lax.broadcasted_iota(jnp.int32, (1, width), 1) % rows) < length_ref[0]

    def assemble(head, own_ref, slot_start, wide_ref, tall_ref):
        here = slice(head * HD, (head + 1) * HD)
        wide_ref[head, :own] = own_ref[:, (first + head) * HD : (first + head + 1) * HD]
        for i, ref in enumerate(slot_refs):
            part = slice(own + i * held, own + (i + 1) * held)
            wide_ref[head, part] = ref[slot_start : slot_start + held, here]
        tall_ref[head] = wide_ref[head].T

    def place(head, pair):
        return slice(pair * width, (pair + 1) * width)

    def scores(head, pair):
        if pair == 0:
            assemble(head, kown_ref, 0, keys_ref, keys_t_ref)
        s_ref[pair % 2] = lax.dot_general(
            keys_ref[head],
            heads_down(q_ref, (first + head) * GROUP + pair * PAIR, PAIR),
            NT,
            preferred_element_type=jnp.float32,
        )

    def softmax(head, pair):
        here = s_ref.at[pair % 2]
        cols = place(head, pair)
        fold = lambda x: x.reshape(x.shape[0] // 8, 8, width)
        top = jnp.full((8, width), -1e30, jnp.float32)
        for at in range(0, n_keys, STEP):
            x = here[at : at + STEP]
            if at < own:
                key_pos = lax.broadcasted_iota(jnp.int32, x.shape, 0) + at
                row_pos = lax.broadcasted_iota(jnp.int32, x.shape, 1) % rows
                x = jnp.where(key_pos <= row_pos, x, -1e30)
                here[at : at + STEP] = x
            top = jnp.maximum(top, jnp.max(fold(x), axis=0))
        top = jnp.max(top, axis=0, keepdims=True) * scale
        top = jnp.broadcast_to(top, (8, width))
        total = jnp.zeros((8, width), jnp.float32)
        for at in range(0, n_keys, STEP):
            e = jnp.exp2(fold(here[at : at + STEP]) * scale - top)
            total = total + jnp.sum(e, axis=0)
            e_ref[head % 2, at : at + STEP, cols] = e.reshape(-1, width).astype(jnp.bfloat16)
        total = jnp.sum(total, axis=0, keepdims=True)
        inverse = jnp.where(live, 1.0 / total, 0.0)
        grad = turned_ref[first + head, :, cols].astype(jnp.float32) * inverse
        dot_ref[head % 2, :, cols] = grad.astype(jnp.bfloat16)
        return inverse

    def attended(head, pair, inverse):
        cols = place(head, pair)
        if pair == 0:
            assemble(head, vown_ref, held, values_ref, values_t_ref)
        grad = dot_ref[head % 2, :, cols]
        dp_ref[pair % 2] = jnp.dot(values_ref[head], grad, preferred_element_type=jnp.float32)
        out = jnp.dot(
            values_t_ref[head], e_ref[head % 2, :, cols], preferred_element_type=jnp.float32
        )
        out = out * inverse
        turned = out.astype(jnp.bfloat16).T
        for i in range(PAIR):
            at = head * GROUP + pair * PAIR + i
            out_ref[:, at * HD : (at + 1) * HD] = turned[i * rows : (i + 1) * rows]
        return jnp.sum(out * grad.astype(jnp.float32), axis=0, keepdims=True)

    def score_grads(head, pair, centre):
        cols = place(head, pair)
        here = dp_ref.at[pair % 2]
        centre = jnp.broadcast_to(centre, (STEP, width))
        for at in range(0, n_keys, STEP):
            e = e_ref[head % 2, at : at + STEP, cols].astype(jnp.float32)
            grad = e * (here[at : at + STEP] - centre)
            ds_ref[head % 2, at : at + STEP, cols] = grad.astype(jnp.bfloat16)

    def query_grads(head, pair):
        cols = place(head, pair)
        dq = jnp.dot(
            keys_t_ref[head], ds_ref[head % 2, :, cols], preferred_element_type=jnp.float32
        )
        turned = (dq * factor).astype(jnp.bfloat16).T
        for i in range(PAIR):
            at = head * GROUP + pair * PAIR + i
            dq_ref[:, at * HD : (at + 1) * HD] = turned[i * rows : (i + 1) * rows]

    def key_grads(head):
        copy = pltpu.make_async_copy(
            out_ref.at[:, columns(head, GROUP * HD)],
            out_hbm.at[:, columns(first + head, GROUP * HD)],
            out_sem.at[head],
        )
        copy.start()
        stores.append(copy)
        here = slice(head * HD, (head + 1) * HD)
        dv = lax.dot_general(
            e_ref[head % 2], dot_ref[head % 2], NT, preferred_element_type=jnp.float32
        ).astype(jnp.bfloat16)
        dvown_ref[:, here] = dv[:own]
        for i, ref in enumerate(term_refs):
            ref[held:, here] = dv[own + i * held : own + (i + 1) * held]
        dk = jnp.dot(
            ds_ref[head % 2],
            heads_down(q_ref, (first + head) * GROUP, GROUP),
            preferred_element_type=jnp.float32,
        )
        dk = (dk * factor).astype(jnp.bfloat16)
        dkown_ref[:, here] = dk[:own]
        for i, ref in enumerate(term_refs):
            ref[:held, here] = dk[own + i * held : own + (i + 1) * held]

    steps = [(head, pair) for head in range(count) for pair in range(pairs)]
    scores(*steps[0])
    inverse = softmax(*steps[0])
    for now, then in zip(steps, steps[1:] + [None]):
        if then:
            scores(*then)
        centre = attended(*now, inverse)
        if then:
            inverse = softmax(*then)
        score_grads(*now, centre)
        query_grads(*now)
        if now[1] + 1 == pairs:
            key_grads(now[0])
    for copy in stores:
        copy.wait()


def turn_kernel(do_ref, after_ref, out_ref):
    out_ref[0] = heads_down(do_ref, 0, GROUP).T


def scale_kernel(slots_all, total_ref, *refs):
    sources, refs = refs[: 3 * CHUNKS], refs[3 * CHUNKS :]
    outs, held, sem = refs[:3], refs[3:6], refs[6]
    weight = slots_all / total_ref[:1, :1]
    copies = []
    for chunk in range(CHUNKS):
        for i in range(3):
            source = sources[chunk * 3 + i]
            cols = pl.ds(chunk * source.shape[1], source.shape[1])
            scaled = source[...].astype(jnp.float32) * weight
            held[i][:, cols] = scaled.astype(jnp.bfloat16)
            copy = pltpu.make_async_copy(held[i].at[:, cols], outs[i].at[:, cols], sem.at[chunk, i])
            copy.start()
            copies.append(copy)
    for copy in copies:
        copy.wait()


def swap(x, axis, by):
    return lax.ppermute(x, axis, [(i, i ^ by) for i in range(lax.axis_size(axis))])


def sum_over(x, axis):
    by = 1
    while by < lax.axis_size(axis):
        x = x + swap(x, axis, by)
        by *= 2
    return x


def far_and_near(block):
    size = lax.axis_size("response")
    order = (3, 1) if size == 4 else range(1, size)
    return {m: swap(block, "response", m) for m in order}


def line_gather(block, sent):
    size = lax.axis_size("response")
    if size == 4:
        sent = {**sent, 2: swap(sent[3], "response", 1)}
    return [block] + [sent[m] for m in range(1, size)]


def line_reduce(slots, order):
    terms = [swap(slots[m], "response", m) for m in order]
    return functools.reduce(jnp.add, [term.astype(jnp.float32) for term in [slots[0]] + terms])


def own_columns(block, chunk, by):
    cols = block.shape[1] // (lax.axis_size("tensor") * CHUNKS)
    rank = lax.axis_index("tensor") ^ by
    return lax.dynamic_slice_in_dim(block, (rank * CHUNKS + chunk) * cols, cols, 1)


def tensor_gather(blocks, chunk):
    parts = lax.axis_size("tensor")
    pieces = []
    for m in range(parts):
        piece = jnp.concatenate([own_columns(block, chunk, m) for block in blocks], axis=0)
        pieces.append(piece if m == 0 else swap(piece, "tensor", m))
    rows = blocks[0].shape[0]
    return jnp.concatenate(
        [piece[i * rows : (i + 1) * rows] for i in range(len(blocks)) for piece in pieces], axis=0
    )


def tensor_spread(total, n_arrays):
    parts = lax.axis_size("tensor")
    rows = total.shape[0] // (n_arrays * parts)
    pieces = []
    for m in range(parts):
        piece = jnp.concatenate(
            [total[(i * parts + m) * rows : (i * parts + m + 1) * rows] for i in range(n_arrays)],
            axis=0,
        )
        pieces.append(piece if m == 0 else swap(piece, "tensor", m))
    return pieces


def whole_columns(chunk_pieces, array):
    parts = lax.axis_size("tensor")
    rank = lax.axis_index("tensor")
    rows = chunk_pieces[0][0].shape[0] // 2
    by_rank = [
        jnp.concatenate([pieces[m][array * rows : (array + 1) * rows] for pieces in chunk_pieces], axis=1)
        for m in range(parts)
    ]
    ordered = []
    for t in range(parts):
        column = by_rank[0]
        for m in range(1, parts):
            column = jnp.where(rank ^ m == t, by_rank[m], column)
        ordered.append(column)
    return jnp.concatenate(ordered, axis=1)


SMEM = pl.BlockSpec(memory_space=pltpu.SMEM)
HBM = pl.BlockSpec(memory_space=pltpu.HBM)
VMEM = pl.BlockSpec(memory_space=pltpu.VMEM)


def like(x):
    return jax.ShapeDtypeStruct(x.shape, x.dtype)


def turn(do, after):
    rows, heads = do.shape[0], do.shape[1] // (GROUP * HD)
    return pl.pallas_call(
        turn_kernel,
        grid=(heads,),
        in_specs=[pl.BlockSpec((rows, GROUP * HD), lambda j: (0, j)), HBM],
        out_specs=pl.BlockSpec((1, HD, GROUP * rows), lambda j: (j, 0, 0)),
        out_shape=jax.ShapeDtypeStruct((heads, HD, GROUP * rows), do.dtype),
        compiler_params=pltpu.CompilerParams(vmem_limit_bytes=SMALL_LIMIT),
        name="turn",
    )(do, after)


def attend(chunk, held, slots, length, q, turned, k, v, carried):
    rows = q.shape[0]
    count = k.shape[1] // (HD * CHUNKS)
    n_slots = len(slots)
    last = chunk + 1 == CHUNKS
    n_keys = rows + n_slots * held
    bf16 = jnp.bfloat16
    unit = 2 * n_keys * GROUP * rows * HD * count
    step_buffer = pltpu.VMEM((2, n_keys, PAIR * rows), jnp.float32)
    head_buffer = pltpu.VMEM((2, n_keys, GROUP * rows), bf16)
    wide = pltpu.VMEM((rows, count * GROUP * HD), bf16)
    down = pltpu.VMEM((count, n_keys, HD), bf16)
    across = pltpu.VMEM((count, HD, n_keys), bf16)
    scratch = [wide, step_buffer, step_buffer, head_buffer, head_buffer]
    scratch += [pltpu.VMEM((2, HD, GROUP * rows), bf16), down, across, down, across]
    scratch += [pltpu.SemaphoreType.DMA((count,))]
    part = lambda x: jax.ShapeDtypeStruct((x.shape[0], x.shape[1] // CHUNKS), bf16)
    terms = [jax.ShapeDtypeStruct((2 * held, count * HD), bf16)] * n_slots
    total = [jax.ShapeDtypeStruct((8, HD), jnp.float32)] * last
    return pl.pallas_call(
        functools.partial(attend_kernel, n_slots, count, chunk, held, 1.0 / math.sqrt(HD)),
        in_specs=[SMEM] + [VMEM] * (4 + n_slots) + [HBM] * last,
        out_specs=[HBM] + [VMEM] * (3 + n_slots + last),
        out_shape=[like(q), part(q), part(k), part(v)] + terms + total,
        input_output_aliases={5 + n_slots: 0} if last else {},
        scratch_shapes=scratch,
        compiler_params=pltpu.CompilerParams(vmem_limit_bytes=VMEM_LIMIT),
        cost_estimate=pl.CostEstimate(
            flops=24 * unit,
            bytes_accessed=8 * rows * GROUP * HD * count,
            transcendentals=count * n_keys * GROUP * rows,
        ),
        name=f"attend_{chunk}",
    )(length, q, turned, k, v, *slots, *carried)


def scale_all(slots_all, total, chunk_grads, shapes):
    flat = [grad for grads in chunk_grads for grad in grads]
    return pl.pallas_call(
        functools.partial(scale_kernel, slots_all),
        in_specs=[VMEM] * (1 + len(flat)),
        out_specs=[HBM] * len(shapes),
        out_shape=shapes,
        scratch_shapes=[pltpu.VMEM(x.shape, x.dtype) for x in shapes]
        + [pltpu.SemaphoreType.DMA((CHUNKS, len(shapes)))],
        compiler_params=pltpu.CompilerParams(vmem_limit_bytes=SMALL_LIMIT),
        cost_estimate=pl.CostEstimate(
            flops=sum(x.size for x in shapes),
            bytes_accessed=sum(4 * x.size for x in shapes),
            transcendentals=0,
        ),
        name="scale",
    )(total, *flat)


def body(queries, keys, values, prefix_keys, prefix_values, lengths, out_grad):
    q, k, v, do = queries[0], keys[0], values[0], out_grad[0]
    length = lengths[0]
    prefix = (prefix_keys[0], prefix_values[0])
    slots_all = q.shape[0] * lax.axis_size("prompt") * lax.axis_size("response")
    first, second = [tensor_gather(prefix, chunk) for chunk in range(CHUNKS)]
    held = first.shape[0] // 2
    sent = far_and_near(first)
    slots = line_gather(first, sent)
    length_rows = length[0].astype(second.dtype) + 0 * slots[-1][-EXTRA:]
    second = jnp.concatenate([second, length_rows], axis=0)
    sent = far_and_near(second)
    turned = turn(do, first)
    results = attend(0, held, slots, length, q, turned, k, v, [])
    if len(slots) == 4:
        far = sent[3]
        sent[3] = jnp.concatenate([far[:-EXTRA] + 0 * results[4], far[-EXTRA:]], axis=0)
    next_slots = line_gather(second, sent)
    next_results = attend(1, held, next_slots, length, q, turned, k, v, results[:1])
    terms, next_terms = results[4:], next_results[4:-1]
    behind = 0 * next_results[3][:1].astype(jnp.float32)
    farthest_first = list(range(len(terms) - 1, 0, -1))
    order = (2, 1, 3) if len(terms) == 4 else farthest_first
    sums = [line_reduce(terms, order) + behind, line_reduce(next_terms, farthest_first)]
    total = sum_over(next_results[-1] + 0 * sums[0][:8, :HD], "prompt")
    weight = jnp.tile(slots_all / total[:1], (1, prefix[0].shape[1] // HD))
    scaled = scale_all(
        slots_all, total + 0 * sums[1][:8, :HD], [results[1:4], next_results[1:4]], [like(q), like(k), like(v)]
    )
    both = jnp.concatenate([terms.astype(jnp.bfloat16) for terms in sums], axis=1)
    pieces = [tensor_spread(both, len(prefix))]
    grads = [whole_columns(pieces, array) for array in range(len(prefix))]
    grads = [(grad.astype(jnp.float32) * weight).astype(jnp.bfloat16) for grad in grads]
    return tuple(x[None] for x in (next_results[0], *scaled, *grads))


def solution(mesh):
    in_specs = (
        P("prompt", "response", "tensor"),
        P("prompt", "response", "tensor"),
        P("prompt", "response", "tensor"),
        P("prompt", ("response", "tensor"), None),
        P("prompt", ("response", "tensor"), None),
        P("prompt", "response"),
        P("prompt", "response", "tensor"),
    )
    out_specs = (
        P("prompt", "response", "tensor"),
        P("prompt", "response", "tensor"),
        P("prompt", "response", "tensor"),
        P("prompt", "response", "tensor"),
        P("prompt", ("response", "tensor"), None),
        P("prompt", ("response", "tensor"), None),
    )
    return jax.shard_map(body, mesh=mesh, in_specs=in_specs, out_specs=out_specs, check_vma=False)
```

```python
import functools
import math

import jax
import jax.numpy as jnp
from jax import lax
from jax.experimental import pallas as pl
from jax.experimental.pallas import tpu as pltpu
from jax.sharding import PartitionSpec as P

HD = 128
GROUP = 8
PAIR = 2
CHUNKS = 2
EXTRA = 16
STEP = 64
VMEM_LIMIT = 40 * 1024 * 1024
SMALL_LIMIT = 8 * 1024 * 1024
NT = (((1,), (1,)), ((), ()))


def heads_down(ref, first, count):
    return jnp.concatenate(
        [ref[:, (first + i) * HD : (first + i + 1) * HD] for i in range(count)], axis=0
    )


def attend_kernel(pieces, count, chunk, held, factor, *refs):
    last = chunk + 1 == CHUNKS
    length_ref, q_ref, turned_ref, kown_ref, vown_ref = refs[:5]
    n_refs = sum(pieces)
    piece_refs, refs = refs[5 : 5 + n_refs], refs[5 + n_refs + last :]
    n_slots = len(pieces)
    out_hbm, dq_ref, dkown_ref, dvown_ref = refs[:4]
    term_refs, refs = refs[4 : 4 + n_slots], refs[4 + n_slots :]
    if last:
        total_ref, refs = refs[0], refs[1:]
        extra = piece_refs[0].shape[0] - EXTRA
        totals = [ref[extra : extra + 8, :HD].astype(jnp.float32) for ref in piece_refs]
        total_ref[...] = functools.reduce(jnp.add, totals)
    out_ref, s_ref, dp_ref, e_ref, ds_ref, dot_ref = refs[:6]
    keys_ref, keys_t_ref, values_ref, values_t_ref, out_sem = refs[6:]
    first = chunk * count
    rows = q_ref.shape[0]
    own = kown_ref.shape[0]
    n_keys = s_ref.shape[1]
    width = PAIR * rows
    pairs = GROUP // PAIR
    scale = factor * math.log2(math.e)

    def columns(head, size):
        return pl.ds(head * size, size)

    stores = []

    live = (lax.broadcasted_iota(jnp.int32, (1, width), 1) % rows) < length_ref[0]

    sources = [
        ref.at[at : at + 2 * held]
        for ref in piece_refs
        for at in range(0, ref.shape[0] - 2 * held + 1, 2 * held)
    ]
    parts = len(sources) // n_slots

    def assemble(head, own_ref, start, wide_ref, tall_ref):
        here = slice(head * HD, (head + 1) * HD)
        wide_ref[head, :own] = own_ref[:, (first + head) * HD : (first + head + 1) * HD]
        for i, ref in enumerate(sources):
            part = slice(own + i * held, own + (i + 1) * held)
            wide_ref[head, part] = ref[start : start + held, here]
        tall_ref[head] = wide_ref[head].T

    def place(head, pair):
        return slice(pair * width, (pair + 1) * width)

    def scores(head, pair):
        if pair == 0:
            assemble(head, kown_ref, 0, keys_ref, keys_t_ref)
        s_ref[pair % 2] = lax.dot_general(
            keys_ref[head],
            heads_down(q_ref, (first + head) * GROUP + pair * PAIR, PAIR),
            NT,
            preferred_element_type=jnp.float32,
        )

    def softmax(head, pair):
        here = s_ref.at[pair % 2]
        cols = place(head, pair)
        fold = lambda x: x.reshape(x.shape[0] // 8, 8, width)
        top = jnp.full((8, width), -1e30, jnp.float32)
        for at in range(0, n_keys, STEP):
            x = here[at : at + STEP]
            if at < own:
                key_pos = lax.broadcasted_iota(jnp.int32, x.shape, 0) + at
                row_pos = lax.broadcasted_iota(jnp.int32, x.shape, 1) % rows
                x = jnp.where(key_pos <= row_pos, x, -1e30)
                here[at : at + STEP] = x
            top = jnp.maximum(top, jnp.max(fold(x), axis=0))
        top = jnp.max(top, axis=0, keepdims=True) * scale
        top = jnp.broadcast_to(top, (8, width))
        total = jnp.zeros((8, width), jnp.float32)
        for at in range(0, n_keys, STEP):
            e = jnp.exp2(fold(here[at : at + STEP]) * scale - top)
            total = total + jnp.sum(e, axis=0)
            e_ref[head % 2, at : at + STEP, cols] = e.reshape(-1, width).astype(jnp.bfloat16)
        total = jnp.sum(total, axis=0, keepdims=True)
        inverse = jnp.where(live, 1.0 / total, 0.0)
        grad = turned_ref[first + head, :, cols].astype(jnp.float32) * inverse
        dot_ref[head % 2, :, cols] = grad.astype(jnp.bfloat16)
        return inverse

    def attended(head, pair, inverse):
        cols = place(head, pair)
        if pair == 0:
            assemble(head, vown_ref, held, values_ref, values_t_ref)
        grad = dot_ref[head % 2, :, cols]
        dp_ref[pair % 2] = jnp.dot(values_ref[head], grad, preferred_element_type=jnp.float32)
        out = jnp.dot(
            values_t_ref[head], e_ref[head % 2, :, cols], preferred_element_type=jnp.float32
        )
        out = out * inverse
        turned = out.astype(jnp.bfloat16).T
        for i in range(PAIR):
            at = head * GROUP + pair * PAIR + i
            out_ref[:, at * HD : (at + 1) * HD] = turned[i * rows : (i + 1) * rows]
        return jnp.sum(out * grad.astype(jnp.float32), axis=0, keepdims=True)

    def score_grads(head, pair, centre):
        cols = place(head, pair)
        here = dp_ref.at[pair % 2]
        centre = jnp.broadcast_to(centre, (STEP, width))
        for at in range(0, n_keys, STEP):
            e = e_ref[head % 2, at : at + STEP, cols].astype(jnp.float32)
            grad = e * (here[at : at + STEP] - centre)
            ds_ref[head % 2, at : at + STEP, cols] = grad.astype(jnp.bfloat16)

    def query_grads(head, pair):
        cols = place(head, pair)
        dq = jnp.dot(
            keys_t_ref[head], ds_ref[head % 2, :, cols], preferred_element_type=jnp.float32
        )
        turned = (dq * factor).astype(jnp.bfloat16).T
        for i in range(PAIR):
            at = head * GROUP + pair * PAIR + i
            dq_ref[:, at * HD : (at + 1) * HD] = turned[i * rows : (i + 1) * rows]

    def key_grads(head):
        copy = pltpu.make_async_copy(
            out_ref.at[:, columns(head, GROUP * HD)],
            out_hbm.at[:, columns(first + head, GROUP * HD)],
            out_sem.at[head],
        )
        copy.start()
        stores.append(copy)
        here = slice(head * HD, (head + 1) * HD)
        dv = lax.dot_general(
            e_ref[head % 2], dot_ref[head % 2], NT, preferred_element_type=jnp.float32
        ).astype(jnp.bfloat16)
        dvown_ref[:, here] = dv[:own]
        for i in range(len(sources)):
            row = i % parts * 2 * held + held
            term = dv[own + i * held : own + (i + 1) * held]
            term_refs[i // parts][row : row + held, here] = term
        dk = jnp.dot(
            ds_ref[head % 2],
            heads_down(q_ref, (first + head) * GROUP, GROUP),
            preferred_element_type=jnp.float32,
        )
        dk = (dk * factor).astype(jnp.bfloat16)
        dkown_ref[:, here] = dk[:own]
        for i in range(len(sources)):
            row = i % parts * 2 * held
            term = dk[own + i * held : own + (i + 1) * held]
            term_refs[i // parts][row : row + held, here] = term

    steps = [(head, pair) for head in range(count) for pair in range(pairs)]
    scores(*steps[0])
    inverse = softmax(*steps[0])
    for now, then in zip(steps, steps[1:] + [None]):
        if then:
            scores(*then)
        centre = attended(*now, inverse)
        if then:
            inverse = softmax(*then)
        score_grads(*now, centre)
        query_grads(*now)
        if now[1] + 1 == pairs:
            key_grads(now[0])
    for copy in stores:
        copy.wait()


def turn_kernel(do_ref, after_ref, out_ref):
    out_ref[0] = heads_down(do_ref, 0, GROUP).T


def scale_kernel(slots_all, total_ref, *refs):
    sources, refs = refs[: 3 * CHUNKS], refs[3 * CHUNKS :]
    outs, held, sem = refs[:3], refs[3:6], refs[6]
    weight = slots_all / total_ref[:1, :1]
    copies = []
    for chunk in range(CHUNKS):
        for i in range(3):
            source = sources[chunk * 3 + i]
            cols = pl.ds(chunk * source.shape[1], source.shape[1])
            scaled = source[...].astype(jnp.float32) * weight
            held[i][:, cols] = scaled.astype(jnp.bfloat16)
            copy = pltpu.make_async_copy(held[i].at[:, cols], outs[i].at[:, cols], sem.at[chunk, i])
            copy.start()
            copies.append(copy)
    for copy in copies:
        copy.wait()


def swap(x, axis, by):
    return lax.ppermute(x, axis, [(i, i ^ by) for i in range(lax.axis_size(axis))])


def sum_over(x, axis):
    by = 1
    while by < lax.axis_size(axis):
        x = x + swap(x, axis, by)
        by *= 2
    return x


def line_reduce(slots, order):
    terms = [swap(slots[m], "response", m) for m in order]
    return functools.reduce(jnp.add, [term.astype(jnp.float32) for term in [slots[0]] + terms])


def own_columns(block, chunk, by):
    cols = block.shape[1] // (lax.axis_size("tensor") * CHUNKS)
    rank = lax.axis_index("tensor") ^ by
    return lax.dynamic_slice_in_dim(block, (rank * CHUNKS + chunk) * cols, cols, 1)


def tensor_gather(blocks, chunk):
    pieces = []
    for m in range(lax.axis_size("tensor")):
        piece = jnp.concatenate([own_columns(block, chunk, m) for block in blocks], axis=0)
        pieces.append(piece if m == 0 else swap(piece, "tensor", m))
    return pieces


def tensor_spread(total):
    pieces = jnp.split(total, lax.axis_size("tensor"), axis=0)
    return [piece if m == 0 else swap(piece, "tensor", m) for m, piece in enumerate(pieces)]


def whole_columns(chunk_pieces, array):
    parts = lax.axis_size("tensor")
    rank = lax.axis_index("tensor")
    rows = chunk_pieces[0][0].shape[0] // 2
    by_rank = [
        jnp.concatenate([pieces[m][array * rows : (array + 1) * rows] for pieces in chunk_pieces], axis=1)
        for m in range(parts)
    ]
    ordered = []
    for t in range(parts):
        column = by_rank[0]
        for m in range(1, parts):
            column = jnp.where(rank ^ m == t, by_rank[m], column)
        ordered.append(column)
    return jnp.concatenate(ordered, axis=1)


SMEM = pl.BlockSpec(memory_space=pltpu.SMEM)
HBM = pl.BlockSpec(memory_space=pltpu.HBM)
VMEM = pl.BlockSpec(memory_space=pltpu.VMEM)


def like(x):
    return jax.ShapeDtypeStruct(x.shape, x.dtype)


def turn(do, after):
    rows, heads = do.shape[0], do.shape[1] // (GROUP * HD)
    return pl.pallas_call(
        turn_kernel,
        grid=(heads,),
        in_specs=[pl.BlockSpec((rows, GROUP * HD), lambda j: (0, j)), HBM],
        out_specs=pl.BlockSpec((1, HD, GROUP * rows), lambda j: (j, 0, 0)),
        out_shape=jax.ShapeDtypeStruct((heads, HD, GROUP * rows), do.dtype),
        compiler_params=pltpu.CompilerParams(vmem_limit_bytes=SMALL_LIMIT),
        name="turn",
    )(do, after)


def attend(chunk, held, slots, length, q, turned, k, v, carried):
    rows = q.shape[0]
    count = k.shape[1] // (HD * CHUNKS)
    n_slots = len(slots)
    pieces = [piece for slot in slots for piece in slot]
    n_refs = len(pieces)
    last = chunk + 1 == CHUNKS
    parts = lax.axis_size("tensor")
    n_keys = rows + n_slots * parts * held
    bf16 = jnp.bfloat16
    unit = 2 * n_keys * GROUP * rows * HD * count
    step_buffer = pltpu.VMEM((2, n_keys, PAIR * rows), jnp.float32)
    head_buffer = pltpu.VMEM((2, n_keys, GROUP * rows), bf16)
    wide = pltpu.VMEM((rows, count * GROUP * HD), bf16)
    down = pltpu.VMEM((count, n_keys, HD), bf16)
    across = pltpu.VMEM((count, HD, n_keys), bf16)
    scratch = [wide, step_buffer, step_buffer, head_buffer, head_buffer]
    scratch += [pltpu.VMEM((2, HD, GROUP * rows), bf16), down, across, down, across]
    scratch += [pltpu.SemaphoreType.DMA((count,))]
    part = lambda x: jax.ShapeDtypeStruct((x.shape[0], x.shape[1] // CHUNKS), bf16)
    terms = [jax.ShapeDtypeStruct((parts * 2 * held, count * HD), bf16)] * n_slots
    total = [jax.ShapeDtypeStruct((8, HD), jnp.float32)] * last
    return pl.pallas_call(
        functools.partial(
            attend_kernel, [len(slot) for slot in slots], count, chunk, held, 1.0 / math.sqrt(HD)
        ),
        in_specs=[SMEM] + [VMEM] * (4 + n_refs) + [HBM] * last,
        out_specs=[HBM] + [VMEM] * (3 + n_slots + last),
        out_shape=[like(q), part(q), part(k), part(v)] + terms + total,
        input_output_aliases={5 + n_refs: 0} if last else {},
        scratch_shapes=scratch,
        compiler_params=pltpu.CompilerParams(vmem_limit_bytes=VMEM_LIMIT),
        cost_estimate=pl.CostEstimate(
            flops=24 * unit,
            bytes_accessed=8 * rows * GROUP * HD * count,
            transcendentals=count * n_keys * GROUP * rows,
        ),
        name=f"attend_{chunk}",
    )(length, q, turned, k, v, *pieces, *carried)


def scale_all(slots_all, total, chunk_grads, shapes):
    flat = [grad for grads in chunk_grads for grad in grads]
    return pl.pallas_call(
        functools.partial(scale_kernel, slots_all),
        in_specs=[VMEM] * (1 + len(flat)),
        out_specs=[HBM] * len(shapes),
        out_shape=shapes,
        scratch_shapes=[pltpu.VMEM(x.shape, x.dtype) for x in shapes]
        + [pltpu.SemaphoreType.DMA((CHUNKS, len(shapes)))],
        compiler_params=pltpu.CompilerParams(vmem_limit_bytes=SMALL_LIMIT),
        cost_estimate=pl.CostEstimate(
            flops=sum(x.size for x in shapes),
            bytes_accessed=sum(4 * x.size for x in shapes),
            transcendentals=0,
        ),
        name="scale",
    )(total, *flat)


def body(queries, keys, values, prefix_keys, prefix_values, lengths, out_grad):
    q, k, v, do = queries[0], keys[0], values[0], out_grad[0]
    length = lengths[0]
    prefix = (prefix_keys[0], prefix_values[0])
    slots_all = q.shape[0] * lax.axis_size("prompt") * lax.axis_size("response")
    first, second = [tensor_gather(prefix, chunk) for chunk in range(CHUNKS)]
    held = prefix[0].shape[0]
    size = lax.axis_size("response")
    line = size == 4
    block = jnp.concatenate(first, axis=0)
    if line:
        far = [swap(piece, "response", 3) for piece in first]
        near = swap(block, "response", 1)
        slots = [first, [near], [swap(jnp.concatenate(far, axis=0), "response", 1)], far]
    else:
        slots = [first] + [[swap(block, "response", m)] for m in range(1, size)]
    length_rows = length[0].astype(block.dtype) + 0 * slots[-1][-1][-EXTRA:]
    second = jnp.concatenate([*second, length_rows], axis=0)
    order = (3, 1) if line else range(1, size)
    sent = {m: swap(second, "response", m) for m in order}
    turned = turn(do, block)
    results = attend(0, held, slots, length, q, turned, k, v, [])
    if line:
        far = jnp.concatenate([sent[3][:-EXTRA] + 0 * results[4], sent[3][-EXTRA:]], axis=0)
        sent[2] = swap(far, "response", 1)
    next_slots = [[second]] + [[sent[m]] for m in range(1, size)]
    next_results = attend(1, held, next_slots, length, q, turned, k, v, results[:1])
    terms, next_terms = results[4:], next_results[4:-1]
    behind = 0 * next_results[3][:1].astype(jnp.float32)
    farthest_first = list(range(len(terms) - 1, 0, -1))
    order = (2, 1, 3) if len(terms) == 4 else farthest_first
    sums = [line_reduce(terms, order) + behind, line_reduce(next_terms, farthest_first)]
    total = sum_over(next_results[-1] + 0 * sums[0][:8, :HD], "prompt")
    weight = jnp.tile(slots_all / total[:1], (1, prefix[0].shape[1] // HD))
    scaled = scale_all(
        slots_all, total + 0 * sums[1][:8, :HD], [results[1:4], next_results[1:4]], [like(q), like(k), like(v)]
    )
    both = jnp.concatenate([terms.astype(jnp.bfloat16) for terms in sums], axis=1)
    pieces = [tensor_spread(both)]
    grads = [whole_columns(pieces, array) for array in range(len(prefix))]
    grads = [(grad.astype(jnp.float32) * weight).astype(jnp.bfloat16) for grad in grads]
    return tuple(x[None] for x in (next_results[0], *scaled, *grads))


def solution(mesh):
    in_specs = (
        P("prompt", "response", "tensor"),
        P("prompt", "response", "tensor"),
        P("prompt", "response", "tensor"),
        P("prompt", ("response", "tensor"), None),
        P("prompt", ("response", "tensor"), None),
        P("prompt", "response"),
        P("prompt", "response", "tensor"),
    )
    out_specs = (
        P("prompt", "response", "tensor"),
        P("prompt", "response", "tensor"),
        P("prompt", "response", "tensor"),
        P("prompt", "response", "tensor"),
        P("prompt", ("response", "tensor"), None),
        P("prompt", ("response", "tensor"), None),
    )
    return jax.shard_map(body, mesh=mesh, in_specs=in_specs, out_specs=out_specs, check_vma=False)
```

```python
import functools
import math

import jax
import jax.numpy as jnp
from jax import lax
from jax.experimental import pallas as pl
from jax.experimental.pallas import tpu as pltpu
from jax.sharding import PartitionSpec as P

HD = 128
GROUP = 8
PAIR = 2
CHUNKS = 2
EXTRA = 16
STEP = 64
VMEM_LIMIT = 40 * 1024 * 1024
SMALL_LIMIT = 8 * 1024 * 1024
NT = (((1,), (1,)), ((), ()))


def heads_down(ref, first, count):
    return jnp.concatenate(
        [ref[:, (first + i) * HD : (first + i + 1) * HD] for i in range(count)], axis=0
    )


def attend_kernel(n_slots, count, chunk, held, factor, *refs):
    last = chunk + 1 == CHUNKS
    length_ref, q_ref, turned_ref, kown_ref, vown_ref = refs[:5]
    slot_refs, refs = refs[5 : 5 + n_slots], refs[5 + n_slots + last :]
    out_hbm, dq_ref, dkown_ref, dvown_ref = refs[:4]
    term_refs, refs = refs[4 : 4 + n_slots], refs[4 + n_slots :]
    if last:
        total_ref, refs = refs[0], refs[1:]
        totals = [ref[2 * held : 2 * held + 8, :HD].astype(jnp.float32) for ref in slot_refs]
        total_ref[...] = functools.reduce(jnp.add, totals)
    out_ref, s_ref, dp_ref, e_ref, ds_ref, dot_ref = refs[:6]
    keys_ref, keys_t_ref, values_ref, values_t_ref, out_sem = refs[6:]
    first = chunk * count
    rows = q_ref.shape[0]
    own = kown_ref.shape[0]
    n_keys = s_ref.shape[1]
    width = PAIR * rows
    pairs = GROUP // PAIR
    scale = factor * math.log2(math.e)

    def columns(head, size):
        return pl.ds(head * size, size)

    stores = []

    live = (lax.broadcasted_iota(jnp.int32, (1, width), 1) % rows) < length_ref[0]

    def assemble(head, own_ref, slot_start, wide_ref, tall_ref):
        here = slice(head * HD, (head + 1) * HD)
        wide_ref[head, :own] = own_ref[:, (first + head) * HD : (first + head + 1) * HD]
        for i, ref in enumerate(slot_refs):
            part = slice(own + i * held, own + (i + 1) * held)
            wide_ref[head, part] = ref[slot_start : slot_start + held, here]
        tall_ref[head] = wide_ref[head].T

    def place(head, pair):
        return slice(pair * width, (pair + 1) * width)

    def scores(head, pair):
        if pair == 0:
            assemble(head, kown_ref, 0, keys_ref, keys_t_ref)
        s_ref[pair % 2] = lax.dot_general(
            keys_ref[head],
            heads_down(q_ref, (first + head) * GROUP + pair * PAIR, PAIR),
            NT,
            preferred_element_type=jnp.float32,
        )

    def softmax(head, pair):
        here = s_ref.at[pair % 2]
        cols = place(head, pair)
        fold = lambda x: x.reshape(x.shape[0] // 8, 8, width)
        top = jnp.full((8, width), -1e30, jnp.float32)
        for at in range(0, n_keys, STEP):
            x = here[at : at + STEP]
            if at < own:
                key_pos = lax.broadcasted_iota(jnp.int32, x.shape, 0) + at
                row_pos = lax.broadcasted_iota(jnp.int32, x.shape, 1) % rows
                x = jnp.where(key_pos <= row_pos, x, -1e30)
                here[at : at + STEP] = x
            top = jnp.maximum(top, jnp.max(fold(x), axis=0))
        top = jnp.max(top, axis=0, keepdims=True) * scale
        top = jnp.broadcast_to(top, (8, width))
        total = jnp.zeros((8, width), jnp.float32)
        for at in range(0, n_keys, STEP):
            e = jnp.exp2(fold(here[at : at + STEP]) * scale - top)
            total = total + jnp.sum(e, axis=0)
            e_ref[head % 2, at : at + STEP, cols] = e.reshape(-1, width).astype(jnp.bfloat16)
        total = jnp.sum(total, axis=0, keepdims=True)
        inverse = jnp.where(live, 1.0 / total, 0.0)
        grad = turned_ref[first + head, :, cols].astype(jnp.float32) * inverse
        dot_ref[head % 2, :, cols] = grad.astype(jnp.bfloat16)
        return inverse

    def attended(head, pair, inverse):
        cols = place(head, pair)
        if pair == 0:
            assemble(head, vown_ref, held, values_ref, values_t_ref)
        grad = dot_ref[head % 2, :, cols]
        dp_ref[pair % 2] = jnp.dot(values_ref[head], grad, preferred_element_type=jnp.float32)
        out = jnp.dot(
            values_t_ref[head], e_ref[head % 2, :, cols], preferred_element_type=jnp.float32
        )
        out = out * inverse
        turned = out.astype(jnp.bfloat16).T
        for i in range(PAIR):
            at = head * GROUP + pair * PAIR + i
            out_ref[:, at * HD : (at + 1) * HD] = turned[i * rows : (i + 1) * rows]
        return jnp.sum(out * grad.astype(jnp.float32), axis=0, keepdims=True)

    def score_grads(head, pair, centre):
        cols = place(head, pair)
        here = dp_ref.at[pair % 2]
        centre = jnp.broadcast_to(centre, (STEP, width))
        for at in range(0, n_keys, STEP):
            e = e_ref[head % 2, at : at + STEP, cols].astype(jnp.float32)
            grad = e * (here[at : at + STEP] - centre)
            ds_ref[head % 2, at : at + STEP, cols] = grad.astype(jnp.bfloat16)

    def query_grads(head, pair):
        cols = place(head, pair)
        dq = jnp.dot(
            keys_t_ref[head], ds_ref[head % 2, :, cols], preferred_element_type=jnp.float32
        )
        turned = (dq * factor).astype(jnp.bfloat16).T
        for i in range(PAIR):
            at = head * GROUP + pair * PAIR + i
            dq_ref[:, at * HD : (at + 1) * HD] = turned[i * rows : (i + 1) * rows]

    def key_grads(head):
        copy = pltpu.make_async_copy(
            out_ref.at[:, columns(head, GROUP * HD)],
            out_hbm.at[:, columns(first + head, GROUP * HD)],
            out_sem.at[head],
        )
        copy.start()
        stores.append(copy)
        here = slice(head * HD, (head + 1) * HD)
        dv = lax.dot_general(
            e_ref[head % 2], dot_ref[head % 2], NT, preferred_element_type=jnp.float32
        ).astype(jnp.bfloat16)
        dvown_ref[:, here] = dv[:own]
        for i, ref in enumerate(term_refs):
            ref[held:, here] = dv[own + i * held : own + (i + 1) * held]
        dk = jnp.dot(
            ds_ref[head % 2],
            heads_down(q_ref, (first + head) * GROUP, GROUP),
            preferred_element_type=jnp.float32,
        )
        dk = (dk * factor).astype(jnp.bfloat16)
        dkown_ref[:, here] = dk[:own]
        for i, ref in enumerate(term_refs):
            ref[:held, here] = dk[own + i * held : own + (i + 1) * held]

    steps = [(head, pair) for head in range(count) for pair in range(pairs)]
    scores(*steps[0])
    inverse = softmax(*steps[0])
    for now, then in zip(steps, steps[1:] + [None]):
        if then:
            scores(*then)
        centre = attended(*now, inverse)
        if then:
            inverse = softmax(*then)
        score_grads(*now, centre)
        query_grads(*now)
        if now[1] + 1 == pairs:
            key_grads(now[0])
    for copy in stores:
        copy.wait()


def turn_kernel(do_ref, after_ref, out_ref):
    out_ref[0] = heads_down(do_ref, 0, GROUP).T


def scale_kernel(slots_all, total_ref, *refs):
    sources, refs = refs[: 3 * CHUNKS], refs[3 * CHUNKS :]
    outs, held, sem = refs[:3], refs[3:6], refs[6]
    weight = slots_all / total_ref[:1, :1]
    copies = []
    for chunk in range(CHUNKS):
        for i in range(3):
            source = sources[chunk * 3 + i]
            cols = pl.ds(chunk * source.shape[1], source.shape[1])
            scaled = source[...].astype(jnp.float32) * weight
            held[i][:, cols] = scaled.astype(jnp.bfloat16)
            copy = pltpu.make_async_copy(held[i].at[:, cols], outs[i].at[:, cols], sem.at[chunk, i])
            copy.start()
            copies.append(copy)
    for copy in copies:
        copy.wait()


def swap(x, axis, by):
    return lax.ppermute(x, axis, [(i, i ^ by) for i in range(lax.axis_size(axis))])


def sum_over(x, axis):
    by = 1
    while by < lax.axis_size(axis):
        x = x + swap(x, axis, by)
        by *= 2
    return x


def far_and_near(block):
    size = lax.axis_size("response")
    order = (3, 1) if size == 4 else range(1, size)
    return {m: swap(block, "response", m) for m in order}


def line_gather(block, sent):
    size = lax.axis_size("response")
    if size == 4:
        sent = {**sent, 2: swap(sent[3], "response", 1)}
    return [block] + [sent[m] for m in range(1, size)]


def far_sum(slots, order):
    terms = [slots[0]] + [swap(slots[m], "response", m) for m in order]
    return functools.reduce(jnp.add, [term.astype(jnp.float32) for term in terms])


def own_columns(block, chunk, by):
    cols = block.shape[1] // (lax.axis_size("tensor") * CHUNKS)
    rank = lax.axis_index("tensor") ^ by
    return lax.dynamic_slice_in_dim(block, (rank * CHUNKS + chunk) * cols, cols, 1)


def tensor_gather(blocks, chunk):
    parts = lax.axis_size("tensor")
    pieces = []
    for m in range(parts):
        piece = jnp.concatenate([own_columns(block, chunk, m) for block in blocks], axis=0)
        pieces.append(piece if m == 0 else swap(piece, "tensor", m))
    rows = blocks[0].shape[0]
    return jnp.concatenate(
        [piece[i * rows : (i + 1) * rows] for i in range(len(blocks)) for piece in pieces], axis=0
    )


def tensor_spread(total, n_arrays):
    parts = lax.axis_size("tensor")
    rows = total.shape[0] // (n_arrays * parts)
    pieces = []
    for m in range(parts):
        piece = jnp.concatenate(
            [total[(i * parts + m) * rows : (i * parts + m + 1) * rows] for i in range(n_arrays)],
            axis=0,
        )
        pieces.append(piece if m == 0 else swap(piece, "tensor", m))
    return pieces


def whole_columns(chunk_pieces, array):
    parts = lax.axis_size("tensor")
    rank = lax.axis_index("tensor")
    rows = chunk_pieces[0][0].shape[0] // 2
    by_rank = [
        jnp.concatenate([pieces[m][array * rows : (array + 1) * rows] for pieces in chunk_pieces], axis=1)
        for m in range(parts)
    ]
    ordered = []
    for t in range(parts):
        column = by_rank[0]
        for m in range(1, parts):
            column = jnp.where(rank ^ m == t, by_rank[m], column)
        ordered.append(column)
    return jnp.concatenate(ordered, axis=1)


SMEM = pl.BlockSpec(memory_space=pltpu.SMEM)
HBM = pl.BlockSpec(memory_space=pltpu.HBM)
VMEM = pl.BlockSpec(memory_space=pltpu.VMEM)


def like(x):
    return jax.ShapeDtypeStruct(x.shape, x.dtype)


def turn(do, after):
    rows, heads = do.shape[0], do.shape[1] // (GROUP * HD)
    return pl.pallas_call(
        turn_kernel,
        grid=(heads,),
        in_specs=[pl.BlockSpec((rows, GROUP * HD), lambda j: (0, j)), HBM],
        out_specs=pl.BlockSpec((1, HD, GROUP * rows), lambda j: (j, 0, 0)),
        out_shape=jax.ShapeDtypeStruct((heads, HD, GROUP * rows), do.dtype),
        compiler_params=pltpu.CompilerParams(vmem_limit_bytes=SMALL_LIMIT),
        name="turn",
    )(do, after)


def attend(chunk, held, slots, length, q, turned, k, v, carried):
    rows = q.shape[0]
    count = k.shape[1] // (HD * CHUNKS)
    n_slots = len(slots)
    last = chunk + 1 == CHUNKS
    n_keys = rows + n_slots * held
    bf16 = jnp.bfloat16
    unit = 2 * n_keys * GROUP * rows * HD * count
    step_buffer = pltpu.VMEM((2, n_keys, PAIR * rows), jnp.float32)
    head_buffer = pltpu.VMEM((2, n_keys, GROUP * rows), bf16)
    wide = pltpu.VMEM((rows, count * GROUP * HD), bf16)
    down = pltpu.VMEM((count, n_keys, HD), bf16)
    across = pltpu.VMEM((count, HD, n_keys), bf16)
    scratch = [wide, step_buffer, step_buffer, head_buffer, head_buffer]
    scratch += [pltpu.VMEM((2, HD, GROUP * rows), bf16), down, across, down, across]
    scratch += [pltpu.SemaphoreType.DMA((count,))]
    part = lambda x: jax.ShapeDtypeStruct((x.shape[0], x.shape[1] // CHUNKS), bf16)
    terms = [jax.ShapeDtypeStruct((2 * held, count * HD), bf16)] * n_slots
    total = [jax.ShapeDtypeStruct((8, HD), jnp.float32)] * last
    return pl.pallas_call(
        functools.partial(attend_kernel, n_slots, count, chunk, held, 1.0 / math.sqrt(HD)),
        in_specs=[SMEM] + [VMEM] * (4 + n_slots) + [HBM] * last,
        out_specs=[HBM] + [VMEM] * (3 + n_slots + last),
        out_shape=[like(q), part(q), part(k), part(v)] + terms + total,
        input_output_aliases={5 + n_slots: 0} if last else {},
        scratch_shapes=scratch,
        compiler_params=pltpu.CompilerParams(vmem_limit_bytes=VMEM_LIMIT),
        cost_estimate=pl.CostEstimate(
            flops=24 * unit,
            bytes_accessed=8 * rows * GROUP * HD * count,
            transcendentals=count * n_keys * GROUP * rows,
        ),
        name=f"attend_{chunk}",
    )(length, q, turned, k, v, *slots, *carried)


def scale_all(slots_all, total, chunk_grads, shapes):
    flat = [grad for grads in chunk_grads for grad in grads]
    return pl.pallas_call(
        functools.partial(scale_kernel, slots_all),
        in_specs=[VMEM] * (1 + len(flat)),
        out_specs=[HBM] * len(shapes),
        out_shape=shapes,
        scratch_shapes=[pltpu.VMEM(x.shape, x.dtype) for x in shapes]
        + [pltpu.SemaphoreType.DMA((CHUNKS, len(shapes)))],
        compiler_params=pltpu.CompilerParams(vmem_limit_bytes=SMALL_LIMIT),
        cost_estimate=pl.CostEstimate(
            flops=sum(x.size for x in shapes),
            bytes_accessed=sum(4 * x.size for x in shapes),
            transcendentals=0,
        ),
        name="scale",
    )(total, *flat)


def body(queries, keys, values, prefix_keys, prefix_values, lengths, out_grad):
    q, k, v, do = queries[0], keys[0], values[0], out_grad[0]
    length = lengths[0]
    prefix = (prefix_keys[0], prefix_values[0])
    slots_all = q.shape[0] * lax.axis_size("prompt") * lax.axis_size("response")
    first, second = [tensor_gather(prefix, chunk) for chunk in range(CHUNKS)]
    held = first.shape[0] // 2
    sent = far_and_near(first)
    slots = line_gather(first, sent)
    length_rows = length[0].astype(second.dtype) + 0 * slots[-1][-EXTRA:]
    second = jnp.concatenate([second, length_rows], axis=0)
    sent = far_and_near(second)
    turned = turn(do, first)
    results = attend(0, held, slots, length, q, turned, k, v, [])
    if len(slots) == 4:
        far = sent[3]
        sent[3] = jnp.concatenate([far[:-EXTRA] + 0 * results[4], far[-EXTRA:]], axis=0)
    next_slots = line_gather(second, sent)
    next_results = attend(1, held, next_slots, length, q, turned, k, v, results[:1])
    terms, next_terms = results[4:], next_results[4:-1]
    behind = 0 * next_results[3][:1].astype(jnp.float32)
    order = list(range(len(terms) - 1, 1, -1))
    sums = [far_sum(terms, order) + behind, far_sum(next_terms, order)]
    nearest = jnp.concatenate([terms[1], next_terms[1]], axis=1)
    near = swap(nearest, "response", 1)
    total = sum_over(next_results[-1] + 0 * nearest[:8, :HD].astype(jnp.float32), "prompt")
    weight = jnp.tile(slots_all / total[:1], (1, prefix[0].shape[1] // HD))
    scaled = scale_all(
        slots_all, total + 0 * sums[1][:8, :HD], [results[1:4], next_results[1:4]], [like(q), like(k), like(v)]
    )
    both = jnp.concatenate(sums, axis=1) + near.astype(jnp.float32)
    both = both.astype(jnp.bfloat16)
    pieces = [tensor_spread(both, len(prefix))]
    grads = [whole_columns(pieces, array) for array in range(len(prefix))]
    grads = [(grad.astype(jnp.float32) * weight).astype(jnp.bfloat16) for grad in grads]
    return tuple(x[None] for x in (next_results[0], *scaled, *grads))


def solution(mesh):
    in_specs = (
        P("prompt", "response", "tensor"),
        P("prompt", "response", "tensor"),
        P("prompt", "response", "tensor"),
        P("prompt", ("response", "tensor"), None),
        P("prompt", ("response", "tensor"), None),
        P("prompt", "response"),
        P("prompt", "response", "tensor"),
    )
    out_specs = (
        P("prompt", "response", "tensor"),
        P("prompt", "response", "tensor"),
        P("prompt", "response", "tensor"),
        P("prompt", "response", "tensor"),
        P("prompt", ("response", "tensor"), None),
        P("prompt", ("response", "tensor"), None),
    )
    return jax.shard_map(body, mesh=mesh, in_specs=in_specs, out_specs=out_specs, check_vma=False)
```

```python
import functools
import math

import jax
import jax.numpy as jnp
from jax import lax
from jax.experimental import pallas as pl
from jax.experimental.pallas import tpu as pltpu
from jax.sharding import PartitionSpec as P

HD = 128
GROUP = 8
PAIR = 2
CHUNKS = 2
EXTRA = 16
STEP = 64
SMALL_LIMIT = 8 * 1024 * 1024
NT = (((1,), (1,)), ((), ()))


def heads_down(ref, first, count):
    return jnp.concatenate(
        [ref[:, (first + i) * HD : (first + i + 1) * HD] for i in range(count)], axis=0
    )


def attend_kernel(n_slots, count, chunk, held, factor, *refs):
    last = chunk + 1 == CHUNKS
    length_ref, q_ref, turned_ref, kown_ref, vown_ref = refs[:5]
    slot_refs, refs = refs[5 : 5 + n_slots], refs[5 + n_slots + last :]
    out_hbm, dq_ref, dkown_ref, dvown_ref = refs[:4]
    term_refs, refs = refs[4 : 4 + n_slots], refs[4 + n_slots :]
    if last:
        total_ref, refs = refs[0], refs[1:]
        totals = [ref[2 * held : 2 * held + 8, :HD].astype(jnp.float32) for ref in slot_refs]
        total_ref[...] = functools.reduce(jnp.add, totals)
    out_ref, s_ref, dp_ref, e_ref, ds_ref, dot_ref = refs[:6]
    keys_ref, keys_t_ref, values_ref, values_t_ref, out_sem = refs[6:]
    first = chunk * count
    rows = q_ref.shape[0]
    own = kown_ref.shape[0]
    n_keys = s_ref.shape[1]
    width = PAIR * rows
    pairs = GROUP // PAIR
    scale = factor * math.log2(math.e)

    def columns(head, size):
        return pl.ds(head * size, size)

    stores = []

    live = (lax.broadcasted_iota(jnp.int32, (1, width), 1) % rows) < length_ref[0]

    def assemble(head, own_ref, slot_start, wide_ref, tall_ref):
        here = slice(head * HD, (head + 1) * HD)
        wide_ref[head, :own] = own_ref[:, (first + head) * HD : (first + head + 1) * HD]
        for i, ref in enumerate(slot_refs):
            part = slice(own + i * held, own + (i + 1) * held)
            wide_ref[head, part] = ref[slot_start : slot_start + held, here]
        tall_ref[head] = wide_ref[head].T

    def place(head, pair):
        return slice(pair * width, (pair + 1) * width)

    def scores(head, pair):
        if pair == 0:
            assemble(head, kown_ref, 0, keys_ref, keys_t_ref)
        s_ref[pair % 2] = lax.dot_general(
            keys_ref[head],
            heads_down(q_ref, (first + head) * GROUP + pair * PAIR, PAIR),
            NT,
            preferred_element_type=jnp.float32,
        )

    def softmax(head, pair):
        here = s_ref.at[pair % 2]
        cols = place(head, pair)
        fold = lambda x: x.reshape(x.shape[0] // 8, 8, width)
        top = jnp.full((8, width), -1e30, jnp.float32)
        for at in range(0, n_keys, STEP):
            x = here[at : at + STEP]
            if at < own:
                key_pos = lax.broadcasted_iota(jnp.int32, x.shape, 0) + at
                row_pos = lax.broadcasted_iota(jnp.int32, x.shape, 1) % rows
                x = jnp.where(key_pos <= row_pos, x, -1e30)
                here[at : at + STEP] = x
            top = jnp.maximum(top, jnp.max(fold(x), axis=0))
        top = jnp.max(top, axis=0, keepdims=True) * scale
        top = jnp.broadcast_to(top, (8, width))
        total = jnp.zeros((8, width), jnp.float32)
        for at in range(0, n_keys, STEP):
            e = jnp.exp2(fold(here[at : at + STEP]) * scale - top)
            total = total + jnp.sum(e, axis=0)
            e_ref[head % 2, at : at + STEP, cols] = e.reshape(-1, width).astype(jnp.bfloat16)
        total = jnp.sum(total, axis=0, keepdims=True)
        inverse = jnp.where(live, 1.0 / total, 0.0)
        grad = turned_ref[first + head, :, cols].astype(jnp.float32) * inverse
        dot_ref[head % 2, :, cols] = grad.astype(jnp.bfloat16)
        return inverse

    def attended(head, pair, inverse):
        cols = place(head, pair)
        if pair == 0:
            assemble(head, vown_ref, held, values_ref, values_t_ref)
        grad = dot_ref[head % 2, :, cols]
        dp_ref[pair % 2] = jnp.dot(values_ref[head], grad, preferred_element_type=jnp.float32)
        out = jnp.dot(
            values_t_ref[head], e_ref[head % 2, :, cols], preferred_element_type=jnp.float32
        )
        out = out * inverse
        turned = out.astype(jnp.bfloat16).T
        for i in range(PAIR):
            at = head * GROUP + pair * PAIR + i
            out_ref[:, at * HD : (at + 1) * HD] = turned[i * rows : (i + 1) * rows]
        return jnp.sum(out * grad.astype(jnp.float32), axis=0, keepdims=True)

    def score_grads(head, pair, centre):
        cols = place(head, pair)
        here = dp_ref.at[pair % 2]
        centre = jnp.broadcast_to(centre, (STEP, width))
        for at in range(0, n_keys, STEP):
            e = e_ref[head % 2, at : at + STEP, cols].astype(jnp.float32)
            grad = e * (here[at : at + STEP] - centre)
            ds_ref[head % 2, at : at + STEP, cols] = grad.astype(jnp.bfloat16)

    def query_grads(head, pair):
        cols = place(head, pair)
        dq = jnp.dot(
            keys_t_ref[head], ds_ref[head % 2, :, cols], preferred_element_type=jnp.float32
        )
        turned = (dq * factor).astype(jnp.bfloat16).T
        for i in range(PAIR):
            at = head * GROUP + pair * PAIR + i
            dq_ref[:, at * HD : (at + 1) * HD] = turned[i * rows : (i + 1) * rows]

    def key_grads(head):
        copy = pltpu.make_async_copy(
            out_ref.at[:, columns(head, GROUP * HD)],
            out_hbm.at[:, columns(first + head, GROUP * HD)],
            out_sem.at[head],
        )
        copy.start()
        stores.append(copy)
        here = slice(head * HD, (head + 1) * HD)
        dv = lax.dot_general(
            e_ref[head % 2], dot_ref[head % 2], NT, preferred_element_type=jnp.float32
        ).astype(jnp.bfloat16)
        dvown_ref[:, here] = dv[:own]
        for i, ref in enumerate(term_refs):
            ref[held:, here] = dv[own + i * held : own + (i + 1) * held]
        dk = jnp.dot(
            ds_ref[head % 2],
            heads_down(q_ref, (first + head) * GROUP, GROUP),
            preferred_element_type=jnp.float32,
        )
        dk = (dk * factor).astype(jnp.bfloat16)
        dkown_ref[:, here] = dk[:own]
        for i, ref in enumerate(term_refs):
            ref[:held, here] = dk[own + i * held : own + (i + 1) * held]

    steps = [(head, pair) for head in range(count) for pair in range(pairs)]
    scores(*steps[0])
    inverse = softmax(*steps[0])
    for now, then in zip(steps, steps[1:] + [None]):
        if then:
            scores(*then)
        centre = attended(*now, inverse)
        if then:
            inverse = softmax(*then)
        score_grads(*now, centre)
        query_grads(*now)
        if now[1] + 1 == pairs:
            key_grads(now[0])
    for copy in stores:
        copy.wait()


def turn_kernel(do_ref, after_ref, out_ref):
    out_ref[0] = heads_down(do_ref, 0, GROUP).T


def scale_kernel(slots_all, total_ref, *refs):
    sources, refs = refs[: 3 * CHUNKS], refs[3 * CHUNKS :]
    outs, held, sem = refs[:3], refs[3:6], refs[6]
    weight = slots_all / total_ref[:1, :1]
    copies = []
    for chunk in range(CHUNKS):
        for i in range(3):
            source = sources[chunk * 3 + i]
            cols = pl.ds(chunk * source.shape[1], source.shape[1])
            scaled = source[...].astype(jnp.float32) * weight
            held[i][:, cols] = scaled.astype(jnp.bfloat16)
            copy = pltpu.make_async_copy(held[i].at[:, cols], outs[i].at[:, cols], sem.at[chunk, i])
            copy.start()
            copies.append(copy)
    for copy in copies:
        copy.wait()


def swap(x, axis, by):
    return lax.ppermute(x, axis, [(i, i ^ by) for i in range(lax.axis_size(axis))])


def sum_over(x, axis):
    by = 1
    while by < lax.axis_size(axis):
        x = x + swap(x, axis, by)
        by *= 2
    return x


def far_and_near(block):
    size = lax.axis_size("response")
    order = (3, 1) if size == 4 else range(1, size)
    return {m: swap(block, "response", m) for m in order}


def line_gather(block, sent):
    size = lax.axis_size("response")
    if size == 4:
        sent = {**sent, 2: swap(sent[3], "response", 1)}
    return [block] + [sent[m] for m in range(1, size)]


def far_sum(slots, order):
    terms = [slots[0]] + [swap(slots[m], "response", m) for m in order]
    return functools.reduce(jnp.add, [term.astype(jnp.float32) for term in terms])


def own_columns(block, chunk, by):
    cols = block.shape[1] // (lax.axis_size("tensor") * CHUNKS)
    rank = lax.axis_index("tensor") ^ by
    return lax.dynamic_slice_in_dim(block, (rank * CHUNKS + chunk) * cols, cols, 1)


def tensor_gather(blocks, chunk):
    parts = lax.axis_size("tensor")
    pieces = []
    for m in range(parts):
        piece = jnp.concatenate([own_columns(block, chunk, m) for block in blocks], axis=0)
        pieces.append(piece if m == 0 else swap(piece, "tensor", m))
    rows = blocks[0].shape[0]
    return jnp.concatenate(
        [piece[i * rows : (i + 1) * rows] for i in range(len(blocks)) for piece in pieces], axis=0
    )


def tensor_spread(total, n_arrays):
    parts = lax.axis_size("tensor")
    rows = total.shape[0] // (n_arrays * parts)
    pieces = []
    for m in range(parts):
        piece = jnp.concatenate(
            [total[(i * parts + m) * rows : (i * parts + m + 1) * rows] for i in range(n_arrays)],
            axis=0,
        )
        pieces.append(piece if m == 0 else swap(piece, "tensor", m))
    return pieces


def whole_columns(chunk_pieces, array):
    parts = lax.axis_size("tensor")
    rank = lax.axis_index("tensor")
    rows = chunk_pieces[0][0].shape[0] // 2
    by_rank = [
        jnp.concatenate([pieces[m][array * rows : (array + 1) * rows] for pieces in chunk_pieces], axis=1)
        for m in range(parts)
    ]
    ordered = []
    for t in range(parts):
        column = by_rank[0]
        for m in range(1, parts):
            column = jnp.where(rank ^ m == t, by_rank[m], column)
        ordered.append(column)
    return jnp.concatenate(ordered, axis=1)


SMEM = pl.BlockSpec(memory_space=pltpu.SMEM)
HBM = pl.BlockSpec(memory_space=pltpu.HBM)
VMEM = pl.BlockSpec(memory_space=pltpu.VMEM)


def like(x):
    return jax.ShapeDtypeStruct(x.shape, x.dtype)


def turn(do, after):
    rows, heads = do.shape[0], do.shape[1] // (GROUP * HD)
    return pl.pallas_call(
        turn_kernel,
        grid=(heads,),
        in_specs=[pl.BlockSpec((rows, GROUP * HD), lambda j: (0, j)), HBM],
        out_specs=pl.BlockSpec((1, HD, GROUP * rows), lambda j: (j, 0, 0)),
        out_shape=jax.ShapeDtypeStruct((heads, HD, GROUP * rows), do.dtype),
        compiler_params=pltpu.CompilerParams(vmem_limit_bytes=SMALL_LIMIT),
        name="turn",
    )(do, after)


def attend(chunk, held, slots, length, q, turned, k, v, carried):
    rows = q.shape[0]
    count = k.shape[1] // (HD * CHUNKS)
    n_slots = len(slots)
    last = chunk + 1 == CHUNKS
    n_keys = rows + n_slots * held
    bf16 = jnp.bfloat16
    unit = 2 * n_keys * GROUP * rows * HD * count
    step_buffer = pltpu.VMEM((2, n_keys, PAIR * rows), jnp.float32)
    head_buffer = pltpu.VMEM((2, n_keys, GROUP * rows), bf16)
    wide = pltpu.VMEM((rows, count * GROUP * HD), bf16)
    down = pltpu.VMEM((count, n_keys, HD), bf16)
    across = pltpu.VMEM((count, HD, n_keys), bf16)
    scratch = [wide, step_buffer, step_buffer, head_buffer, head_buffer]
    scratch += [pltpu.VMEM((2, HD, GROUP * rows), bf16), down, across, down, across]
    in_buffers = sum(math.prod(x.shape) * jnp.dtype(x.dtype).itemsize for x in scratch)
    part = lambda x: jax.ShapeDtypeStruct((x.shape[0], x.shape[1] // CHUNKS), bf16)
    terms = [jax.ShapeDtypeStruct((2 * held, count * HD), bf16)] * n_slots
    total = [jax.ShapeDtypeStruct((8, HD), jnp.float32)] * last
    return pl.pallas_call(
        functools.partial(attend_kernel, n_slots, count, chunk, held, 1.0 / math.sqrt(HD)),
        in_specs=[SMEM] + [VMEM] * (4 + n_slots) + [HBM] * last,
        out_specs=[HBM] + [VMEM] * (3 + n_slots + last),
        out_shape=[like(q), part(q), part(k), part(v)] + terms + total,
        input_output_aliases={5 + n_slots: 0} if last else {},
        scratch_shapes=scratch + [pltpu.SemaphoreType.DMA((count,))],
        compiler_params=pltpu.CompilerParams(vmem_limit_bytes=in_buffers * 5 // 4 + SMALL_LIMIT // 2),
        cost_estimate=pl.CostEstimate(
            flops=24 * unit,
            bytes_accessed=8 * rows * GROUP * HD * count,
            transcendentals=count * n_keys * GROUP * rows,
        ),
        name=f"attend_{chunk}",
    )(length, q, turned, k, v, *slots, *carried)


def scale_all(slots_all, total, chunk_grads, shapes):
    flat = [grad for grads in chunk_grads for grad in grads]
    return pl.pallas_call(
        functools.partial(scale_kernel, slots_all),
        in_specs=[VMEM] * (1 + len(flat)),
        out_specs=[HBM] * len(shapes),
        out_shape=shapes,
        scratch_shapes=[pltpu.VMEM(x.shape, x.dtype) for x in shapes]
        + [pltpu.SemaphoreType.DMA((CHUNKS, len(shapes)))],
        compiler_params=pltpu.CompilerParams(vmem_limit_bytes=SMALL_LIMIT),
        cost_estimate=pl.CostEstimate(
            flops=sum(x.size for x in shapes),
            bytes_accessed=sum(4 * x.size for x in shapes),
            transcendentals=0,
        ),
        name="scale",
    )(total, *flat)


def body(queries, keys, values, prefix_keys, prefix_values, lengths, out_grad):
    q, k, v, do = queries[0], keys[0], values[0], out_grad[0]
    length = lengths[0]
    prefix = (prefix_keys[0], prefix_values[0])
    slots_all = q.shape[0] * lax.axis_size("prompt") * lax.axis_size("response")
    first, second = [tensor_gather(prefix, chunk) for chunk in range(CHUNKS)]
    held = first.shape[0] // 2
    sent = far_and_near(first)
    slots = line_gather(first, sent)
    length_rows = length[0].astype(second.dtype) + 0 * slots[-1][-EXTRA:]
    second = jnp.concatenate([second, length_rows], axis=0)
    sent = far_and_near(second)
    turned = turn(do, first)
    results = attend(0, held, slots, length, q, turned, k, v, [])
    if len(slots) == 4:
        far = sent[3]
        sent[3] = jnp.concatenate([far[:-EXTRA] + 0 * results[4], far[-EXTRA:]], axis=0)
    next_slots = line_gather(second, sent)
    next_results = attend(1, held, next_slots, length, q, turned, k, v, results[:1])
    terms, next_terms = results[4:], next_results[4:-1]
    behind = 0 * next_results[3][:1].astype(jnp.float32)
    order = list(range(len(terms) - 1, 1, -1))
    sums = [far_sum(terms, order) + behind, far_sum(next_terms, order)]
    nearest = jnp.concatenate([terms[1], next_terms[1]], axis=1)
    near = swap(nearest, "response", 1)
    total = sum_over(next_results[-1] + 0 * nearest[:8, :HD].astype(jnp.float32), "prompt")
    weight = jnp.tile(slots_all / total[:1], (1, prefix[0].shape[1] // HD))
    scaled = scale_all(
        slots_all, total + 0 * sums[1][:8, :HD], [results[1:4], next_results[1:4]], [like(q), like(k), like(v)]
    )
    both = jnp.concatenate(sums, axis=1) + near.astype(jnp.float32)
    both = both.astype(jnp.bfloat16)
    pieces = [tensor_spread(both, len(prefix))]
    grads = [whole_columns(pieces, array) for array in range(len(prefix))]
    grads = [(grad.astype(jnp.float32) * weight).astype(jnp.bfloat16) for grad in grads]
    return tuple(x[None] for x in (next_results[0], *scaled, *grads))


def solution(mesh):
    in_specs = (
        P("prompt", "response", "tensor"),
        P("prompt", "response", "tensor"),
        P("prompt", "response", "tensor"),
        P("prompt", ("response", "tensor"), None),
        P("prompt", ("response", "tensor"), None),
        P("prompt", "response"),
        P("prompt", "response", "tensor"),
    )
    out_specs = (
        P("prompt", "response", "tensor"),
        P("prompt", "response", "tensor"),
        P("prompt", "response", "tensor"),
        P("prompt", "response", "tensor"),
        P("prompt", ("response", "tensor"), None),
        P("prompt", ("response", "tensor"), None),
    )
    return jax.shard_map(body, mesh=mesh, in_specs=in_specs, out_specs=out_specs, check_vma=False)
```

```python
import functools
import math

import jax
import jax.numpy as jnp
from jax import lax
from jax.experimental import pallas as pl
from jax.experimental.pallas import tpu as pltpu
from jax.sharding import PartitionSpec as P

HD = 128
GROUP = 8
PAIR = 2
CHUNKS = 2
EXTRA = 16
STEP = 64
VMEM_LIMIT = 40 * 1024 * 1024
SMALL_LIMIT = 8 * 1024 * 1024
NT = (((1,), (1,)), ((), ()))


def heads_down(ref, first, count):
    return jnp.concatenate(
        [ref[:, (first + i) * HD : (first + i + 1) * HD] for i in range(count)], axis=0
    )


def attend_kernel(n_slots, count, chunk, held, factor, *refs):
    last = chunk + 1 == CHUNKS
    length_ref, q_ref, turned_ref, kown_ref, vown_ref = refs[:5]
    slot_refs, refs = refs[5 : 5 + n_slots], refs[5 + n_slots + last :]
    out_hbm, dq_ref, dkown_ref, dvown_ref = refs[:4]
    term_refs, refs = refs[4 : 4 + n_slots], refs[4 + n_slots :]
    if last:
        total_ref, refs = refs[0], refs[1:]
        totals = [ref[2 * held : 2 * held + 8, :HD].astype(jnp.float32) for ref in slot_refs]
        total_ref[...] = functools.reduce(jnp.add, totals)
    out_ref, s_ref, e_ref, ds_ref, dot_ref = refs[:5]
    keys_ref, keys_t_ref, values_ref, values_t_ref, out_sem = refs[5:]
    first = chunk * count
    rows = q_ref.shape[0]
    own = kown_ref.shape[0]
    n_keys = s_ref.shape[1]
    width = PAIR * rows
    pairs = GROUP // PAIR
    scale = factor * math.log2(math.e)

    def columns(head, size):
        return pl.ds(head * size, size)

    stores = []

    live = (lax.broadcasted_iota(jnp.int32, (1, width), 1) % rows) < length_ref[0]

    def assemble(head, own_ref, slot_start, wide_ref, tall_ref):
        here = slice(head * HD, (head + 1) * HD)
        wide_ref[head, :own] = own_ref[:, (first + head) * HD : (first + head + 1) * HD]
        for i, ref in enumerate(slot_refs):
            part = slice(own + i * held, own + (i + 1) * held)
            wide_ref[head, part] = ref[slot_start : slot_start + held, here]
        tall_ref[head] = wide_ref[head].T

    def place(head, pair):
        return slice(pair * width, (pair + 1) * width)

    def fold(x):
        return x.reshape(x.shape[0] // 8, 8, width)

    def scores(head, pair):
        if pair == 0:
            assemble(head, kown_ref, 0, keys_ref, keys_t_ref)
        s = lax.dot_general(
            keys_ref[head],
            heads_down(q_ref, (first + head) * GROUP + pair * PAIR, PAIR),
            NT,
            preferred_element_type=jnp.float32,
        )
        top = jnp.full((8, width), -1e30, jnp.float32)
        for at in range(0, n_keys, STEP):
            x = s[at : at + STEP]
            if at < own:
                key_pos = lax.broadcasted_iota(jnp.int32, x.shape, 0) + at
                row_pos = lax.broadcasted_iota(jnp.int32, x.shape, 1) % rows
                x = jnp.where(key_pos <= row_pos, x, -1e30)
            s_ref[pair % 2, at : at + STEP] = x
            top = jnp.maximum(top, jnp.max(fold(x), axis=0))
        top = jnp.max(top, axis=0, keepdims=True) * scale
        return jnp.broadcast_to(top, (8, width))

    def softmax(head, pair, top):
        here = s_ref.at[pair % 2]
        cols = place(head, pair)
        total = jnp.zeros((8, width), jnp.float32)
        for at in range(0, n_keys, STEP):
            e = jnp.exp2(fold(here[at : at + STEP]) * scale - top)
            total = total + jnp.sum(e, axis=0)
            e_ref[head % 2, at : at + STEP, cols] = e.reshape(-1, width).astype(jnp.bfloat16)
        total = jnp.sum(total, axis=0, keepdims=True)
        inverse = jnp.where(live, 1.0 / total, 0.0)
        grad = turned_ref[first + head, :, cols].astype(jnp.float32) * inverse
        dot_ref[head % 2, :, cols] = grad.astype(jnp.bfloat16)
        return inverse

    def attended(head, pair, inverse):
        cols = place(head, pair)
        if pair == 0:
            assemble(head, vown_ref, held, values_ref, values_t_ref)
        grad = dot_ref[head % 2, :, cols]
        out = jnp.dot(
            values_t_ref[head], e_ref[head % 2, :, cols], preferred_element_type=jnp.float32
        )
        out = out * inverse
        turned = out.astype(jnp.bfloat16).T
        for i in range(PAIR):
            at = head * GROUP + pair * PAIR + i
            out_ref[:, at * HD : (at + 1) * HD] = turned[i * rows : (i + 1) * rows]
        return jnp.sum(out * grad.astype(jnp.float32), axis=0, keepdims=True)

    def score_grads(head, pair, centre):
        cols = place(head, pair)
        dp = jnp.dot(
            values_ref[head], dot_ref[head % 2, :, cols], preferred_element_type=jnp.float32
        )
        centre = jnp.broadcast_to(centre, (STEP, width))
        for at in range(0, n_keys, STEP):
            e = e_ref[head % 2, at : at + STEP, cols].astype(jnp.float32)
            grad = e * (dp[at : at + STEP] - centre)
            ds_ref[head % 2, at : at + STEP, cols] = grad.astype(jnp.bfloat16)

    def query_grads(head, pair):
        cols = place(head, pair)
        dq = jnp.dot(
            keys_t_ref[head], ds_ref[head % 2, :, cols], preferred_element_type=jnp.float32
        )
        turned = (dq * factor).astype(jnp.bfloat16).T
        for i in range(PAIR):
            at = head * GROUP + pair * PAIR + i
            dq_ref[:, at * HD : (at + 1) * HD] = turned[i * rows : (i + 1) * rows]

    def key_grads(head):
        copy = pltpu.make_async_copy(
            out_ref.at[:, columns(head, GROUP * HD)],
            out_hbm.at[:, columns(first + head, GROUP * HD)],
            out_sem.at[head],
        )
        copy.start()
        stores.append(copy)
        here = slice(head * HD, (head + 1) * HD)
        dv = lax.dot_general(
            e_ref[head % 2], dot_ref[head % 2], NT, preferred_element_type=jnp.float32
        ).astype(jnp.bfloat16)
        dvown_ref[:, here] = dv[:own]
        for i, ref in enumerate(term_refs):
            ref[held:, here] = dv[own + i * held : own + (i + 1) * held]
        dk = jnp.dot(
            ds_ref[head % 2],
            heads_down(q_ref, (first + head) * GROUP, GROUP),
            preferred_element_type=jnp.float32,
        )
        dk = (dk * factor).astype(jnp.bfloat16)
        dkown_ref[:, here] = dk[:own]
        for i, ref in enumerate(term_refs):
            ref[:held, here] = dk[own + i * held : own + (i + 1) * held]

    steps = [(head, pair) for head in range(count) for pair in range(pairs)]
    inverse = softmax(*steps[0], scores(*steps[0]))
    for now, then in zip(steps, steps[1:] + [None]):
        if then:
            top = scores(*then)
        centre = attended(*now, inverse)
        if then:
            inverse = softmax(*then, top)
        score_grads(*now, centre)
        query_grads(*now)
        if now[1] + 1 == pairs:
            key_grads(now[0])
    for copy in stores:
        copy.wait()


def turn_kernel(do_ref, after_ref, out_ref):
    out_ref[0] = heads_down(do_ref, 0, GROUP).T


def scale_kernel(slots_all, total_ref, *refs):
    sources, refs = refs[: 3 * CHUNKS], refs[3 * CHUNKS :]
    outs, held, sem = refs[:3], refs[3:6], refs[6]
    weight = slots_all / total_ref[:1, :1]
    copies = []
    for chunk in range(CHUNKS):
        for i in range(3):
            source = sources[chunk * 3 + i]
            cols = pl.ds(chunk * source.shape[1], source.shape[1])
            scaled = source[...].astype(jnp.float32) * weight
            held[i][:, cols] = scaled.astype(jnp.bfloat16)
            copy = pltpu.make_async_copy(held[i].at[:, cols], outs[i].at[:, cols], sem.at[chunk, i])
            copy.start()
            copies.append(copy)
    for copy in copies:
        copy.wait()


def swap(x, axis, by):
    return lax.ppermute(x, axis, [(i, i ^ by) for i in range(lax.axis_size(axis))])


def sum_over(x, axis):
    by = 1
    while by < lax.axis_size(axis):
        x = x + swap(x, axis, by)
        by *= 2
    return x


def far_and_near(block):
    size = lax.axis_size("response")
    order = (3, 1) if size == 4 else range(1, size)
    return {m: swap(block, "response", m) for m in order}


def line_gather(block, sent):
    size = lax.axis_size("response")
    if size == 4:
        sent = {**sent, 2: swap(sent[3], "response", 1)}
    return [block] + [sent[m] for m in range(1, size)]


def line_reduce(slots, order):
    terms = [swap(slots[m], "response", m) for m in order]
    return functools.reduce(jnp.add, [term.astype(jnp.float32) for term in [slots[0]] + terms])


def own_columns(block, chunk, by):
    cols = block.shape[1] // (lax.axis_size("tensor") * CHUNKS)
    rank = lax.axis_index("tensor") ^ by
    return lax.dynamic_slice_in_dim(block, (rank * CHUNKS + chunk) * cols, cols, 1)


def tensor_gather(blocks, chunk):
    parts = lax.axis_size("tensor")
    pieces = []
    for m in range(parts):
        piece = jnp.concatenate([own_columns(block, chunk, m) for block in blocks], axis=0)
        pieces.append(piece if m == 0 else swap(piece, "tensor", m))
    rows = blocks[0].shape[0]
    return jnp.concatenate(
        [piece[i * rows : (i + 1) * rows] for i in range(len(blocks)) for piece in pieces], axis=0
    )


def tensor_spread(total, n_arrays):
    parts = lax.axis_size("tensor")
    rows = total.shape[0] // (n_arrays * parts)
    pieces = []
    for m in range(parts):
        piece = jnp.concatenate(
            [total[(i * parts + m) * rows : (i * parts + m + 1) * rows] for i in range(n_arrays)],
            axis=0,
        )
        pieces.append(piece if m == 0 else swap(piece, "tensor", m))
    return pieces


def whole_columns(chunk_pieces, array):
    parts = lax.axis_size("tensor")
    rank = lax.axis_index("tensor")
    rows = chunk_pieces[0][0].shape[0] // 2
    by_rank = [
        jnp.concatenate([pieces[m][array * rows : (array + 1) * rows] for pieces in chunk_pieces], axis=1)
        for m in range(parts)
    ]
    ordered = []
    for t in range(parts):
        column = by_rank[0]
        for m in range(1, parts):
            column = jnp.where(rank ^ m == t, by_rank[m], column)
        ordered.append(column)
    return jnp.concatenate(ordered, axis=1)


SMEM = pl.BlockSpec(memory_space=pltpu.SMEM)
HBM = pl.BlockSpec(memory_space=pltpu.HBM)
VMEM = pl.BlockSpec(memory_space=pltpu.VMEM)


def like(x):
    return jax.ShapeDtypeStruct(x.shape, x.dtype)


def turn(do, after):
    rows, heads = do.shape[0], do.shape[1] // (GROUP * HD)
    return pl.pallas_call(
        turn_kernel,
        grid=(heads,),
        in_specs=[pl.BlockSpec((rows, GROUP * HD), lambda j: (0, j)), HBM],
        out_specs=pl.BlockSpec((1, HD, GROUP * rows), lambda j: (j, 0, 0)),
        out_shape=jax.ShapeDtypeStruct((heads, HD, GROUP * rows), do.dtype),
        compiler_params=pltpu.CompilerParams(vmem_limit_bytes=SMALL_LIMIT),
        name="turn",
    )(do, after)


def attend(chunk, held, slots, length, q, turned, k, v, carried):
    rows = q.shape[0]
    count = k.shape[1] // (HD * CHUNKS)
    n_slots = len(slots)
    last = chunk + 1 == CHUNKS
    n_keys = rows + n_slots * held
    bf16 = jnp.bfloat16
    unit = 2 * n_keys * GROUP * rows * HD * count
    step_buffer = pltpu.VMEM((2, n_keys, PAIR * rows), jnp.float32)
    head_buffer = pltpu.VMEM((2, n_keys, GROUP * rows), bf16)
    wide = pltpu.VMEM((rows, count * GROUP * HD), bf16)
    down = pltpu.VMEM((count, n_keys, HD), bf16)
    across = pltpu.VMEM((count, HD, n_keys), bf16)
    scratch = [wide, step_buffer, head_buffer, head_buffer]
    scratch += [pltpu.VMEM((2, HD, GROUP * rows), bf16), down, across, down, across]
    scratch += [pltpu.SemaphoreType.DMA((count,))]
    part = lambda x: jax.ShapeDtypeStruct((x.shape[0], x.shape[1] // CHUNKS), bf16)
    terms = [jax.ShapeDtypeStruct((2 * held, count * HD), bf16)] * n_slots
    total = [jax.ShapeDtypeStruct((8, HD), jnp.float32)] * last
    return pl.pallas_call(
        functools.partial(attend_kernel, n_slots, count, chunk, held, 1.0 / math.sqrt(HD)),
        in_specs=[SMEM] + [VMEM] * (4 + n_slots) + [HBM] * last,
        out_specs=[HBM] + [VMEM] * (3 + n_slots + last),
        out_shape=[like(q), part(q), part(k), part(v)] + terms + total,
        input_output_aliases={5 + n_slots: 0} if last else {},
        scratch_shapes=scratch,
        compiler_params=pltpu.CompilerParams(vmem_limit_bytes=VMEM_LIMIT),
        cost_estimate=pl.CostEstimate(
            flops=24 * unit,
            bytes_accessed=8 * rows * GROUP * HD * count,
            transcendentals=count * n_keys * GROUP * rows,
        ),
        name=f"attend_{chunk}",
    )(length, q, turned, k, v, *slots, *carried)


def scale_all(slots_all, total, chunk_grads, shapes):
    flat = [grad for grads in chunk_grads for grad in grads]
    return pl.pallas_call(
        functools.partial(scale_kernel, slots_all),
        in_specs=[VMEM] * (1 + len(flat)),
        out_specs=[HBM] * len(shapes),
        out_shape=shapes,
        scratch_shapes=[pltpu.VMEM(x.shape, x.dtype) for x in shapes]
        + [pltpu.SemaphoreType.DMA((CHUNKS, len(shapes)))],
        compiler_params=pltpu.CompilerParams(vmem_limit_bytes=SMALL_LIMIT),
        cost_estimate=pl.CostEstimate(
            flops=sum(x.size for x in shapes),
            bytes_accessed=sum(4 * x.size for x in shapes),
            transcendentals=0,
        ),
        name="scale",
    )(total, *flat)


def body(queries, keys, values, prefix_keys, prefix_values, lengths, out_grad):
    q, k, v, do = queries[0], keys[0], values[0], out_grad[0]
    length = lengths[0]
    prefix = (prefix_keys[0], prefix_values[0])
    slots_all = q.shape[0] * lax.axis_size("prompt") * lax.axis_size("response")
    first, second = [tensor_gather(prefix, chunk) for chunk in range(CHUNKS)]
    held = first.shape[0] // 2
    sent = far_and_near(first)
    slots = line_gather(first, sent)
    length_rows = length[0].astype(second.dtype) + 0 * slots[-1][-EXTRA:]
    second = jnp.concatenate([second, length_rows], axis=0)
    sent = far_and_near(second)
    turned = turn(do, first)
    results = attend(0, held, slots, length, q, turned, k, v, [])
    if len(slots) == 4:
        far = sent[3]
        sent[3] = jnp.concatenate([far[:-EXTRA] + 0 * results[4], far[-EXTRA:]], axis=0)
    next_slots = line_gather(second, sent)
    next_results = attend(1, held, next_slots, length, q, turned, k, v, results[:1])
    terms, next_terms = results[4:], next_results[4:-1]
    behind = 0 * next_results[3][:1].astype(jnp.float32)
    farthest_first = list(range(len(terms) - 1, 0, -1))
    order = (2, 1, 3) if len(terms) == 4 else farthest_first
    sums = [line_reduce(terms, order) + behind, line_reduce(next_terms, farthest_first)]
    total = sum_over(next_results[-1] + 0 * sums[0][:8, :HD], "prompt")
    weight = jnp.tile(slots_all / total[:1], (1, prefix[0].shape[1] // HD))
    scaled = scale_all(
        slots_all, total + 0 * sums[1][:8, :HD], [results[1:4], next_results[1:4]], [like(q), like(k), like(v)]
    )
    both = jnp.concatenate([terms.astype(jnp.bfloat16) for terms in sums], axis=1)
    pieces = [tensor_spread(both, len(prefix))]
    grads = [whole_columns(pieces, array) for array in range(len(prefix))]
    grads = [(grad.astype(jnp.float32) * weight).astype(jnp.bfloat16) for grad in grads]
    return tuple(x[None] for x in (next_results[0], *scaled, *grads))


def solution(mesh):
    in_specs = (
        P("prompt", "response", "tensor"),
        P("prompt", "response", "tensor"),
        P("prompt", "response", "tensor"),
        P("prompt", ("response", "tensor"), None),
        P("prompt", ("response", "tensor"), None),
        P("prompt", "response"),
        P("prompt", "response", "tensor"),
    )
    out_specs = (
        P("prompt", "response", "tensor"),
        P("prompt", "response", "tensor"),
        P("prompt", "response", "tensor"),
        P("prompt", "response", "tensor"),
        P("prompt", ("response", "tensor"), None),
        P("prompt", ("response", "tensor"), None),
    )
    return jax.shard_map(body, mesh=mesh, in_specs=in_specs, out_specs=out_specs, check_vma=False)
```

```python
import functools
import math

import jax
import jax.numpy as jnp
from jax import lax
from jax.experimental import pallas as pl
from jax.experimental.pallas import tpu as pltpu
from jax.sharding import PartitionSpec as P

HD = 128
GROUP = 8
PAIR = 4
CHUNKS = 2
EXTRA = 16
STEP = 64
SMALL_LIMIT = 8 * 1024 * 1024
NT = (((1,), (1,)), ((), ()))


def heads_down(ref, first, count):
    return jnp.concatenate(
        [ref[:, (first + i) * HD : (first + i + 1) * HD] for i in range(count)], axis=0
    )


def attend_kernel(n_slots, count, chunk, held, factor, *refs):
    last = chunk + 1 == CHUNKS
    length_ref, q_ref, turned_ref, kown_ref, vown_ref = refs[:5]
    slot_refs, refs = refs[5 : 5 + n_slots], refs[5 + n_slots + last :]
    out_hbm, dq_ref, dkown_ref, dvown_ref = refs[:4]
    term_refs, refs = refs[4 : 4 + n_slots], refs[4 + n_slots :]
    if last:
        total_ref, refs = refs[0], refs[1:]
        totals = [ref[2 * held : 2 * held + 8, :HD].astype(jnp.float32) for ref in slot_refs]
        total_ref[...] = functools.reduce(jnp.add, totals)
    out_ref, s_ref, dp_ref, e_ref, ds_ref, dot_ref = refs[:6]
    keys_ref, keys_t_ref, values_ref, values_t_ref, out_sem = refs[6:]
    first = chunk * count
    rows = q_ref.shape[0]
    own = kown_ref.shape[0]
    n_keys = s_ref.shape[1]
    width = PAIR * rows
    pairs = GROUP // PAIR
    scale = factor * math.log2(math.e)

    def columns(head, size):
        return pl.ds(head * size, size)

    stores = []

    live = (lax.broadcasted_iota(jnp.int32, (1, width), 1) % rows) < length_ref[0]

    def assemble(head, own_ref, slot_start, wide_ref, tall_ref):
        here = slice(head * HD, (head + 1) * HD)
        wide_ref[head, :own] = own_ref[:, (first + head) * HD : (first + head + 1) * HD]
        for i, ref in enumerate(slot_refs):
            part = slice(own + i * held, own + (i + 1) * held)
            wide_ref[head, part] = ref[slot_start : slot_start + held, here]
        tall_ref[head] = wide_ref[head].T

    def place(head, pair):
        return slice(pair * width, (pair + 1) * width)

    def scores(head, pair):
        if pair == 0:
            assemble(head, kown_ref, 0, keys_ref, keys_t_ref)
        s_ref[pair % 2] = lax.dot_general(
            keys_ref[head],
            heads_down(q_ref, (first + head) * GROUP + pair * PAIR, PAIR),
            NT,
            preferred_element_type=jnp.float32,
        )

    def softmax(head, pair):
        here = s_ref.at[pair % 2]
        cols = place(head, pair)
        fold = lambda x: x.reshape(x.shape[0] // 8, 8, width)
        top = jnp.full((8, width), -1e30, jnp.float32)
        for at in range(0, n_keys, STEP):
            x = here[at : at + STEP]
            if at < own:
                key_pos = lax.broadcasted_iota(jnp.int32, x.shape, 0) + at
                row_pos = lax.broadcasted_iota(jnp.int32, x.shape, 1) % rows
                x = jnp.where(key_pos <= row_pos, x, -1e30)
                here[at : at + STEP] = x
            top = jnp.maximum(top, jnp.max(fold(x), axis=0))
        top = jnp.max(top, axis=0, keepdims=True) * scale
        top = jnp.broadcast_to(top, (8, width))
        total = jnp.zeros((8, width), jnp.float32)
        for at in range(0, n_keys, STEP):
            e = jnp.exp2(fold(here[at : at + STEP]) * scale - top)
            total = total + jnp.sum(e, axis=0)
            e_ref[head % 2, at : at + STEP, cols] = e.reshape(-1, width).astype(jnp.bfloat16)
        total = jnp.sum(total, axis=0, keepdims=True)
        inverse = jnp.where(live, 1.0 / total, 0.0)
        grad = turned_ref[first + head, :, cols].astype(jnp.float32) * inverse
        dot_ref[head % 2, :, cols] = grad.astype(jnp.bfloat16)
        return inverse

    def attended(head, pair, inverse):
        cols = place(head, pair)
        if pair == 0:
            assemble(head, vown_ref, held, values_ref, values_t_ref)
        grad = dot_ref[head % 2, :, cols]
        dp_ref[pair % 2] = jnp.dot(values_ref[head], grad, preferred_element_type=jnp.float32)
        out = jnp.dot(
            values_t_ref[head], e_ref[head % 2, :, cols], preferred_element_type=jnp.float32
        )
        out = out * inverse
        turned = out.astype(jnp.bfloat16).T
        for i in range(PAIR):
            at = head * GROUP + pair * PAIR + i
            out_ref[:, at * HD : (at + 1) * HD] = turned[i * rows : (i + 1) * rows]
        return jnp.sum(out * grad.astype(jnp.float32), axis=0, keepdims=True)

    def score_grads(head, pair, centre):
        cols = place(head, pair)
        here = dp_ref.at[pair % 2]
        centre = jnp.broadcast_to(centre, (STEP, width))
        for at in range(0, n_keys, STEP):
            e = e_ref[head % 2, at : at + STEP, cols].astype(jnp.float32)
            grad = e * (here[at : at + STEP] - centre)
            ds_ref[head % 2, at : at + STEP, cols] = grad.astype(jnp.bfloat16)

    def query_grads(head, pair):
        cols = place(head, pair)
        dq = jnp.dot(
            keys_t_ref[head], ds_ref[head % 2, :, cols], preferred_element_type=jnp.float32
        )
        turned = (dq * factor).astype(jnp.bfloat16).T
        for i in range(PAIR):
            at = head * GROUP + pair * PAIR + i
            dq_ref[:, at * HD : (at + 1) * HD] = turned[i * rows : (i + 1) * rows]

    def key_grads(head):
        copy = pltpu.make_async_copy(
            out_ref.at[:, columns(head, GROUP * HD)],
            out_hbm.at[:, columns(first + head, GROUP * HD)],
            out_sem.at[head],
        )
        copy.start()
        stores.append(copy)
        here = slice(head * HD, (head + 1) * HD)
        dv = lax.dot_general(
            e_ref[head % 2], dot_ref[head % 2], NT, preferred_element_type=jnp.float32
        ).astype(jnp.bfloat16)
        dvown_ref[:, here] = dv[:own]
        for i, ref in enumerate(term_refs):
            ref[held:, here] = dv[own + i * held : own + (i + 1) * held]
        dk = jnp.dot(
            ds_ref[head % 2],
            heads_down(q_ref, (first + head) * GROUP, GROUP),
            preferred_element_type=jnp.float32,
        )
        dk = (dk * factor).astype(jnp.bfloat16)
        dkown_ref[:, here] = dk[:own]
        for i, ref in enumerate(term_refs):
            ref[:held, here] = dk[own + i * held : own + (i + 1) * held]

    steps = [(head, pair) for head in range(count) for pair in range(pairs)]
    scores(*steps[0])
    inverse = softmax(*steps[0])
    for now, then in zip(steps, steps[1:] + [None]):
        if then:
            scores(*then)
        centre = attended(*now, inverse)
        if then:
            inverse = softmax(*then)
        score_grads(*now, centre)
        query_grads(*now)
        if now[1] + 1 == pairs:
            key_grads(now[0])
    for copy in stores:
        copy.wait()


def turn_kernel(do_ref, after_ref, out_ref):
    out_ref[0] = heads_down(do_ref, 0, GROUP).T


def scale_kernel(slots_all, total_ref, *refs):
    sources, refs = refs[: 3 * CHUNKS], refs[3 * CHUNKS :]
    outs, held, sem = refs[:3], refs[3:6], refs[6]
    weight = slots_all / total_ref[:1, :1]
    copies = []
    for chunk in range(CHUNKS):
        for i in range(3):
            source = sources[chunk * 3 + i]
            cols = pl.ds(chunk * source.shape[1], source.shape[1])
            scaled = source[...].astype(jnp.float32) * weight
            held[i][:, cols] = scaled.astype(jnp.bfloat16)
            copy = pltpu.make_async_copy(held[i].at[:, cols], outs[i].at[:, cols], sem.at[chunk, i])
            copy.start()
            copies.append(copy)
    for copy in copies:
        copy.wait()


def swap(x, axis, by):
    return lax.ppermute(x, axis, [(i, i ^ by) for i in range(lax.axis_size(axis))])


def sum_over(x, axis):
    by = 1
    while by < lax.axis_size(axis):
        x = x + swap(x, axis, by)
        by *= 2
    return x


def far_and_near(block):
    size = lax.axis_size("response")
    order = (3, 1) if size == 4 else range(1, size)
    return {m: swap(block, "response", m) for m in order}


def line_gather(block, sent):
    size = lax.axis_size("response")
    if size == 4:
        sent = {**sent, 2: swap(sent[3], "response", 1)}
    return [block] + [sent[m] for m in range(1, size)]


def line_reduce(slots, order):
    terms = [swap(slots[m], "response", m) for m in order]
    return functools.reduce(jnp.add, [term.astype(jnp.float32) for term in [slots[0]] + terms])


def own_columns(block, chunk, by):
    cols = block.shape[1] // (lax.axis_size("tensor") * CHUNKS)
    rank = lax.axis_index("tensor") ^ by
    return lax.dynamic_slice_in_dim(block, (rank * CHUNKS + chunk) * cols, cols, 1)


def tensor_gather(blocks, chunk):
    parts = lax.axis_size("tensor")
    pieces = []
    for m in range(parts):
        piece = jnp.concatenate([own_columns(block, chunk, m) for block in blocks], axis=0)
        pieces.append(piece if m == 0 else swap(piece, "tensor", m))
    rows = blocks[0].shape[0]
    return jnp.concatenate(
        [piece[i * rows : (i + 1) * rows] for i in range(len(blocks)) for piece in pieces], axis=0
    )


def tensor_spread(total, n_arrays):
    parts = lax.axis_size("tensor")
    rows = total.shape[0] // (n_arrays * parts)
    pieces = []
    for m in range(parts):
        piece = jnp.concatenate(
            [total[(i * parts + m) * rows : (i * parts + m + 1) * rows] for i in range(n_arrays)],
            axis=0,
        )
        pieces.append(piece if m == 0 else swap(piece, "tensor", m))
    return pieces


def whole_columns(chunk_pieces, array):
    parts = lax.axis_size("tensor")
    rank = lax.axis_index("tensor")
    rows = chunk_pieces[0][0].shape[0] // 2
    by_rank = [
        jnp.concatenate([pieces[m][array * rows : (array + 1) * rows] for pieces in chunk_pieces], axis=1)
        for m in range(parts)
    ]
    ordered = []
    for t in range(parts):
        column = by_rank[0]
        for m in range(1, parts):
            column = jnp.where(rank ^ m == t, by_rank[m], column)
        ordered.append(column)
    return jnp.concatenate(ordered, axis=1)


SMEM = pl.BlockSpec(memory_space=pltpu.SMEM)
HBM = pl.BlockSpec(memory_space=pltpu.HBM)
VMEM = pl.BlockSpec(memory_space=pltpu.VMEM)


def like(x):
    return jax.ShapeDtypeStruct(x.shape, x.dtype)


def turn(do, after):
    rows, heads = do.shape[0], do.shape[1] // (GROUP * HD)
    return pl.pallas_call(
        turn_kernel,
        grid=(heads,),
        in_specs=[pl.BlockSpec((rows, GROUP * HD), lambda j: (0, j)), HBM],
        out_specs=pl.BlockSpec((1, HD, GROUP * rows), lambda j: (j, 0, 0)),
        out_shape=jax.ShapeDtypeStruct((heads, HD, GROUP * rows), do.dtype),
        compiler_params=pltpu.CompilerParams(vmem_limit_bytes=SMALL_LIMIT),
        name="turn",
    )(do, after)


def attend(chunk, held, slots, length, q, turned, k, v, carried):
    rows = q.shape[0]
    count = k.shape[1] // (HD * CHUNKS)
    n_slots = len(slots)
    last = chunk + 1 == CHUNKS
    n_keys = rows + n_slots * held
    bf16 = jnp.bfloat16
    unit = 2 * n_keys * GROUP * rows * HD * count
    step_buffer = pltpu.VMEM((2, n_keys, PAIR * rows), jnp.float32)
    head_buffer = pltpu.VMEM((2, n_keys, GROUP * rows), bf16)
    wide = pltpu.VMEM((rows, count * GROUP * HD), bf16)
    down = pltpu.VMEM((count, n_keys, HD), bf16)
    across = pltpu.VMEM((count, HD, n_keys), bf16)
    scratch = [wide, step_buffer, step_buffer, head_buffer, head_buffer]
    scratch += [pltpu.VMEM((2, HD, GROUP * rows), bf16), down, across, down, across]
    in_buffers = sum(math.prod(x.shape) * jnp.dtype(x.dtype).itemsize for x in scratch)
    part = lambda x: jax.ShapeDtypeStruct((x.shape[0], x.shape[1] // CHUNKS), bf16)
    terms = [jax.ShapeDtypeStruct((2 * held, count * HD), bf16)] * n_slots
    total = [jax.ShapeDtypeStruct((8, HD), jnp.float32)] * last
    return pl.pallas_call(
        functools.partial(attend_kernel, n_slots, count, chunk, held, 1.0 / math.sqrt(HD)),
        in_specs=[SMEM] + [VMEM] * (4 + n_slots) + [HBM] * last,
        out_specs=[HBM] + [VMEM] * (3 + n_slots + last),
        out_shape=[like(q), part(q), part(k), part(v)] + terms + total,
        input_output_aliases={5 + n_slots: 0} if last else {},
        scratch_shapes=scratch + [pltpu.SemaphoreType.DMA((count,))],
        compiler_params=pltpu.CompilerParams(vmem_limit_bytes=in_buffers * 5 // 4 + SMALL_LIMIT // 2),
        cost_estimate=pl.CostEstimate(
            flops=24 * unit,
            bytes_accessed=8 * rows * GROUP * HD * count,
            transcendentals=count * n_keys * GROUP * rows,
        ),
        name=f"attend_{chunk}",
    )(length, q, turned, k, v, *slots, *carried)


def scale_all(slots_all, total, chunk_grads, shapes):
    flat = [grad for grads in chunk_grads for grad in grads]
    return pl.pallas_call(
        functools.partial(scale_kernel, slots_all),
        in_specs=[VMEM] * (1 + len(flat)),
        out_specs=[HBM] * len(shapes),
        out_shape=shapes,
        scratch_shapes=[pltpu.VMEM(x.shape, x.dtype) for x in shapes]
        + [pltpu.SemaphoreType.DMA((CHUNKS, len(shapes)))],
        compiler_params=pltpu.CompilerParams(vmem_limit_bytes=SMALL_LIMIT),
        cost_estimate=pl.CostEstimate(
            flops=sum(x.size for x in shapes),
            bytes_accessed=sum(4 * x.size for x in shapes),
            transcendentals=0,
        ),
        name="scale",
    )(total, *flat)


def body(queries, keys, values, prefix_keys, prefix_values, lengths, out_grad):
    q, k, v, do = queries[0], keys[0], values[0], out_grad[0]
    length = lengths[0]
    prefix = (prefix_keys[0], prefix_values[0])
    slots_all = q.shape[0] * lax.axis_size("prompt") * lax.axis_size("response")
    first, second = [tensor_gather(prefix, chunk) for chunk in range(CHUNKS)]
    held = first.shape[0] // 2
    sent = far_and_near(first)
    slots = line_gather(first, sent)
    length_rows = length[0].astype(second.dtype) + 0 * slots[-1][-EXTRA:]
    second = jnp.concatenate([second, length_rows], axis=0)
    sent = far_and_near(second)
    turned = turn(do, first)
    results = attend(0, held, slots, length, q, turned, k, v, [])
    if len(slots) == 4:
        far = sent[3]
        sent[3] = jnp.concatenate([far[:-EXTRA] + 0 * results[4], far[-EXTRA:]], axis=0)
    next_slots = line_gather(second, sent)
    next_results = attend(1, held, next_slots, length, q, turned, k, v, results[:1])
    terms, next_terms = results[4:], next_results[4:-1]
    behind = 0 * next_results[3][:1].astype(jnp.float32)
    farthest_first = list(range(len(terms) - 1, 0, -1))
    order = (2, 1, 3) if len(terms) == 4 else farthest_first
    sums = [line_reduce(terms, order) + behind, line_reduce(next_terms, farthest_first)]
    total = sum_over(next_results[-1] + 0 * sums[0][:8, :HD], "prompt")
    weight = jnp.tile(slots_all / total[:1], (1, prefix[0].shape[1] // HD))
    scaled = scale_all(
        slots_all, total + 0 * sums[1][:8, :HD], [results[1:4], next_results[1:4]], [like(q), like(k), like(v)]
    )
    both = jnp.concatenate([terms.astype(jnp.bfloat16) for terms in sums], axis=1)
    pieces = [tensor_spread(both, len(prefix))]
    grads = [whole_columns(pieces, array) for array in range(len(prefix))]
    grads = [(grad.astype(jnp.float32) * weight).astype(jnp.bfloat16) for grad in grads]
    return tuple(x[None] for x in (next_results[0], *scaled, *grads))


def solution(mesh):
    in_specs = (
        P("prompt", "response", "tensor"),
        P("prompt", "response", "tensor"),
        P("prompt", "response", "tensor"),
        P("prompt", ("response", "tensor"), None),
        P("prompt", ("response", "tensor"), None),
        P("prompt", "response"),
        P("prompt", "response", "tensor"),
    )
    out_specs = (
        P("prompt", "response", "tensor"),
        P("prompt", "response", "tensor"),
        P("prompt", "response", "tensor"),
        P("prompt", "response", "tensor"),
        P("prompt", ("response", "tensor"), None),
        P("prompt", ("response", "tensor"), None),
    )
    return jax.shard_map(body, mesh=mesh, in_specs=in_specs, out_specs=out_specs, check_vma=False)
```

```python
import functools
import math

import jax
import jax.numpy as jnp
from jax import lax
from jax.experimental import pallas as pl
from jax.experimental.pallas import tpu as pltpu
from jax.sharding import PartitionSpec as P

HD = 128
GROUP = 8
PAIR = 2
CHUNKS = 2
EXTRA = 16
STEP = 64
VMEM_LIMIT = 40 * 1024 * 1024
SMALL_LIMIT = 8 * 1024 * 1024
NT = (((1,), (1,)), ((), ()))


def heads_down(ref, first, count):
    return jnp.concatenate(
        [ref[:, (first + i) * HD : (first + i + 1) * HD] for i in range(count)], axis=0
    )


def attend_kernel(n_slots, count, chunk, held, factor, *refs):
    last = chunk + 1 == CHUNKS
    length_ref, q_ref, turned_ref, kown_ref, vown_ref = refs[:5]
    slot_refs, refs = refs[5 : 5 + n_slots], refs[5 + n_slots + last :]
    out_hbm, dq_ref, dkown_ref, dvown_ref = refs[:4]
    term_refs, refs = refs[4 : 4 + n_slots], refs[4 + n_slots :]
    if last:
        total_ref, refs = refs[0], refs[1:]
        totals = [ref[2 * held : 2 * held + 8, :HD].astype(jnp.float32) for ref in slot_refs]
        total_ref[...] = functools.reduce(jnp.add, totals)
    out_ref, s_ref, dp_ref, e_ref, ds_ref, dot_ref = refs[:6]
    keys_ref, keys_t_ref, values_ref, values_t_ref, out_sem = refs[6:]
    first = chunk * count
    rows = q_ref.shape[0]
    own = kown_ref.shape[0]
    n_keys = s_ref.shape[1]
    width = PAIR * rows
    pairs = GROUP // PAIR
    scale = factor * math.log2(math.e)

    def columns(head, size):
        return pl.ds(head * size, size)

    stores = []

    live = (lax.broadcasted_iota(jnp.int32, (1, width), 1) % rows) < length_ref[0]

    def assemble(head, own_ref, slot_start, wide_ref, tall_ref):
        here = slice(head * HD, (head + 1) * HD)
        wide_ref[head, :own] = own_ref[:, (first + head) * HD : (first + head + 1) * HD]
        for i, ref in enumerate(slot_refs):
            part = slice(own + i * held, own + (i + 1) * held)
            wide_ref[head, part] = ref[slot_start : slot_start + held, here]
        tall_ref[head] = wide_ref[head].T

    def place(head, pair):
        return slice(pair * width, (pair + 1) * width)

    def scores(head, pair):
        if pair == 0:
            assemble(head, kown_ref, 0, keys_ref, keys_t_ref)
        s_ref[pair % 2] = lax.dot_general(
            keys_ref[head],
            heads_down(q_ref, (first + head) * GROUP + pair * PAIR, PAIR),
            NT,
            preferred_element_type=jnp.float32,
        )

    def softmax(head, pair):
        here = s_ref.at[pair % 2]
        cols = place(head, pair)
        fold = lambda x: x.reshape(x.shape[0] // 8, 8, width)
        top = jnp.full((8, width), -1e30, jnp.float32)
        for at in range(0, n_keys, STEP):
            x = here[at : at + STEP]
            if at < own:
                key_pos = lax.broadcasted_iota(jnp.int32, x.shape, 0) + at
                row_pos = lax.broadcasted_iota(jnp.int32, x.shape, 1) % rows
                x = jnp.where(key_pos <= row_pos, x, -1e30)
                here[at : at + STEP] = x
            top = jnp.maximum(top, jnp.max(fold(x), axis=0))
        top = jnp.max(top, axis=0, keepdims=True) * scale
        top = jnp.broadcast_to(top, (8, width))
        total = jnp.zeros((8, width), jnp.float32)
        for at in range(0, n_keys, STEP):
            e = jnp.exp2(fold(here[at : at + STEP]) * scale - top)
            total = total + jnp.sum(e, axis=0)
            e_ref[head % 2, at : at + STEP, cols] = e.reshape(-1, width).astype(jnp.bfloat16)
        total = jnp.sum(total, axis=0, keepdims=True)
        inverse = jnp.where(live, 1.0 / total, 0.0)
        grad = turned_ref[first + head, :, cols].astype(jnp.float32) * inverse
        dot_ref[head % 2, :, cols] = grad.astype(jnp.bfloat16)
        return inverse

    def attended(head, pair, inverse):
        cols = place(head, pair)
        if pair == 0:
            assemble(head, vown_ref, held, values_ref, values_t_ref)
        grad = dot_ref[head % 2, :, cols]
        out = jnp.dot(
            values_t_ref[head], e_ref[head % 2, :, cols], preferred_element_type=jnp.float32
        )
        dp_ref[pair % 2] = jnp.dot(values_ref[head], grad, preferred_element_type=jnp.float32)
        out = out * inverse
        turned = out.astype(jnp.bfloat16).T
        for i in range(PAIR):
            at = head * GROUP + pair * PAIR + i
            out_ref[:, at * HD : (at + 1) * HD] = turned[i * rows : (i + 1) * rows]
        return jnp.sum(out * grad.astype(jnp.float32), axis=0, keepdims=True)

    def score_grads(head, pair, centre):
        cols = place(head, pair)
        here = dp_ref.at[pair % 2]
        centre = jnp.broadcast_to(centre, (STEP, width))
        for at in range(0, n_keys, STEP):
            e = e_ref[head % 2, at : at + STEP, cols].astype(jnp.float32)
            grad = e * (here[at : at + STEP] - centre)
            ds_ref[head % 2, at : at + STEP, cols] = grad.astype(jnp.bfloat16)

    def query_grads(head, pair):
        cols = place(head, pair)
        dq = jnp.dot(
            keys_t_ref[head], ds_ref[head % 2, :, cols], preferred_element_type=jnp.float32
        )
        turned = (dq * factor).astype(jnp.bfloat16).T
        for i in range(PAIR):
            at = head * GROUP + pair * PAIR + i
            dq_ref[:, at * HD : (at + 1) * HD] = turned[i * rows : (i + 1) * rows]

    def value_grads(head):
        here = slice(head * HD, (head + 1) * HD)
        dv = lax.dot_general(
            e_ref[head % 2], dot_ref[head % 2], NT, preferred_element_type=jnp.float32
        ).astype(jnp.bfloat16)
        dvown_ref[:, here] = dv[:own]
        for i, ref in enumerate(term_refs):
            ref[held:, here] = dv[own + i * held : own + (i + 1) * held]

    def key_grads(head):
        copy = pltpu.make_async_copy(
            out_ref.at[:, columns(head, GROUP * HD)],
            out_hbm.at[:, columns(first + head, GROUP * HD)],
            out_sem.at[head],
        )
        copy.start()
        stores.append(copy)
        here = slice(head * HD, (head + 1) * HD)
        dk = jnp.dot(
            ds_ref[head % 2],
            heads_down(q_ref, (first + head) * GROUP, GROUP),
            preferred_element_type=jnp.float32,
        )
        dk = (dk * factor).astype(jnp.bfloat16)
        dkown_ref[:, here] = dk[:own]
        for i, ref in enumerate(term_refs):
            ref[:held, here] = dk[own + i * held : own + (i + 1) * held]

    steps = [(head, pair) for head in range(count) for pair in range(pairs)]
    scores(*steps[0])
    inverse = softmax(*steps[0])
    for now, then in zip(steps, steps[1:] + [None]):
        if then:
            scores(*then)
        centre = attended(*now, inverse)
        if now[1] + 1 == pairs:
            value_grads(now[0])
        if then:
            inverse = softmax(*then)
        score_grads(*now, centre)
        query_grads(*now)
        if now[1] + 1 == pairs:
            key_grads(now[0])
    for copy in stores:
        copy.wait()


def turn_kernel(do_ref, after_ref, out_ref):
    out_ref[0] = heads_down(do_ref, 0, GROUP).T


def scale_kernel(slots_all, total_ref, *refs):
    sources, refs = refs[: 3 * CHUNKS], refs[3 * CHUNKS :]
    outs, held, sem = refs[:3], refs[3:6], refs[6]
    weight = slots_all / total_ref[:1, :1]
    copies = []
    for chunk in range(CHUNKS):
        for i in range(3):
            source = sources[chunk * 3 + i]
            cols = pl.ds(chunk * source.shape[1], source.shape[1])
            scaled = source[...].astype(jnp.float32) * weight
            held[i][:, cols] = scaled.astype(jnp.bfloat16)
            copy = pltpu.make_async_copy(held[i].at[:, cols], outs[i].at[:, cols], sem.at[chunk, i])
            copy.start()
            copies.append(copy)
    for copy in copies:
        copy.wait()


def swap(x, axis, by):
    return lax.ppermute(x, axis, [(i, i ^ by) for i in range(lax.axis_size(axis))])


def sum_over(x, axis):
    by = 1
    while by < lax.axis_size(axis):
        x = x + swap(x, axis, by)
        by *= 2
    return x


def far_and_near(block):
    size = lax.axis_size("response")
    order = (3, 1) if size == 4 else range(1, size)
    return {m: swap(block, "response", m) for m in order}


def line_gather(block, sent):
    size = lax.axis_size("response")
    if size == 4:
        sent = {**sent, 2: swap(sent[3], "response", 1)}
    return [block] + [sent[m] for m in range(1, size)]


def line_reduce(slots, order):
    terms = [swap(slots[m], "response", m) for m in order]
    return functools.reduce(jnp.add, [term.astype(jnp.float32) for term in [slots[0]] + terms])


def own_columns(block, chunk, by):
    cols = block.shape[1] // (lax.axis_size("tensor") * CHUNKS)
    rank = lax.axis_index("tensor") ^ by
    return lax.dynamic_slice_in_dim(block, (rank * CHUNKS + chunk) * cols, cols, 1)


def tensor_gather(blocks, chunk):
    parts = lax.axis_size("tensor")
    pieces = []
    for m in range(parts):
        piece = jnp.concatenate([own_columns(block, chunk, m) for block in blocks], axis=0)
        pieces.append(piece if m == 0 else swap(piece, "tensor", m))
    rows = blocks[0].shape[0]
    return jnp.concatenate(
        [piece[i * rows : (i + 1) * rows] for i in range(len(blocks)) for piece in pieces], axis=0
    )


def tensor_spread(total, n_arrays):
    parts = lax.axis_size("tensor")
    rows = total.shape[0] // (n_arrays * parts)
    pieces = []
    for m in range(parts):
        piece = jnp.concatenate(
            [total[(i * parts + m) * rows : (i * parts + m + 1) * rows] for i in range(n_arrays)],
            axis=0,
        )
        pieces.append(piece if m == 0 else swap(piece, "tensor", m))
    return pieces


def whole_columns(chunk_pieces, array):
    parts = lax.axis_size("tensor")
    rank = lax.axis_index("tensor")
    rows = chunk_pieces[0][0].shape[0] // 2
    by_rank = [
        jnp.concatenate([pieces[m][array * rows : (array + 1) * rows] for pieces in chunk_pieces], axis=1)
        for m in range(parts)
    ]
    ordered = []
    for t in range(parts):
        column = by_rank[0]
        for m in range(1, parts):
            column = jnp.where(rank ^ m == t, by_rank[m], column)
        ordered.append(column)
    return jnp.concatenate(ordered, axis=1)


SMEM = pl.BlockSpec(memory_space=pltpu.SMEM)
HBM = pl.BlockSpec(memory_space=pltpu.HBM)
VMEM = pl.BlockSpec(memory_space=pltpu.VMEM)


def like(x):
    return jax.ShapeDtypeStruct(x.shape, x.dtype)


def turn(do, after):
    rows, heads = do.shape[0], do.shape[1] // (GROUP * HD)
    return pl.pallas_call(
        turn_kernel,
        grid=(heads,),
        in_specs=[pl.BlockSpec((rows, GROUP * HD), lambda j: (0, j)), HBM],
        out_specs=pl.BlockSpec((1, HD, GROUP * rows), lambda j: (j, 0, 0)),
        out_shape=jax.ShapeDtypeStruct((heads, HD, GROUP * rows), do.dtype),
        compiler_params=pltpu.CompilerParams(vmem_limit_bytes=SMALL_LIMIT),
        name="turn",
    )(do, after)


def attend(chunk, held, slots, length, q, turned, k, v, carried):
    rows = q.shape[0]
    count = k.shape[1] // (HD * CHUNKS)
    n_slots = len(slots)
    last = chunk + 1 == CHUNKS
    n_keys = rows + n_slots * held
    bf16 = jnp.bfloat16
    unit = 2 * n_keys * GROUP * rows * HD * count
    step_buffer = pltpu.VMEM((2, n_keys, PAIR * rows), jnp.float32)
    head_buffer = pltpu.VMEM((2, n_keys, GROUP * rows), bf16)
    wide = pltpu.VMEM((rows, count * GROUP * HD), bf16)
    down = pltpu.VMEM((count, n_keys, HD), bf16)
    across = pltpu.VMEM((count, HD, n_keys), bf16)
    scratch = [wide, step_buffer, step_buffer, head_buffer, head_buffer]
    scratch += [pltpu.VMEM((2, HD, GROUP * rows), bf16), down, across, down, across]
    scratch += [pltpu.SemaphoreType.DMA((count,))]
    part = lambda x: jax.ShapeDtypeStruct((x.shape[0], x.shape[1] // CHUNKS), bf16)
    terms = [jax.ShapeDtypeStruct((2 * held, count * HD), bf16)] * n_slots
    total = [jax.ShapeDtypeStruct((8, HD), jnp.float32)] * last
    return pl.pallas_call(
        functools.partial(attend_kernel, n_slots, count, chunk, held, 1.0 / math.sqrt(HD)),
        in_specs=[SMEM] + [VMEM] * (4 + n_slots) + [HBM] * last,
        out_specs=[HBM] + [VMEM] * (3 + n_slots + last),
        out_shape=[like(q), part(q), part(k), part(v)] + terms + total,
        input_output_aliases={5 + n_slots: 0} if last else {},
        scratch_shapes=scratch,
        compiler_params=pltpu.CompilerParams(vmem_limit_bytes=VMEM_LIMIT),
        cost_estimate=pl.CostEstimate(
            flops=24 * unit,
            bytes_accessed=8 * rows * GROUP * HD * count,
            transcendentals=count * n_keys * GROUP * rows,
        ),
        name=f"attend_{chunk}",
    )(length, q, turned, k, v, *slots, *carried)


def scale_all(slots_all, total, chunk_grads, shapes):
    flat = [grad for grads in chunk_grads for grad in grads]
    return pl.pallas_call(
        functools.partial(scale_kernel, slots_all),
        in_specs=[VMEM] * (1 + len(flat)),
        out_specs=[HBM] * len(shapes),
        out_shape=shapes,
        scratch_shapes=[pltpu.VMEM(x.shape, x.dtype) for x in shapes]
        + [pltpu.SemaphoreType.DMA((CHUNKS, len(shapes)))],
        compiler_params=pltpu.CompilerParams(vmem_limit_bytes=SMALL_LIMIT),
        cost_estimate=pl.CostEstimate(
            flops=sum(x.size for x in shapes),
            bytes_accessed=sum(4 * x.size for x in shapes),
            transcendentals=0,
        ),
        name="scale",
    )(total, *flat)


def body(queries, keys, values, prefix_keys, prefix_values, lengths, out_grad):
    q, k, v, do = queries[0], keys[0], values[0], out_grad[0]
    length = lengths[0]
    prefix = (prefix_keys[0], prefix_values[0])
    slots_all = q.shape[0] * lax.axis_size("prompt") * lax.axis_size("response")
    first, second = [tensor_gather(prefix, chunk) for chunk in range(CHUNKS)]
    held = first.shape[0] // 2
    sent = far_and_near(first)
    slots = line_gather(first, sent)
    length_rows = length[0].astype(second.dtype) + 0 * slots[-1][-EXTRA:]
    second = jnp.concatenate([second, length_rows], axis=0)
    sent = far_and_near(second)
    turned = turn(do, first)
    results = attend(0, held, slots, length, q, turned, k, v, [])
    if len(slots) == 4:
        far = sent[3]
        sent[3] = jnp.concatenate([far[:-EXTRA] + 0 * results[4], far[-EXTRA:]], axis=0)
    next_slots = line_gather(second, sent)
    next_results = attend(1, held, next_slots, length, q, turned, k, v, results[:1])
    terms, next_terms = results[4:], next_results[4:-1]
    behind = 0 * next_results[3][:1].astype(jnp.float32)
    farthest_first = list(range(len(terms) - 1, 0, -1))
    order = (2, 1, 3) if len(terms) == 4 else farthest_first
    sums = [line_reduce(terms, order) + behind, line_reduce(next_terms, farthest_first)]
    total = sum_over(next_results[-1] + 0 * sums[0][:8, :HD], "prompt")
    weight = jnp.tile(slots_all / total[:1], (1, prefix[0].shape[1] // HD))
    scaled = scale_all(
        slots_all, total + 0 * sums[1][:8, :HD], [results[1:4], next_results[1:4]], [like(q), like(k), like(v)]
    )
    both = jnp.concatenate([terms.astype(jnp.bfloat16) for terms in sums], axis=1)
    pieces = [tensor_spread(both, len(prefix))]
    grads = [whole_columns(pieces, array) for array in range(len(prefix))]
    grads = [(grad.astype(jnp.float32) * weight).astype(jnp.bfloat16) for grad in grads]
    return tuple(x[None] for x in (next_results[0], *scaled, *grads))


def solution(mesh):
    in_specs = (
        P("prompt", "response", "tensor"),
        P("prompt", "response", "tensor"),
        P("prompt", "response", "tensor"),
        P("prompt", ("response", "tensor"), None),
        P("prompt", ("response", "tensor"), None),
        P("prompt", "response"),
        P("prompt", "response", "tensor"),
    )
    out_specs = (
        P("prompt", "response", "tensor"),
        P("prompt", "response", "tensor"),
        P("prompt", "response", "tensor"),
        P("prompt", "response", "tensor"),
        P("prompt", ("response", "tensor"), None),
        P("prompt", ("response", "tensor"), None),
    )
    return jax.shard_map(body, mesh=mesh, in_specs=in_specs, out_specs=out_specs, check_vma=False)
```
